256 devices in a mesh: tok: 32 (over y, z), proto: 8 (over x, core).
Axes of the slice: x: 4, y: 4, z: 8, core: 2. Of those that a mesh axis runs over, the one named last changes fastest.
Arguments:
- teacher_patches: bfloat16 [16384, 256], P('tok'), as said below
- student_patches: bfloat16 [16384, 256], P('tok')
- prototypes: bfloat16 [65536, 256], P(('proto', 'tok'))
- mask_index: int32 [32, 512], P('tok'), may hold values from 0 to 511, each once within a row
- counts: int32 [32], P('tok'), may hold values from 1 to 256, 4096 in all
Outputs:
- grad_patches: float32 [16384, 256], P('tok')
- grad_prototypes: float32 [65536, 256], P(('proto', 'tok'))
The draws below stay inside these ranges and needn't reach their ends.
Inputs may be any that keep to these rules, and one draw needn't show every extreme that they name: `teacher_patches`: teacher features and prototypes are real-valued. `mask_index`: each row is a permutation; only its first counts[d] entries are used. The counts sum to 4096; the largest is exactly 256.
All inputs are finite; a program needn't handle non-finite values. No bound on the sum of `counts` on one device may be relied on, other than what follows from the above.
Results may differ from the reference program's by a relative error of at most 0.0065.
Values may be sent and summed in bfloat16 or wider, within the bound.
No kernel may reach another device: no remote copies, remote signals or barrier semaphores. Data moves between devices by JAX's collectives and lax.ppermute only.
A program may use at most 128 MiB of HBM per device.

```python
import math
import jax
import jax.numpy as jnp
import numpy as np
from jax import lax

D_BOT = 256
K = 65536
ITERS = 3
PATCH_DEV = 512
CAP = 256
BAL = 128
TOTAL = 4096
PATCH_ROWS = 16384
N_TOK = 32
N_PROTO = 8


def shared_prototypes(key):
    return jax.random.normal(key, (K, D_BOT), jnp.float32) * (1.0 / 16.0)


def draw_prototypes(key, part):
    return shared_prototypes(key).astype(jnp.bfloat16)


def drawn_rows(protos, keys, low, high):
    first = jax.random.randint(keys[2], (PATCH_ROWS,), 0, K)
    second = jax.random.randint(keys[3], (PATCH_ROWS,), 0, K)
    strength = jax.random.uniform(keys[4], (PATCH_ROWS, 1), jnp.float32, low, high)
    return strength * (protos[first] + 0.985 * protos[second])


def draw_teacher_patches(key, part):
    protos = shared_prototypes(key)
    key = jax.random.fold_in(key, 7)
    keys = jax.random.split(key, 6)
    scales = jnp.exp(jax.random.uniform(keys[0], (PATCH_ROWS, 1), jnp.float32, jnp.log(0.05), jnp.log(0.5)))
    base = jax.random.normal(keys[1], (PATCH_ROWS, D_BOT), jnp.float32) * scales
    aligned = drawn_rows(protos, keys, 8.0, 16.0)
    chosen = (jnp.arange(PATCH_ROWS) % 8 == 0)[:, None]
    return jnp.where(chosen, aligned, base).astype(jnp.bfloat16)


def draw_student_patches(key, part):
    protos = shared_prototypes(key)
    key = jax.random.fold_in(key, 11)
    keys = jax.random.split(key, 6)
    base = jax.random.normal(keys[1], (PATCH_ROWS, D_BOT), jnp.float32) * 0.15
    aligned = drawn_rows(protos, keys, 12.0, 24.0)
    chosen = (jnp.arange(PATCH_ROWS) % 8 == 4)[:, None]
    return jnp.where(chosen, aligned, base).astype(jnp.bfloat16)


def length_profile(amount, total, limit, slope):
    portions = [(1 << 20) // math.isqrt(standing ** slope) + 1 for standing in range(2, amount + 1)]
    surplus, given = total - limit - (amount - 1), [1] * (amount - 1)
    while surplus > 0:
        candidates = [i for i in range(amount - 1) if given[i] < limit]
        mass, left = sum([portions[i] for i in candidates]), surplus
        for i in candidates:
            extra = min(limit - given[i], max(1, left * portions[i] // mass), surplus)
            given[i] = given[i] + extra
            surplus = surplus - extra
    return np.array([limit] + given)


def ragged_sizes(key, number_of, total, reach, slope):
    if number_of == 2:
        one = jax.random.randint(key, (), max(1, total - reach), min(reach, total - 1) + 1)
        return jnp.stack([one, total - one])
    sizes = jnp.asarray(length_profile(number_of, total, reach, slope), jnp.int32)
    twos = (number_of - 1) // 2
    giver, receiver = sizes[1:1 + 2 * twos:2], sizes[2:2 + 2 * twos:2]
    room = jnp.minimum(giver - 1, reach - receiver)
    moved = jax.random.randint(jax.random.fold_in(key, 1), (twos,), 0, 1 << 20) % (room + 1)
    sizes = sizes.at[1:1 + 2 * twos:2].set(giver - moved).at[2:2 + 2 * twos:2].set(receiver + moved)
    return sizes[jax.random.permutation(jax.random.fold_in(key, 2), number_of)]


def setup_inputs(seed: int = 0) -> dict:
    seeds = jax.random.split(jax.random.key(seed), 6)
    return {
        "teacher_patches": draw_teacher_patches(jax.random.fold_in(seeds[5], 71), 0),
        "student_patches": draw_student_patches(jax.random.fold_in(seeds[5], 71), 0),
        "prototypes": draw_prototypes(jax.random.fold_in(seeds[5], 71), 0),
        "mask_index": jax.vmap(lambda own: jax.random.permutation(own, PATCH_DEV))(jax.random.split(seeds[3], N_TOK)).reshape((N_TOK, PATCH_DEV)).astype(jnp.int32),
        "counts": ragged_sizes(seeds[4], N_TOK, BAL * N_TOK, CAP, 2).astype(jnp.int32),
    }


TEACHER_TEMP = 0.07
STUDENT_TEMP = 0.1


def scores(block, rows, temp):
    return jnp.dot(rows, block.T, preferred_element_type=jnp.float32) * (1.0 / temp)


def reference(teacher_patches, student_patches, prototypes, mask_index, counts):
    ends = jnp.cumsum(counts).astype(jnp.int32)
    starts = (ends - counts).astype(jnp.int32)
    places = jnp.arange(TOTAL, dtype=jnp.int32)
    owner = jnp.sum((places[:, None] >= ends[None, :]).astype(jnp.int32), axis=1).astype(jnp.int32)
    inner = (places - starts[owner]).astype(jnp.int32)
    patch_rows = (owner * PATCH_DEV + mask_index[owner, inner]).astype(jnp.int32)
    teach = teacher_patches[patch_rows]
    stud = student_patches[patch_rows]
    blocks = prototypes.reshape(N_PROTO, K // N_PROTO, D_BOT)
    row_pot = jnp.zeros((TOTAL,), jnp.float32)
    col_pot = jnp.zeros((N_PROTO, K // N_PROTO), jnp.float32)
    for step in range(ITERS):
        col_pot = lax.map(lambda block: -jax.nn.logsumexp(scores(block, teach, TEACHER_TEMP) + row_pot[:, None], axis=0), blocks)
        partial_value = lax.map(lambda pair: jax.nn.logsumexp(scores(pair[0], teach, TEACHER_TEMP) + pair[1][None, :], axis=1), (blocks, col_pot))
        row_pot = -jax.nn.logsumexp(partial_value, axis=0)
    student_parts = lax.map(lambda block: jax.nn.logsumexp(scores(block, stud, STUDENT_TEMP), axis=1), blocks)
    student_lse = jax.nn.logsumexp(student_parts, axis=0)

    def backward(pair):
        block, pot = pair
        target = jnp.exp(scores(block, teach, TEACHER_TEMP) + row_pot[:, None] + pot[None, :])
        student = jnp.exp(scores(block, stud, STUDENT_TEMP) - student_lse[:, None])
        grads = ((student - target) * (1.0 / STUDENT_TEMP)).astype(jnp.bfloat16)
        feature_part = jnp.dot(grads, block, preferred_element_type=jnp.float32)
        proto_part = jnp.dot(grads.T, stud, preferred_element_type=jnp.float32)
        return feature_part, proto_part

    feature_parts, proto_parts = lax.map(backward, (blocks, col_pot))
    grad_tok = jnp.sum(feature_parts, axis=0)
    grad_patches = jnp.zeros((PATCH_ROWS, D_BOT), jnp.float32).at[patch_rows].set(grad_tok)
    return grad_patches, proto_parts.reshape(K, D_BOT)
```

```python
import functools

import jax
import jax.numpy as jnp
from jax import lax
from jax.experimental import pallas as pl
from jax.experimental.pallas import tpu as pltpu
from jax.sharding import PartitionSpec as P

CAP = 256
BAL = 128
PROTO = 8
SLOTS = CAP // PROTO
PAY = SLOTS + 16
LANES = 128
TEACHER_SCALE = 1.0 / 0.07
STUDENT_SCALE = 1.0 / 0.1
FAR_BELOW = -1e30
VMEM = 40 * 1024 * 1024
F32 = jnp.float32
BF16 = jnp.bfloat16
HIGH = lax.Precision.HIGHEST


def iota(shape, dim):
    return lax.broadcasted_iota(jnp.int32, shape, dim)


def dot_nt(a, b, precision=None):
    return lax.dot_general(
        a, b, (((1,), (1,)), ((), ())), precision=precision, preferred_element_type=F32
    )


def dot_tn(a, b, precision=None):
    return lax.dot_general(
        a, b, (((0,), (0,)), ((), ())), precision=precision, preferred_element_type=F32
    )


def dot_nn(a, b, precision=None):
    return jnp.dot(a, b, precision=precision, preferred_element_type=F32)


def turned(rows, block, first_lane_only):
    at = iota((8, LANES), 0) == block
    if first_lane_only:
        at = at & (iota((8, LANES), 1) == 0)
    return dot_nt(at.astype(F32), rows, HIGH)


def column(packed, block):
    at = (iota((8, LANES), 0) == block).astype(F32)
    return dot_tn(packed, at, HIGH)


def lse_over_first(values):
    top = jnp.max(values, axis=0)
    return top + jnp.log(jnp.sum(jnp.exp(values - top[None]), axis=0))


def row_offset(group, device):
    return lax.rem(group + device, PROTO)


def pick_kernel(place_ref, count_ref, mask_ref, teacher_ref, student_ref, teach_ref, stud_ref):
    patches = teacher_ref.shape[0]
    offset = row_offset(place_ref[0], place_ref[1])
    at = iota((SLOTS, patches), 1) == iota((SLOTS, patches), 0) * PROTO + offset
    mask = jnp.broadcast_to(mask_ref[...].astype(F32), (LANES, patches))
    chosen = dot_nt(at.astype(F32), mask, HIGH)[:, :1]
    chosen = (chosen + 0.5).astype(jnp.int32)
    onehot = (iota((SLOTS, patches), 1) == chosen).astype(BF16)
    teach = dot_nn(onehot, teacher_ref[...]).astype(BF16)
    stud_ref[...] = dot_nn(onehot, student_ref[...]).astype(BF16)
    count = jnp.full((PAY - SLOTS, teach.shape[1]), count_ref[0], jnp.int32).astype(F32).astype(BF16)
    teach_ref[...] = jnp.broadcast_to(jnp.concatenate([teach, count], axis=0)[None], teach_ref.shape)


def place_onehot(place, rows):
    tokens = rows
    return (iota((tokens, place.shape[1]), 0).astype(F32) == place).astype(BF16)


def first_kernel(place_ref, pay_ref, protos_ref, teach_ref, place_out_ref, valid_ref, col_ref):
    devices, _, width = pay_ref.shape
    tokens = teach_ref.shape[0]
    group = place_ref[0]
    extra = PAY - SLOTS
    counts_rows = pay_ref[:, SLOTS:, :].reshape(devices * extra, width)
    pick = (iota((8, width), 1) == 0).astype(BF16)
    counts = dot_nt(pick, counts_rows)
    owner = iota(counts.shape, 1) // extra
    held = (counts + 0.5).astype(jnp.int32) - row_offset(group, owner) + (PROTO - 1)
    held = (held // PROTO).astype(F32).astype(BF16)
    slots = devices * SLOTS
    source = iota((devices * extra, slots), 0)
    target = iota((devices * extra, slots), 1) // SLOTS
    leads = source % extra == 0
    before = dot_nn(held, (leads & (source // extra < target)).astype(BF16))[:1]
    own = dot_nn(held, (leads & (source // extra == target)).astype(BF16))[:1]
    inner = (iota((1, slots), 1) % SLOTS).astype(F32)
    place = jnp.where(inner < own, before + inner, -1.0)
    place_out_ref[...] = jnp.broadcast_to(place, place_out_ref.shape)
    total = jnp.max(jnp.where(inner < own, before + inner + 1.0, 0.0), axis=1, keepdims=True)
    order = iota((8, LANES), 0) * LANES + iota((8, LANES), 1)
    valid_ref[...] = (order.astype(F32) < total).astype(F32)
    packed = pay_ref[:, :SLOTS, :].reshape(slots, width)
    teach = dot_nn(place_onehot(place, tokens), packed).astype(BF16)
    teach_ref[...] = teach
    step = 2 * LANES
    alive = iota((tokens, step), 0).astype(F32) < total
    rows = []
    for start in range(0, protos_ref.shape[0], step):
        scores = dot_nt(teach, protos_ref[start : start + step, :]) * TEACHER_SCALE
        scores = jnp.where(alive, scores, FAR_BELOW)
        top = jnp.max(scores, axis=0, keepdims=True)
        lse = top + jnp.log(jnp.sum(jnp.exp(scores - top), axis=0, keepdims=True))
        rows += [lse[:, :LANES], lse[:, LANES:]]
    col_ref[...] = jnp.broadcast_to(jnp.concatenate(rows, axis=0)[None], col_ref.shape)


def wide(packed):
    return jnp.concatenate([packed[i : i + 1, :] for i in range(packed.shape[0])], axis=1)


def second_kernel(teach_ref, protos_ref, col_ref, exp_ref, top_ref, row_ref):
    col_pot = -wide(lse_over_first(col_ref[...]))
    tops = jnp.zeros((8, LANES), F32)
    lses = jnp.zeros((8, LANES), F32)
    for block in range(teach_ref.shape[0] // LANES):
        rows = pl.ds(block * LANES, LANES)
        scores = dot_nt(teach_ref[rows, :], protos_ref[...]) * TEACHER_SCALE + col_pot
        top = jnp.max(scores, axis=1, keepdims=True)
        exps = jnp.exp(scores - top)
        exp_ref[rows, :] = exps
        total = jnp.sum(exps, axis=1, keepdims=True)
        tops += turned(jnp.broadcast_to(top, (LANES, LANES)), block, True)
        lses += turned(jnp.broadcast_to(top + jnp.log(total), (LANES, LANES)), block, True)
    top_ref[...] = tops
    row_ref[...] = jnp.broadcast_to(lses[None], row_ref.shape)


def weighted_columns(exp_ref, weight):
    chunks = exp_ref.shape[1] // LANES
    sums = [jnp.zeros((8, LANES), F32) for _ in range(chunks)]
    for block in range(exp_ref.shape[0] // LANES):
        factor = column(weight, block)
        for chunk in range(chunks):
            part = exp_ref[block * LANES : (block + 1) * LANES, chunk * LANES : (chunk + 1) * LANES]
            part = (part * factor).reshape(LANES // 8, 8, LANES)
            sums[chunk] += jnp.sum(part, axis=0)
    return jnp.concatenate([jnp.sum(part, axis=0, keepdims=True) for part in sums], axis=0)


def third_kernel(exp_ref, top_ref, valid_ref, row_ref, factor_ref, col_ref):
    row_pot = -lse_over_first(row_ref[...])
    factor = jnp.where(valid_ref[...] > 0.0, jnp.exp(top_ref[...] + row_pot), 0.0)
    factor_ref[...] = factor
    col_ref[...] = jnp.broadcast_to(weighted_columns(exp_ref, factor)[None], col_ref.shape)


def row_scale(valid_ref, sums):
    alive = valid_ref[...] > 0.0
    return jnp.where(alive, 1.0 / jnp.where(alive, sums, 1.0), 0.0)


def column_kernel(exp_ref, factor_ref, valid_ref, row_ref, col_ref):
    weight = row_scale(valid_ref, jnp.sum(row_ref[...], axis=0)) * factor_ref[...]
    col_ref[...] = jnp.broadcast_to(weighted_columns(exp_ref, weight)[None], col_ref.shape)


def weighted_rows(exp_ref, weight):
    sums = jnp.zeros((8, LANES), F32)
    for block in range(exp_ref.shape[0] // LANES):
        part = jnp.zeros((LANES, LANES), F32)
        for chunk in range(weight.shape[0]):
            values = exp_ref[block * LANES : (block + 1) * LANES, chunk * LANES : (chunk + 1) * LANES]
            part += values * weight[chunk : chunk + 1, :]
        sums += turned(part, block, False)
    return sums


def row_kernel(exp_ref, factor_ref, col_ref, row_ref):
    weight = 1.0 / jnp.sum(col_ref[...], axis=0)
    sums = weighted_rows(exp_ref, weight) * factor_ref[...]
    row_ref[...] = jnp.broadcast_to(sums[None], row_ref.shape)


def student_kernel(slots_ref, place_ref, protos_ref, stud_ref, row_ref):
    tokens = stud_ref.shape[0]
    devices, slots, width = slots_ref.shape
    packed = slots_ref[...].reshape(devices * slots, width)
    stud_ref[...] = dot_nn(place_onehot(place_ref[:1, :], tokens), packed).astype(BF16)
    lses = jnp.zeros((8, LANES), F32)
    for block in range(tokens // LANES):
        rows = pl.ds(block * LANES, LANES)
        scores = dot_nt(stud_ref[rows, :], protos_ref[...]) * STUDENT_SCALE
        top = jnp.max(scores, axis=1, keepdims=True)
        total = jnp.sum(jnp.exp(scores - top), axis=1, keepdims=True)
        lses += turned(jnp.broadcast_to(top + jnp.log(total), (LANES, LANES)), block, True)
    row_ref[...] = lses


def last_row_kernel(exp_ref, factor_ref, col_ref, stud_row_ref, row_ref):
    weight = 1.0 / jnp.sum(col_ref[...], axis=0)
    sums = weighted_rows(exp_ref, weight) * factor_ref[...]
    both = jnp.concatenate([sums, stud_row_ref[...]], axis=0)
    row_ref[...] = jnp.broadcast_to(both[None], row_ref.shape)


def gradient_kernel(
    place_ref, exp_ref, factor_ref, valid_ref, col_ref, row_ref, stud_ref, protos_ref, slot_ref,
    tok_ref, proto_ref, weight_ref, scale_ref, lse_ref, total_ref,
):
    tokens, width = stud_ref.shape
    share = width
    group = place_ref[0]
    weights = 1.0 / jnp.sum(col_ref[...], axis=0)
    for owner in range(PROTO):
        weight_ref[owner, :, :] = wide(weights[2 * owner : 2 * owner + 2, :])
    sums = jnp.sum(row_ref[:, :8, :], axis=0)
    scale = row_scale(valid_ref, sums) * (factor_ref[...] * STUDENT_SCALE)
    lses = lse_over_first(row_ref[:, 8:, :])
    for block in range(tokens // LANES):
        rows = pl.ds(block * LANES, LANES)
        part = column(scale, block)
        scale_ref[rows, :] = jnp.concatenate([part, part], axis=1)
        part = column(lses, block)
        lse_ref[rows, :] = jnp.concatenate([part, part], axis=1)
    total_ref[...] = jnp.zeros_like(total_ref)
    alive = scale_ref[...] > 0.0
    for away in range(PROTO):
        x = lax.rem(group // 2 + away % 4, PROTO // 2)
        core = lax.rem(group + away // 4, 2)
        owner = 2 * x + core
        start = pl.multiple_of(owner * share, share)
        block = protos_ref[pl.ds(start, share), :]
        scores = dot_nt(stud_ref[...], block) * STUDENT_SCALE
        student = jnp.exp(scores - lse_ref[...]) * STUDENT_SCALE
        target = exp_ref[:, pl.ds(start, share)] * scale_ref[...] * weight_ref[owner]
        grads = jnp.where(alive, student - target, 0.0).astype(BF16)
        proto_ref[away, :, :] = dot_tn(grads, stud_ref[...])
        total_ref[...] += dot_nn(grads, block)
    onehot = place_onehot(slot_ref[:1, :], tokens)
    slots = dot_tn(onehot, total_ref[...].astype(BF16)).astype(BF16)
    tok_ref[...] = slots.reshape(tok_ref.shape)


def sum_kernel(parts_ref, out_ref):
    total = jnp.sum(parts_ref[...].astype(F32), axis=0)
    out_ref[...] = jnp.broadcast_to(total[None], out_ref.shape)


def spread_kernel(place_ref, count_ref, mask_ref, rows_ref, out_ref):
    patches, width = out_ref.shape
    device = place_ref[1]
    wanted = iota((patches, CAP), 1)
    rank = (wanted % SLOTS) * PROTO + row_offset(wanted // SLOTS, device)
    at = (iota((patches, CAP), 0) == rank).astype(F32)
    mask = jnp.broadcast_to(mask_ref[...].astype(F32), (8, patches))
    chosen = (dot_nn(mask, at, HIGH)[:1] + 0.5).astype(jnp.int32)
    chosen = jnp.where(rank[:1, :] < count_ref[0], chosen, -1)
    onehot = (iota((patches, CAP), 0) == chosen).astype(F32)
    out_ref[...] = dot_nn(onehot, rows_ref[...].reshape(CAP, width), HIGH)


def call(kernel, outs, inputs, scalars=0, scratch=()):
    smem = [pl.BlockSpec(memory_space=pltpu.SMEM)] * scalars
    vmem = [pl.BlockSpec(memory_space=pltpu.VMEM)] * (len(inputs) - scalars)
    return pl.pallas_call(
        kernel,
        out_shape=[jax.ShapeDtypeStruct(shape, dtype) for shape, dtype in outs],
        in_specs=smem + vmem,
        out_specs=[pl.BlockSpec(memory_space=pltpu.VMEM)] * len(outs),
        scratch_shapes=list(scratch),
        compiler_params=pltpu.CompilerParams(vmem_limit_bytes=VMEM),
    )(*inputs)


def exchange(parts, axis):
    return lax.all_to_all(parts, axis, 0, 0, tiled=True)


def on_device(devices, teacher_patches, student_patches, prototypes, mask_index, counts):
    patches, width = teacher_patches.shape
    share = prototypes.shape[0]
    protos_held = PROTO * share
    chunks = protos_held // LANES
    tokens = -(-(BAL * devices // PROTO + devices) // LANES) * LANES
    group = lax.axis_index("proto")
    device = lax.axis_index("tok")
    place = jnp.stack([group, device]).astype(jnp.int32)

    teach_pay, stud_own = call(
        pick_kernel,
        [((devices, PAY, width), BF16), ((SLOTS, width), BF16)],
        (place, counts, mask_index, teacher_patches, student_patches),
        scalars=2,
    )
    protos = lax.all_gather(prototypes, "proto", axis=0, tiled=True)
    teach_slots = exchange(teach_pay, "tok")
    stud_slots = lax.all_gather(stud_own, "tok", axis=0)

    packed = ((8, LANES), F32)
    col_out = ((PROTO, chunks, LANES), F32)
    row_out = ((devices, 8, LANES), F32)
    teach, slots, valid, col = call(
        first_kernel,
        [((tokens, width), BF16), ((8, devices * SLOTS), F32), packed, col_out],
        (place, teach_slots, protos),
        scalars=1,
    )
    col = exchange(col, "proto")
    exps, top, row = call(
        second_kernel, [((tokens, protos_held), F32), packed, row_out], (teach, protos, col)
    )
    row = exchange(row, "tok")
    factor, col = call(third_kernel, [packed, col_out], (exps, top, valid, row))
    col = exchange(col, "proto")
    (row,) = call(row_kernel, [row_out], (exps, factor, col))
    row = exchange(row, "tok")
    (col,) = call(column_kernel, [col_out], (exps, factor, valid, row))
    col = exchange(col, "proto")
    stud, stud_row = call(
        student_kernel, [((tokens, width), BF16), packed], (stud_slots, slots, protos)
    )
    (row,) = call(
        last_row_kernel, [((devices, 16, LANES), F32)], (exps, factor, col, stud_row)
    )
    row = exchange(row, "tok")
    grad_slots, grad_parts = call(
        gradient_kernel,
        [((devices, SLOTS, width), BF16), ((PROTO, share, width), F32)],
        (place, exps, factor, valid, col, row, stud, protos, slots),
        scalars=1,
        scratch=(
            pltpu.VMEM((PROTO, 1, share), F32),
            pltpu.VMEM((tokens, share), F32),
            pltpu.VMEM((tokens, share), F32),
            pltpu.VMEM((tokens, width), F32),
        ),
    )
    half = PROTO // 2
    swap = [(p, p ^ 1) for p in range(PROTO)]
    mine = grad_parts[:half] + lax.ppermute(grad_parts[half:], "proto", swap)
    grad_prototypes = mine[0]
    for away in range(1, half):
        route = [(p, (p + 2 * away) % PROTO) for p in range(PROTO)]
        grad_prototypes = grad_prototypes + lax.ppermute(mine[away], "proto", route)

    (rows,) = call(sum_kernel, [((PROTO, SLOTS, width), F32)], (exchange(grad_slots, "tok"),))
    rows = exchange(rows, "proto")
    (grad_patches,) = call(
        spread_kernel, [((patches, width), F32)], (place, counts, mask_index, rows), scalars=2
    )
    return (grad_patches, grad_prototypes)


def solution(mesh):
    return jax.shard_map(
        functools.partial(on_device, mesh.shape["tok"]),
        mesh=mesh,
        in_specs=(
            P("tok", None),
            P("tok", None),
            P(("proto", "tok"), None),
            P("tok", None),
            P("tok"),
        ),
        out_specs=(P("tok", None), P(("proto", "tok"), None)),
        check_vma=False,
    )
```

```python
import functools

import jax
import jax.numpy as jnp
from jax import lax
from jax.experimental import pallas as pl
from jax.experimental.pallas import tpu as pltpu
from jax.sharding import PartitionSpec as P

CAP = 256
BAL = 128
PROTO = 8
SLOTS = CAP // PROTO
LANES = 128
TEACHER_SCALE = 1.0 / 0.07
STUDENT_SCALE = 1.0 / 0.1
FAR_BELOW = -1e30
VMEM = 40 * 1024 * 1024
F32 = jnp.float32
BF16 = jnp.bfloat16
HIGH = lax.Precision.HIGHEST


def iota(shape, dim):
    return lax.broadcasted_iota(jnp.int32, shape, dim)


def dot_nt(a, b, precision=None):
    return lax.dot_general(
        a, b, (((1,), (1,)), ((), ())), precision=precision, preferred_element_type=F32
    )


def dot_tn(a, b, precision=None):
    return lax.dot_general(
        a, b, (((0,), (0,)), ((), ())), precision=precision, preferred_element_type=F32
    )


def dot_nn(a, b, precision=None):
    return jnp.dot(a, b, precision=precision, preferred_element_type=F32)


def turned(rows, block, first_lane_only):
    at = iota((8, LANES), 0) == block
    if first_lane_only:
        at = at & (iota((8, LANES), 1) == 0)
    return dot_nt(at.astype(F32), rows, HIGH)


def column(packed, block):
    at = (iota((8, LANES), 0) == block).astype(F32)
    return dot_tn(packed, at, HIGH)


def lse_over_first(values):
    top = jnp.max(values, axis=0)
    return top + jnp.log(jnp.sum(jnp.exp(values - top[None]), axis=0))


def row_offset(group, device):
    return lax.rem(group + device, PROTO)


def pick_kernel(place_ref, count_ref, mask_ref, teacher_ref, student_ref, pay_ref, patch_ref, sem_ref):
    copies = [
        pltpu.make_async_copy(source, patch_ref.at[which], sem_ref.at[which])
        for which, source in enumerate((teacher_ref, student_ref))
    ]
    for copy in copies:
        copy.start()
    patches, width = teacher_ref.shape
    offset = row_offset(place_ref[0], place_ref[1])
    at = iota((SLOTS, patches), 1) == iota((SLOTS, patches), 0) * PROTO + offset
    mask = jnp.broadcast_to(mask_ref[...].astype(F32), (LANES, patches))
    chosen = dot_nt(at.astype(F32), mask, HIGH)[:, :1]
    chosen = (chosen + 0.5).astype(jnp.int32)
    onehot = (iota((SLOTS, patches), 1) == chosen).astype(BF16)
    held = iota((SLOTS, width), 0) * PROTO + offset < count_ref[0]
    for copy in copies:
        copy.wait()
    teach = jnp.where(held, dot_nn(onehot, patch_ref[0]), jnp.inf).astype(BF16)
    stud = dot_nn(onehot, patch_ref[1]).astype(BF16)
    both = jnp.concatenate([teach, stud], axis=0)
    pay_ref[...] = jnp.broadcast_to(both[None], pay_ref.shape)


def place_onehot(place, tokens):
    return (iota((tokens, place.shape[1]), 0).astype(F32) == place).astype(BF16)


def first_kernel(
    place_ref, pay_ref, near_ref, far_ref,
    teach_ref, stud_ref, protos_ref, place_out_ref, valid_ref, col_ref,
):
    devices, _, width = pay_ref.shape
    tokens = teach_ref.shape[0]
    share = near_ref.shape[1]
    group = place_ref[0]
    for away in range(PROTO // 2):
        x = lax.rem(group // 2 + away, PROTO // 2)
        core = lax.rem(group, 2)
        start = pl.multiple_of((2 * x + core) * share, share)
        protos_ref[pl.ds(start, share), :] = near_ref[away]
        start = pl.multiple_of((2 * x + 1 - core) * share, share)
        protos_ref[pl.ds(start, share), :] = far_ref[away]
    slots = devices * SLOTS
    arrived = pay_ref[:, :SLOTS, :].reshape(slots, width).astype(F32)
    real = arrived < jnp.inf
    pick = (iota((8, width), 1) == 0).astype(BF16)
    flags = dot_nt(pick, real.astype(F32).astype(BF16))
    held = dot_nn(
        flags.astype(BF16), (iota((slots, LANES), 0) // SLOTS == iota((slots, LANES), 1)).astype(BF16)
    )
    before = dot_nn(
        held.astype(BF16), (iota((LANES, slots), 0) < iota((LANES, slots), 1) // SLOTS).astype(BF16)
    )[:1]
    inner = (iota((1, slots), 1) % SLOTS).astype(F32)
    place = jnp.where(flags[:1] > 0.5, before + inner, -1.0)
    place_out_ref[...] = jnp.broadcast_to(place, place_out_ref.shape)
    total = jnp.max(place, axis=1, keepdims=True) + 1.0
    order = iota((8, LANES), 0) * LANES + iota((8, LANES), 1)
    valid_ref[...] = (order.astype(F32) < total).astype(F32)
    onehot = place_onehot(place, tokens)
    teach = dot_nn(onehot, jnp.where(real, arrived, 0.0).astype(BF16)).astype(BF16)
    teach_ref[...] = teach
    stud_ref[...] = dot_nn(onehot, pay_ref[:, SLOTS:, :].reshape(slots, width)).astype(BF16)
    step = 2 * LANES
    alive = iota((tokens, step), 0).astype(F32) < total
    rows = []
    for start in range(0, protos_ref.shape[0], step):
        scores = dot_nt(teach, protos_ref[start : start + step, :]) * TEACHER_SCALE
        scores = jnp.where(alive, scores, FAR_BELOW)
        top = jnp.max(scores, axis=0, keepdims=True)
        lse = top + jnp.log(jnp.sum(jnp.exp(scores - top), axis=0, keepdims=True))
        rows += [lse[:, :LANES], lse[:, LANES:]]
    col_ref[...] = jnp.broadcast_to(jnp.concatenate(rows, axis=0)[None], col_ref.shape)


def wide(packed):
    return jnp.concatenate([packed[i : i + 1, :] for i in range(packed.shape[0])], axis=1)


def second_kernel(teach_ref, protos_ref, col_ref, exp_ref, top_ref, row_ref):
    col_pot = -wide(lse_over_first(col_ref[...]))
    tops = jnp.zeros((8, LANES), F32)
    lses = jnp.zeros((8, LANES), F32)
    for block in range(teach_ref.shape[0] // LANES):
        rows = pl.ds(block * LANES, LANES)
        scores = dot_nt(teach_ref[rows, :], protos_ref[...]) * TEACHER_SCALE + col_pot
        top = jnp.max(scores, axis=1, keepdims=True)
        exps = jnp.exp(scores - top)
        exp_ref[rows, :] = exps
        total = jnp.sum(exps, axis=1, keepdims=True)
        tops += turned(jnp.broadcast_to(top, (LANES, LANES)), block, True)
        lses += turned(jnp.broadcast_to(top + jnp.log(total), (LANES, LANES)), block, True)
    top_ref[...] = tops
    row_ref[...] = jnp.broadcast_to(lses[None], row_ref.shape)


def weighted_columns(exp_ref, weight):
    chunks = exp_ref.shape[1] // LANES
    sums = [jnp.zeros((8, LANES), F32) for _ in range(chunks)]
    for block in range(exp_ref.shape[0] // LANES):
        factor = column(weight, block)
        for chunk in range(chunks):
            part = exp_ref[block * LANES : (block + 1) * LANES, chunk * LANES : (chunk + 1) * LANES]
            part = (part * factor).reshape(LANES // 8, 8, LANES)
            sums[chunk] += jnp.sum(part, axis=0)
    return jnp.concatenate([jnp.sum(part, axis=0, keepdims=True) for part in sums], axis=0)


def third_kernel(exp_ref, top_ref, valid_ref, row_ref, factor_ref, col_ref):
    row_pot = -lse_over_first(row_ref[...])
    factor = jnp.where(valid_ref[...] > 0.0, jnp.exp(top_ref[...] + row_pot), 0.0)
    factor_ref[...] = factor
    col_ref[...] = jnp.broadcast_to(weighted_columns(exp_ref, factor)[None], col_ref.shape)


def row_scale(valid_ref, sums):
    alive = valid_ref[...] > 0.0
    return jnp.where(alive, 1.0 / jnp.where(alive, sums, 1.0), 0.0)


def column_kernel(exp_ref, factor_ref, valid_ref, row_ref, col_ref):
    weight = row_scale(valid_ref, jnp.sum(row_ref[...], axis=0)) * factor_ref[...]
    col_ref[...] = jnp.broadcast_to(weighted_columns(exp_ref, weight)[None], col_ref.shape)


def weighted_rows(exp_ref, weight):
    sums = jnp.zeros((8, LANES), F32)
    for block in range(exp_ref.shape[0] // LANES):
        part = jnp.zeros((LANES, LANES), F32)
        for chunk in range(weight.shape[0]):
            values = exp_ref[block * LANES : (block + 1) * LANES, chunk * LANES : (chunk + 1) * LANES]
            part += values * weight[chunk : chunk + 1, :]
        sums += turned(part, block, False)
    return sums


def row_kernel(exp_ref, factor_ref, col_ref, row_ref):
    weight = 1.0 / jnp.sum(col_ref[...], axis=0)
    sums = weighted_rows(exp_ref, weight) * factor_ref[...]
    row_ref[...] = jnp.broadcast_to(sums[None], row_ref.shape)


def student_kernel(protos_ref, stud_ref, row_ref):
    lses = jnp.zeros((8, LANES), F32)
    for block in range(stud_ref.shape[0] // LANES):
        rows = pl.ds(block * LANES, LANES)
        scores = dot_nt(stud_ref[rows, :], protos_ref[...]) * STUDENT_SCALE
        top = jnp.max(scores, axis=1, keepdims=True)
        total = jnp.sum(jnp.exp(scores - top), axis=1, keepdims=True)
        lses += turned(jnp.broadcast_to(top + jnp.log(total), (LANES, LANES)), block, True)
    row_ref[...] = lses


def last_row_kernel(exp_ref, factor_ref, col_ref, stud_row_ref, row_ref):
    weight = 1.0 / jnp.sum(col_ref[...], axis=0)
    sums = weighted_rows(exp_ref, weight) * factor_ref[...]
    both = jnp.concatenate([sums, stud_row_ref[...]], axis=0)
    row_ref[...] = jnp.broadcast_to(both[None], row_ref.shape)


def gradient_kernel(
    exp_ref, factor_ref, valid_ref, col_ref, row_ref, stud_ref, protos_ref, slot_ref,
    tok_ref, grad_ref, scale_ref, lse_ref, total_ref,
):
    tokens, width = stud_ref.shape
    weights = 1.0 / jnp.sum(col_ref[...], axis=0)
    sums = jnp.sum(row_ref[:, :8, :], axis=0)
    scale = row_scale(valid_ref, sums) * (factor_ref[...] * STUDENT_SCALE)
    lses = lse_over_first(row_ref[:, 8:, :])
    alive = valid_ref[...]
    lses = jnp.where(alive > 0.0, lses, -FAR_BELOW)
    for block in range(tokens // LANES):
        rows = pl.ds(block * LANES, LANES)
        part = column(scale, block)
        scale_ref[rows, :] = jnp.concatenate([part, part], axis=1)
        part = column(lses, block)
        lse_ref[rows, :] = jnp.concatenate([part, part], axis=1)
    total_ref[...] = jnp.zeros_like(total_ref)
    step = 2 * LANES
    for chunk in range(protos_ref.shape[0] // step):
        part = pl.ds(chunk * step, step)
        block = protos_ref[part, :]
        scores = dot_nt(stud_ref[...], block) * STUDENT_SCALE
        student = jnp.exp(scores - lse_ref[...]) * STUDENT_SCALE
        target = exp_ref[:, part] * scale_ref[...] * wide(weights[2 * chunk : 2 * chunk + 2, :])
        grads = (student - target).astype(BF16)
        grad_ref[:, part] = grads
        total_ref[...] += dot_nn(grads, block)
    onehot = place_onehot(slot_ref[:1, :], tokens)
    slots = dot_tn(onehot, total_ref[...].astype(BF16)).astype(BF16)
    tok_ref[...] = slots.reshape(tok_ref.shape)


def proto_kernel(place_ref, grad_ref, stud_ref, near_ref, far_ref):
    share = near_ref.shape[1]
    group = place_ref[0]
    for away in range(PROTO // 2):
        x = lax.rem(group // 2 + away, PROTO // 2)
        core = lax.rem(group, 2)
        start = pl.multiple_of((2 * x + 1 - core) * share, share)
        far_ref[away, :, :] = dot_tn(grad_ref[:, pl.ds(start, share)], stud_ref[...])
        start = pl.multiple_of((2 * x + core) * share, share)
        near_ref[away, :, :] = dot_tn(grad_ref[:, pl.ds(start, share)], stud_ref[...])


def sum_kernel(parts_ref, out_ref):
    total = jnp.sum(parts_ref[...].astype(F32), axis=0)
    out_ref[...] = jnp.broadcast_to(total[None], out_ref.shape)


def spread_kernel(place_ref, count_ref, mask_ref, rows_ref, out_ref):
    patches, width = out_ref.shape
    device = place_ref[1]
    wanted = iota((patches, CAP), 1)
    rank = (wanted % SLOTS) * PROTO + row_offset(wanted // SLOTS, device)
    at = (iota((patches, CAP), 0) == rank).astype(F32)
    mask = jnp.broadcast_to(mask_ref[...].astype(F32), (8, patches))
    chosen = (dot_nn(mask, at, HIGH)[:1] + 0.5).astype(jnp.int32)
    chosen = jnp.where(rank[:1, :] < count_ref[0], chosen, -1)
    onehot = (iota((patches, CAP), 0) == chosen).astype(F32)
    out_ref[...] = dot_nn(onehot, rows_ref[...].reshape(CAP, width), HIGH)


def call(kernel, outs, inputs, scalars=0, scratch=()):
    smem = [pl.BlockSpec(memory_space=pltpu.SMEM)] * scalars
    vmem = [pl.BlockSpec(memory_space=pltpu.VMEM)] * (len(inputs) - scalars)
    return pl.pallas_call(
        kernel,
        out_shape=[jax.ShapeDtypeStruct(shape, dtype) for shape, dtype in outs],
        in_specs=smem + vmem,
        out_specs=[pl.BlockSpec(memory_space=pltpu.VMEM)] * len(outs),
        scratch_shapes=list(scratch),
        compiler_params=pltpu.CompilerParams(vmem_limit_bytes=VMEM),
    )(*inputs)


def exchange(parts, axis):
    return lax.all_to_all(parts, axis, 0, 0, tiled=True)


def on_device(devices, teacher_patches, student_patches, prototypes, mask_index, counts):
    patches, width = teacher_patches.shape
    share = prototypes.shape[0]
    protos_held = PROTO * share
    chunks = protos_held // LANES
    tokens = -(-(BAL * devices // PROTO + devices) // LANES) * LANES
    group = lax.axis_index("proto")
    device = lax.axis_index("tok")
    place = jnp.stack([group, device]).astype(jnp.int32)

    half = PROTO // 2
    swap = [(p, p ^ 1) for p in range(PROTO)]
    routes = [[(p, (p + 2 * away) % PROTO) for p in range(PROTO)] for away in range(half)]
    (pay,) = pl.pallas_call(
        pick_kernel,
        out_shape=[jax.ShapeDtypeStruct((devices, 2 * SLOTS, width), BF16)],
        in_specs=[
            pl.BlockSpec(memory_space=pltpu.SMEM),
            pl.BlockSpec(memory_space=pltpu.SMEM),
            pl.BlockSpec(memory_space=pltpu.VMEM),
            pl.BlockSpec(memory_space=pl.ANY),
            pl.BlockSpec(memory_space=pl.ANY),
        ],
        out_specs=[pl.BlockSpec(memory_space=pltpu.VMEM)],
        scratch_shapes=[pltpu.VMEM((2, patches, width), BF16), pltpu.SemaphoreType.DMA((2,))],
        compiler_params=pltpu.CompilerParams(vmem_limit_bytes=VMEM),
    )(place, counts, mask_index, teacher_patches, student_patches)
    pay = exchange(pay, "tok")
    near = [lax.ppermute(prototypes, "proto", routes[-away % half]) for away in range(1, half)]
    near = jnp.stack([prototypes] + near)
    far = lax.ppermute(near, "proto", swap)

    packed = ((8, LANES), F32)
    col_out = ((PROTO, chunks, LANES), F32)
    row_out = ((devices, 8, LANES), F32)
    teach, stud, protos, slots, valid, col = call(
        first_kernel,
        [
            ((tokens, width), BF16),
            ((tokens, width), BF16),
            ((protos_held, width), BF16),
            ((8, devices * SLOTS), F32),
            packed,
            col_out,
        ],
        (place, pay, near, far),
        scalars=1,
    )
    col = exchange(col, "proto")
    exps, top, row = call(
        second_kernel, [((tokens, protos_held), F32), packed, row_out], (teach, protos, col)
    )
    row = exchange(row, "tok")
    factor, col = call(third_kernel, [packed, col_out], (exps, top, valid, row))
    col = exchange(col, "proto")
    (row,) = call(row_kernel, [row_out], (exps, factor, col))
    row = exchange(row, "tok")
    (col,) = call(column_kernel, [col_out], (exps, factor, valid, row))
    col = exchange(col, "proto")
    (stud_row,) = call(student_kernel, [packed], (protos, stud))
    (row,) = call(
        last_row_kernel, [((devices, 16, LANES), F32)], (exps, factor, col, stud_row)
    )
    row = exchange(row, "tok")
    grad_slots, grads = call(
        gradient_kernel,
        [((devices, SLOTS, width), BF16), ((tokens, protos_held), BF16)],
        (exps, factor, valid, col, row, stud, protos, slots),
        scratch=(
            pltpu.VMEM((tokens, share), F32),
            pltpu.VMEM((tokens, share), F32),
            pltpu.VMEM((tokens, width), F32),
        ),
    )
    near, far = call(
        proto_kernel,
        [((half, share, width), F32), ((half, share, width), F32)],
        (place, grads, stud),
        scalars=1,
    )
    mine = near + lax.ppermute(far, "proto", swap)
    grad_prototypes = mine[0]
    for away in range(1, half):
        grad_prototypes = grad_prototypes + lax.ppermute(mine[away], "proto", routes[away])

    (rows,) = call(sum_kernel, [((PROTO, SLOTS, width), F32)], (exchange(grad_slots, "tok"),))
    rows = exchange(rows, "proto")
    (grad_patches,) = call(
        spread_kernel, [((patches, width), F32)], (place, counts, mask_index, rows), scalars=2
    )
    return (grad_patches, grad_prototypes)


def solution(mesh):
    return jax.shard_map(
        functools.partial(on_device, mesh.shape["tok"]),
        mesh=mesh,
        in_specs=(
            P("tok", None),
            P("tok", None),
            P(("proto", "tok"), None),
            P("tok", None),
            P("tok"),
        ),
        out_specs=(P("tok", None), P(("proto", "tok"), None)),
        check_vma=False,
    )
```

```python
import functools
import math

import jax
import jax.numpy as jnp
from jax import lax
from jax.experimental import pallas as pl
from jax.experimental.pallas import tpu as pltpu
from jax.sharding import Mesh, PartitionSpec as P

CAP = 256
BAL = 128
PROTO = 8
SLOTS = CAP // PROTO
ROWS = 4
TOK = ("y", "z")
LANES = 128
TEACHER_SCALE = 1.0 / 0.07
STUDENT_SCALE = 1.0 / 0.1
FAR_BELOW = -1e30
VMEM = 24 * 1024 * 1024
F32 = jnp.float32
BF16 = jnp.bfloat16
HIGH = lax.Precision.HIGHEST


def iota(shape, dim):
    return lax.broadcasted_iota(jnp.int32, shape, dim)


def dot_nt(a, b, precision=None):
    return lax.dot_general(
        a, b, (((1,), (1,)), ((), ())), precision=precision, preferred_element_type=F32
    )


def dot_tn(a, b, precision=None):
    return lax.dot_general(
        a, b, (((0,), (0,)), ((), ())), precision=precision, preferred_element_type=F32
    )


def dot_nn(a, b, precision=None):
    return jnp.dot(a, b, precision=precision, preferred_element_type=F32)


def blocks(tokens):
    return [(at // LANES, slice(at, min(at + LANES, tokens))) for at in range(0, tokens, LANES)]


def turned(rows, block, first_lane_only):
    at = iota((8, LANES), 0) == block
    if first_lane_only:
        at = at & (iota((8, LANES), 1) == 0)
    short = LANES - rows.shape[0]
    if short:
        rows = jnp.concatenate([rows, jnp.zeros((short, LANES), F32)], axis=0)
    return dot_nt(at.astype(F32), rows, HIGH)


def column(packed, block, size):
    at = (iota((8, LANES), 0) == block).astype(F32)
    return dot_tn(packed, at, HIGH)[:size]


def lse_over_first(values):
    top = jnp.max(values, axis=0)
    return top + jnp.log(jnp.sum(jnp.exp(values - top[None]), axis=0))


def row_offset(group, device):
    return lax.rem(group + device, PROTO)


def pick_kernel(place_ref, count_ref, mask_ref, teacher_ref, student_ref, pay_ref, patch_ref, sem_ref):
    copies = [
        pltpu.make_async_copy(source, patch_ref.at[which], sem_ref.at[which])
        for which, source in enumerate((teacher_ref, student_ref))
    ]
    for copy in copies:
        copy.start()
    patches, width = teacher_ref.shape
    offset = row_offset(place_ref[0], place_ref[1])
    at = iota((SLOTS, patches), 1) == iota((SLOTS, patches), 0) * PROTO + offset
    mask = jnp.broadcast_to(mask_ref[...].astype(F32), (LANES, patches))
    chosen = dot_nt(at.astype(F32), mask, HIGH)[:, :1]
    chosen = (chosen + 0.5).astype(jnp.int32)
    onehot = (iota((SLOTS, patches), 1) == chosen).astype(BF16)
    held = iota((SLOTS, width), 0) * PROTO + offset < count_ref[0]
    for copy in copies:
        copy.wait()
    teach = jnp.where(held, dot_nn(onehot, patch_ref[0]), jnp.inf).astype(BF16)
    stud = dot_nn(onehot, patch_ref[1]).astype(BF16)
    both = jnp.concatenate([teach, stud], axis=0)
    pay_ref[...] = jnp.broadcast_to(both[None], pay_ref.shape)


def place_onehot(place, tokens):
    return (iota((tokens, place.shape[1]), 0).astype(F32) == place).astype(BF16)


def prototypes_kernel(place_ref, near_ref, far_ref, protos_ref):
    share = near_ref.shape[1]
    group = place_ref[0]
    for away in range(PROTO // 2):
        x = lax.rem(group // 2 + away, PROTO // 2)
        core = lax.rem(group, 2)
        start = pl.multiple_of((2 * x + core) * share, share)
        protos_ref[pl.ds(start, share), :] = near_ref[away]
        start = pl.multiple_of((2 * x + 1 - core) * share, share)
        protos_ref[pl.ds(start, share), :] = far_ref[away]


def first_kernel(*refs):
    place_ref, *line_refs = refs[: ROWS + 1]
    protos_ref, teach_ref, stud_ref, place_out_ref, valid_ref, col_ref, pay_ref = refs[ROWS + 1 :]
    line, _, width = line_refs[0].shape
    devices = ROWS * line
    tokens = teach_ref.shape[0]
    for away in range(ROWS):
        y = lax.rem(place_ref[2] + away, ROWS)
        pay_ref[pl.ds(y * line, line), :, :] = line_refs[away][...]
    slots = devices * SLOTS
    arrived = pay_ref[:, :SLOTS, :].reshape(slots, width).astype(F32)
    real = arrived < jnp.inf
    pick = (iota((8, width), 1) == 0).astype(BF16)
    flags = dot_nt(pick, real.astype(F32).astype(BF16))
    held = dot_nn(
        flags.astype(BF16), (iota((slots, LANES), 0) // SLOTS == iota((slots, LANES), 1)).astype(BF16)
    )
    before = dot_nn(
        held.astype(BF16), (iota((LANES, slots), 0) < iota((LANES, slots), 1) // SLOTS).astype(BF16)
    )[:1]
    inner = (iota((1, slots), 1) % SLOTS).astype(F32)
    place = jnp.where(flags[:1] > 0.5, before + inner, -1.0)
    place_out_ref[...] = jnp.broadcast_to(place, place_out_ref.shape)
    total = jnp.max(place, axis=1, keepdims=True) + 1.0
    order = iota((8, LANES), 0) * LANES + iota((8, LANES), 1)
    valid_ref[...] = (order.astype(F32) < total).astype(F32)
    onehot = place_onehot(place, tokens)
    teach = dot_nn(onehot, jnp.where(real, arrived, 0.0).astype(BF16)).astype(BF16)
    teach_ref[...] = teach
    stud_ref[...] = dot_nn(onehot, pay_ref[:, SLOTS:, :].reshape(slots, width)).astype(BF16)
    step = 2 * LANES
    alive = iota((tokens, step), 0).astype(F32) < total
    rows = []
    for start in range(0, protos_ref.shape[0], step):
        scores = dot_nt(teach, protos_ref[start : start + step, :]) * TEACHER_SCALE
        scores = jnp.where(alive, scores, FAR_BELOW)
        top = jnp.max(scores, axis=0, keepdims=True)
        lse = top + jnp.log(jnp.sum(jnp.exp(scores - top), axis=0, keepdims=True))
        rows += [lse[:, :LANES], lse[:, LANES:]]
    col_ref[...] = jnp.broadcast_to(jnp.concatenate(rows, axis=0)[None], col_ref.shape)


def wide(packed):
    return jnp.concatenate([packed[i : i + 1, :] for i in range(packed.shape[0])], axis=1)


def exps_below_top(left_ref, rows, protos_ref, scale, shift, out_ref, out_rows):
    step = 2 * LANES
    tops = None
    for start in range(0, protos_ref.shape[0], step):
        scores = dot_nt(left_ref[rows, :], protos_ref[start : start + step, :]) * scale
        if shift is not None:
            scores = scores + shift[:, start : start + step]
        out_ref[out_rows, start : start + step] = scores
        top = jnp.maximum(scores[:, :LANES], scores[:, LANES:])
        tops = top if tops is None else jnp.maximum(tops, top)
    top = jnp.broadcast_to(jnp.max(tops, axis=1, keepdims=True), tops.shape)
    sums = jnp.zeros_like(tops)
    for start in range(0, protos_ref.shape[0], LANES):
        exps = jnp.exp(out_ref[out_rows, start : start + LANES] - top)
        out_ref[out_rows, start : start + LANES] = exps
        sums += exps
    return top, sums


def second_kernel(teach_ref, protos_ref, col_ref, exp_ref, top_ref, row_ref):
    col_pot = -wide(lse_over_first(col_ref[...]))
    tops = jnp.zeros((8, LANES), F32)
    totals = jnp.zeros((8, LANES), F32)
    for block, rows in blocks(teach_ref.shape[0]):
        top, sums = exps_below_top(teach_ref, rows, protos_ref, TEACHER_SCALE, col_pot, exp_ref, rows)
        tops += turned(top, block, True)
        totals += turned(sums, block, False)
    top_ref[...] = tops
    lses = tops + jnp.log(jnp.where(totals > 0.0, totals, 1.0))
    row_ref[...] = jnp.broadcast_to(lses[None], row_ref.shape)


def weighted_columns(exp_ref, weight):
    chunks = exp_ref.shape[1] // LANES
    sums = [jnp.zeros((8, LANES), F32) for _ in range(chunks)]
    for block, rows in blocks(exp_ref.shape[0]):
        size = rows.stop - rows.start
        factor = column(weight, block, size)
        for chunk in range(chunks):
            part = exp_ref[rows, chunk * LANES : (chunk + 1) * LANES] * factor
            sums[chunk] += jnp.sum(part.reshape(size // 8, 8, LANES), axis=0)
    return jnp.concatenate([jnp.sum(part, axis=0, keepdims=True) for part in sums], axis=0)


def third_kernel(exp_ref, top_ref, valid_ref, row_ref, factor_ref, col_ref):
    row_pot = -lse_over_first(row_ref[...])
    factor = jnp.where(valid_ref[...] > 0.0, jnp.exp(top_ref[...] + row_pot), 0.0)
    factor_ref[...] = factor
    col_ref[...] = jnp.broadcast_to(weighted_columns(exp_ref, factor)[None], col_ref.shape)


def row_scale(valid_ref, sums):
    alive = valid_ref[...] > 0.0
    return jnp.where(alive, 1.0 / jnp.where(alive, sums, 1.0), 0.0)


def column_kernel(exp_ref, factor_ref, valid_ref, row_ref, col_ref):
    weight = row_scale(valid_ref, jnp.sum(row_ref[...], axis=0)) * factor_ref[...]
    col_ref[...] = jnp.broadcast_to(weighted_columns(exp_ref, weight)[None], col_ref.shape)


def weighted_rows(exp_ref, weight):
    sums = jnp.zeros((8, LANES), F32)
    for block, rows in blocks(exp_ref.shape[0]):
        part = jnp.zeros((rows.stop - rows.start, LANES), F32)
        for chunk in range(weight.shape[0]):
            values = exp_ref[rows, chunk * LANES : (chunk + 1) * LANES]
            part += values * weight[chunk : chunk + 1, :]
        sums += turned(part, block, False)
    return sums


def row_kernel(exp_ref, factor_ref, col_ref, row_ref):
    weight = 1.0 / jnp.sum(col_ref[...], axis=0)
    sums = weighted_rows(exp_ref, weight) * factor_ref[...]
    row_ref[...] = jnp.broadcast_to(sums[None], row_ref.shape)


def student_kernel(protos_ref, stud_ref, row_ref, exp_ref):
    tops = jnp.zeros((8, LANES), F32)
    totals = jnp.zeros((8, LANES), F32)
    for block, rows in blocks(stud_ref.shape[0]):
        out_rows = slice(0, rows.stop - rows.start)
        top, sums = exps_below_top(
            stud_ref, rows, protos_ref, STUDENT_SCALE, None, exp_ref.at[block % 2], out_rows
        )
        tops += turned(top, block, True)
        totals += turned(sums, block, False)
    row_ref[...] = tops + jnp.log(jnp.where(totals > 0.0, totals, 1.0))


def last_row_kernel(exp_ref, factor_ref, col_ref, stud_row_ref, row_ref):
    weight = 1.0 / jnp.sum(col_ref[...], axis=0)
    sums = weighted_rows(exp_ref, weight) * factor_ref[...]
    both = jnp.concatenate([sums, stud_row_ref[...]], axis=0)
    row_ref[...] = jnp.broadcast_to(both[None], row_ref.shape)


def gradient_kernel(
    exp_ref, factor_ref, valid_ref, col_ref, row_ref, stud_ref, protos_ref, slot_ref,
    tok_ref, grad_ref,
):
    tokens, width = stud_ref.shape
    weights = 1.0 / jnp.sum(col_ref[...], axis=0)
    sums = jnp.sum(row_ref[:, :8, :], axis=0)
    scale = row_scale(valid_ref, sums) * (factor_ref[...] * STUDENT_SCALE)
    lses = lse_over_first(row_ref[:, 8:, :]) - math.log(STUDENT_SCALE)
    lses = jnp.where(valid_ref[...] > 0.0, lses, -FAR_BELOW)
    step = 2 * LANES
    for block, rows in blocks(tokens):
        size = rows.stop - rows.start
        row_factor = column(scale, block, size)
        row_lse = column(lses, block, size)
        for chunk in range(protos_ref.shape[0] // step):
            scores = dot_nt(stud_ref[rows, :], protos_ref[chunk * step : (chunk + 1) * step, :])
            for half in range(2):
                index = 2 * chunk + half
                lanes = slice(index * LANES, (index + 1) * LANES)
                part = scores[:, half * LANES : (half + 1) * LANES] * STUDENT_SCALE
                student = jnp.exp(part - row_lse)
                target = exp_ref[rows, lanes] * row_factor * weights[index : index + 1, :]
                grad_ref[rows, lanes] = (student - target).astype(BF16)
    total = dot_nn(grad_ref[...], protos_ref[...])
    onehot = place_onehot(slot_ref[:1, :], tokens)
    slots = dot_tn(onehot, total.astype(BF16)).astype(BF16)
    tok_ref[...] = slots.reshape(tok_ref.shape)


def proto_kernel(place_ref, grad_ref, stud_ref, near_ref, far_ref):
    share = near_ref.shape[1]
    group = place_ref[0]
    for away in range(PROTO // 2):
        x = lax.rem(group // 2 + away, PROTO // 2)
        core = lax.rem(group, 2)
        start = pl.multiple_of((2 * x + 1 - core) * share, share)
        far_ref[away, :, :] = dot_tn(grad_ref[:, pl.ds(start, share)], stud_ref[...])
        start = pl.multiple_of((2 * x + core) * share, share)
        near_ref[away, :, :] = dot_tn(grad_ref[:, pl.ds(start, share)], stud_ref[...])


def sum_kernel(parts_ref, out_ref):
    total = jnp.sum(parts_ref[...].astype(F32), axis=0)
    out_ref[...] = jnp.broadcast_to(total[None], out_ref.shape)


def patch_kernel(place_ref, count_ref, mask_ref, onehot_ref):
    patches = onehot_ref.shape[0]
    device = place_ref[1]
    wanted = iota((patches, CAP), 1)
    rank = (wanted % SLOTS) * PROTO + row_offset(wanted // SLOTS, device)
    at = (iota((patches, CAP), 0) == rank).astype(F32)
    mask = jnp.broadcast_to(mask_ref[...].astype(F32), (8, patches))
    chosen = (dot_nn(mask, at, HIGH)[:1] + 0.5).astype(jnp.int32)
    chosen = jnp.where(rank[:1, :] < count_ref[0], chosen, -1)
    onehot_ref[...] = (iota((patches, CAP), 0) == chosen).astype(BF16)


def spread_kernel(onehot_ref, rows_ref, out_ref):
    rest = rows_ref[...].reshape(CAP, out_ref.shape[1])
    total = None
    for _ in range(3):
        part = rest.astype(BF16)
        rest = rest - part.astype(F32)
        moved = dot_nn(onehot_ref[...], part)
        total = moved if total is None else total + moved
    out_ref[...] = total


def call(kernel, outs, inputs, scalars=0, scratch=(), vmem=VMEM):
    smem = [pl.BlockSpec(memory_space=pltpu.SMEM)] * scalars
    arrays = [pl.BlockSpec(memory_space=pltpu.VMEM)] * (len(inputs) - scalars)
    return pl.pallas_call(
        kernel,
        out_shape=[jax.ShapeDtypeStruct(shape, dtype) for shape, dtype in outs],
        in_specs=smem + arrays,
        out_specs=[pl.BlockSpec(memory_space=pltpu.VMEM)] * len(outs),
        scratch_shapes=list(scratch),
        compiler_params=pltpu.CompilerParams(vmem_limit_bytes=vmem),
    )(*inputs)


def most_tokens(devices):
    slack = sum((PROTO - 1 - device % PROTO) for device in range(devices))
    return -(-((BAL * devices + slack) // PROTO) // 16) * 16


def exchange(parts, axis):
    return lax.all_to_all(parts, axis, 0, 0, tiled=True)


def on_device(devices, teacher_patches, student_patches, prototypes, mask_index, counts):
    patches, width = teacher_patches.shape
    share = prototypes.shape[0]
    protos_held = PROTO * share
    chunks = protos_held // LANES
    tokens = most_tokens(devices)
    line = devices // ROWS
    group = lax.axis_index("proto")
    y = lax.axis_index("y")
    device = y * line + lax.axis_index("z")
    place = jnp.stack([group, device, y]).astype(jnp.int32)

    half = PROTO // 2
    swap = [(p, p ^ 1) for p in range(PROTO)]
    routes = [[(p, (p + 2 * away) % PROTO) for p in range(PROTO)] for away in range(half)]
    (pay,) = pl.pallas_call(
        pick_kernel,
        out_shape=[jax.ShapeDtypeStruct((line, 2 * SLOTS, width), BF16)],
        in_specs=[
            pl.BlockSpec(memory_space=pltpu.SMEM),
            pl.BlockSpec(memory_space=pltpu.SMEM),
            pl.BlockSpec(memory_space=pltpu.VMEM),
            pl.BlockSpec(memory_space=pl.ANY),
            pl.BlockSpec(memory_space=pl.ANY),
        ],
        out_specs=[pl.BlockSpec(memory_space=pltpu.VMEM)],
        scratch_shapes=[pltpu.VMEM((2, patches, width), BF16), pltpu.SemaphoreType.DMA((2,))],
        compiler_params=pltpu.CompilerParams(vmem_limit_bytes=60 * 1024 * 1024),
    )(place, counts, mask_index, teacher_patches, student_patches)
    pay = exchange(pay, "z")
    lines = [pay]
    for away in range(1, ROWS):
        route = [(i, (i - away) % ROWS) for i in range(ROWS)]
        lines.append(lax.ppermute(pay, "y", route))
    near = [lax.ppermute(prototypes, "proto", routes[-away % half]) for away in range(1, half)]
    near = jnp.stack([prototypes] + near)
    far = lax.ppermute(near, "proto", swap)
    (protos,) = call(
        prototypes_kernel, [((protos_held, width), BF16)], (place, near, far), scalars=1
    )
    (onehot,) = call(
        patch_kernel, [((patches, CAP), BF16)], (place, counts, mask_index), scalars=2
    )

    packed = ((8, LANES), F32)
    col_out = ((PROTO, chunks, LANES), F32)
    row_out = ((devices, 8, LANES), F32)
    teach, stud, slots, valid, col = call(
        first_kernel,
        [
            ((tokens, width), BF16),
            ((tokens, width), BF16),
            ((8, devices * SLOTS), F32),
            packed,
            col_out,
        ],
        (place, *lines, protos),
        scalars=1,
        scratch=(pltpu.VMEM((devices, 2 * SLOTS, width), BF16),),
    )
    col = exchange(col, "proto")
    exps, top, row = call(
        second_kernel, [((tokens, protos_held), F32), packed, row_out], (teach, protos, col)
    )
    row = exchange(row, TOK)
    factor, col = call(third_kernel, [packed, col_out], (exps, top, valid, row))
    col = exchange(col, "proto")
    (row,) = call(row_kernel, [row_out], (exps, factor, col))
    row = exchange(row, TOK)
    (col,) = call(column_kernel, [col_out], (exps, factor, valid, row))
    col = exchange(col, "proto")
    (stud_row,) = call(
        student_kernel,
        [packed],
        (protos, stud),
        scratch=(pltpu.VMEM((2, LANES, protos_held), F32),),
    )
    (row,) = call(
        last_row_kernel, [((devices, 16, LANES), F32)], (exps, factor, col, stud_row)
    )
    row = exchange(row, TOK)
    grad_slots, grads = call(
        gradient_kernel,
        [((devices, SLOTS, width), BF16), ((tokens, protos_held), BF16)],
        (exps, factor, valid, col, row, stud, protos, slots),
    )
    near, far = call(
        proto_kernel,
        [((half, share, width), F32), ((half, share, width), F32)],
        (place, grads, stud),
        scalars=1,
    )
    mine = near + lax.ppermute(far, "proto", swap)
    grad_prototypes = mine[0]
    for away in range(1, half):
        grad_prototypes = grad_prototypes + lax.ppermute(mine[away], "proto", routes[away])

    (rows,) = call(sum_kernel, [((PROTO, SLOTS, width), F32)], (exchange(grad_slots, TOK),))
    rows = exchange(rows, "proto")
    (grad_patches,) = call(spread_kernel, [((patches, width), F32)], (onehot, rows))
    return (grad_patches, grad_prototypes)


def solution(mesh):
    devices, protos = mesh.devices.shape
    shape = (ROWS, devices // ROWS, protos)
    mesh = Mesh(mesh.devices.reshape(shape), (*TOK, "proto"))
    return jax.shard_map(
        functools.partial(on_device, devices),
        mesh=mesh,
        in_specs=(
            P(TOK, None),
            P(TOK, None),
            P(("proto", *TOK), None),
            P(TOK, None),
            P(TOK),
        ),
        out_specs=(P(TOK, None), P(("proto", *TOK), None)),
        check_vma=False,
    )
```

```python
import functools
import math

import jax
import jax.numpy as jnp
from jax import lax
from jax.experimental import pallas as pl
from jax.experimental.pallas import tpu as pltpu
from jax.sharding import Mesh, PartitionSpec as P

CAP = 256
BAL = 128
PROTO = 8
SLOTS = CAP // PROTO
ROWS = 4
TOK = ("y", "z")
LANES = 128
TEACHER_SCALE = 1.0 / 0.07
STUDENT_SCALE = 1.0 / 0.1
FAR_BELOW = -1e30
VMEM = 24 * 1024 * 1024
F32 = jnp.float32
BF16 = jnp.bfloat16
HIGH = lax.Precision.HIGHEST


def iota(shape, dim):
    return lax.broadcasted_iota(jnp.int32, shape, dim)


def dot_nt(a, b, precision=None):
    return lax.dot_general(
        a, b, (((1,), (1,)), ((), ())), precision=precision, preferred_element_type=F32
    )


def dot_tn(a, b, precision=None):
    return lax.dot_general(
        a, b, (((0,), (0,)), ((), ())), precision=precision, preferred_element_type=F32
    )


def dot_nn(a, b, precision=None):
    return jnp.dot(a, b, precision=precision, preferred_element_type=F32)


def blocks(tokens):
    return [(at // LANES, slice(at, min(at + LANES, tokens))) for at in range(0, tokens, LANES)]


def turned(rows, block, first_lane_only):
    at = iota((8, LANES), 0) == block
    if first_lane_only:
        at = at & (iota((8, LANES), 1) == 0)
    short = LANES - rows.shape[0]
    if short:
        rows = jnp.concatenate([rows, jnp.zeros((short, LANES), F32)], axis=0)
    return dot_nt(at.astype(F32), rows, HIGH)


def column(packed, block, size):
    at = (iota((8, LANES), 0) == block).astype(F32)
    return dot_tn(packed, at, HIGH)[:size]


def lse_over_first(values):
    top = jnp.max(values, axis=0)
    return top + jnp.log(jnp.sum(jnp.exp(values - top[None]), axis=0))


def row_offset(group, device):
    return lax.rem(group + device, PROTO)


def pick_kernel(
    place_ref, count_ref, mask_ref, teacher_ref, student_ref, protos_ref,
    pay_ref, own_ref, patch_ref, sem_ref,
):
    sources = (teacher_ref, student_ref, protos_ref)
    targets = (patch_ref.at[0], patch_ref.at[1], own_ref)
    copies = [
        pltpu.make_async_copy(source, target, sem_ref.at[which])
        for which, (source, target) in enumerate(zip(sources, targets))
    ]
    for copy in copies:
        copy.start()
    patches, width = teacher_ref.shape
    offset = row_offset(place_ref[0], place_ref[1])
    at = (iota((SLOTS, patches), 1) == iota((SLOTS, patches), 0) * PROTO + offset).astype(BF16)
    mask = jnp.broadcast_to(mask_ref[...], (LANES, patches))
    high = dot_nt(at, (mask // 256).astype(F32).astype(BF16))
    low = dot_nt(at, (mask % 256).astype(F32).astype(BF16))
    chosen = (high * 256.0 + low + 0.5).astype(jnp.int32)
    lane = iota((SLOTS, LANES), 1)
    onehot = jnp.concatenate(
        [(lane + start == chosen).astype(F32).astype(BF16) for start in range(0, patches, LANES)],
        axis=1,
    )
    held = iota((SLOTS, width), 0) * PROTO + offset < count_ref[0]
    copies[0].wait()
    teach = jnp.where(held, dot_nn(onehot, patch_ref[0]), jnp.inf).astype(BF16)
    copies[1].wait()
    stud = dot_nn(onehot, patch_ref[1]).astype(BF16)
    both = jnp.concatenate([teach, stud], axis=0)
    pay_ref[...] = jnp.broadcast_to(both[None], pay_ref.shape)
    copies[2].wait()


def place_onehot(place, tokens):
    return (iota((tokens, place.shape[1]), 0).astype(F32) == place).astype(BF16)


def prototypes_kernel(place_ref, near_ref, far_ref, protos_ref):
    share = near_ref.shape[1]
    group = place_ref[0]
    for away in range(PROTO // 2):
        x = lax.rem(group // 2 + away, PROTO // 2)
        core = lax.rem(group, 2)
        start = pl.multiple_of((2 * x + core) * share, share)
        protos_ref[pl.ds(start, share), :] = near_ref[away]
        start = pl.multiple_of((2 * x + 1 - core) * share, share)
        protos_ref[pl.ds(start, share), :] = far_ref[away]


def in_order(y, line_refs, pay_ref):
    line = line_refs[0].shape[0]
    for away in range(ROWS):
        start = lax.rem(y + away, ROWS) * line
        pay_ref[pl.ds(start, line), :, :] = line_refs[away][...]
    devices, slots, width = pay_ref.shape
    return pay_ref[...].reshape(devices * slots, width)


def first_kernel(*refs):
    place_ref, *line_refs = refs[: ROWS + 1]
    protos_ref, teach_ref, place_out_ref, valid_ref, col_ref, pay_ref = refs[ROWS + 1 :]
    arrived = in_order(place_ref[2], line_refs, pay_ref).astype(F32)
    tokens = teach_ref.shape[0]
    slots, width = arrived.shape
    real = arrived < jnp.inf
    pick = (iota((8, width), 1) == 0).astype(BF16)
    flags = dot_nt(pick, real.astype(F32).astype(BF16))
    held = dot_nn(
        flags.astype(BF16), (iota((slots, LANES), 0) // SLOTS == iota((slots, LANES), 1)).astype(BF16)
    )
    before = dot_nn(
        held.astype(BF16), (iota((LANES, slots), 0) < iota((LANES, slots), 1) // SLOTS).astype(BF16)
    )[:1]
    inner = (iota((1, slots), 1) % SLOTS).astype(F32)
    place = jnp.where(flags[:1] > 0.5, before + inner, -1.0)
    place_out_ref[...] = jnp.broadcast_to(place, place_out_ref.shape)
    total = jnp.max(place, axis=1, keepdims=True) + 1.0
    order = iota((8, LANES), 0) * LANES + iota((8, LANES), 1)
    valid_ref[...] = (order.astype(F32) < total).astype(F32)
    onehot = place_onehot(place, tokens)
    teach = dot_nn(onehot, jnp.where(real, arrived, 0.0).astype(BF16)).astype(BF16)
    teach_ref[...] = teach
    step = 2 * LANES
    alive = iota((tokens, step), 0).astype(F32) < total
    rows = []
    for start in range(0, protos_ref.shape[0], step):
        scores = dot_nt(teach, protos_ref[start : start + step, :]) * TEACHER_SCALE
        scores = jnp.where(alive, scores, FAR_BELOW)
        top = jnp.max(scores, axis=0, keepdims=True)
        lse = top + jnp.log(jnp.sum(jnp.exp(scores - top), axis=0, keepdims=True))
        rows += [lse[:, :LANES], lse[:, LANES:]]
    col_ref[...] = jnp.broadcast_to(jnp.concatenate(rows, axis=0)[None], col_ref.shape)


def wide(packed):
    return jnp.concatenate([packed[i : i + 1, :] for i in range(packed.shape[0])], axis=1)


def exps_below_top(left_ref, protos_ref, scale, shift, out_ref):
    step = 2 * LANES
    for start in range(0, protos_ref.shape[0], step):
        scores = dot_nt(left_ref[...], protos_ref[start : start + step, :]) * scale
        if shift is not None:
            scores = scores + shift[:, start : start + step]
        out_ref[:, start : start + step] = scores
    tops = jnp.zeros((8, LANES), F32)
    totals = jnp.zeros((8, LANES), F32)
    starts = range(0, protos_ref.shape[0], LANES)
    for block, rows in blocks(left_ref.shape[0]):
        top = out_ref[rows, :LANES]
        for start in starts[1:]:
            top = jnp.maximum(top, out_ref[rows, start : start + LANES])
        top = jnp.broadcast_to(jnp.max(top, axis=1, keepdims=True), top.shape)
        sums = jnp.zeros_like(top)
        for start in starts:
            exps = jnp.exp(out_ref[rows, start : start + LANES] - top)
            out_ref[rows, start : start + LANES] = exps
            sums += exps
        tops += turned(top, block, True)
        totals += turned(sums, block, False)
    return tops, totals


def second_kernel(teach_ref, protos_ref, col_ref, stud_row_ref, exp_ref, top_ref, row_ref, stud_out_ref):
    col_pot = -wide(lse_over_first(col_ref[...]))
    tops, totals = exps_below_top(teach_ref, protos_ref, TEACHER_SCALE, col_pot, exp_ref)
    top_ref[...] = tops
    lses = tops + jnp.log(jnp.where(totals > 0.0, totals, 1.0))
    row_ref[...] = jnp.broadcast_to(lses[None], row_ref.shape)
    stud_out_ref[...] = stud_row_ref[...]


def weighted_columns(exp_ref, weight):
    chunks = exp_ref.shape[1] // LANES
    sums = [jnp.zeros((8, LANES), F32) for _ in range(chunks)]
    for block, rows in blocks(exp_ref.shape[0]):
        size = rows.stop - rows.start
        factor = column(weight, block, size)
        for chunk in range(chunks):
            part = exp_ref[rows, chunk * LANES : (chunk + 1) * LANES] * factor
            sums[chunk] += jnp.sum(part.reshape(size // 8, 8, LANES), axis=0)
    return jnp.concatenate([jnp.sum(part, axis=0, keepdims=True) for part in sums], axis=0)


def third_kernel(exp_ref, top_ref, valid_ref, row_ref, factor_ref, col_ref):
    row_pot = -lse_over_first(row_ref[...])
    factor = jnp.where(valid_ref[...] > 0.0, jnp.exp(top_ref[...] + row_pot), 0.0)
    factor_ref[...] = factor
    col_ref[...] = jnp.broadcast_to(weighted_columns(exp_ref, factor)[None], col_ref.shape)


def row_scale(valid_ref, sums):
    alive = valid_ref[...] > 0.0
    return jnp.where(alive, 1.0 / jnp.where(alive, sums, 1.0), 0.0)


def column_kernel(exp_ref, factor_ref, valid_ref, row_ref, col_ref):
    weight = row_scale(valid_ref, jnp.sum(row_ref[...], axis=0)) * factor_ref[...]
    col_ref[...] = jnp.broadcast_to(weighted_columns(exp_ref, weight)[None], col_ref.shape)


def weighted_rows(exp_ref, weight):
    sums = jnp.zeros((8, LANES), F32)
    for block, rows in blocks(exp_ref.shape[0]):
        part = jnp.zeros((rows.stop - rows.start, LANES), F32)
        for chunk in range(weight.shape[0]):
            values = exp_ref[rows, chunk * LANES : (chunk + 1) * LANES]
            part += values * weight[chunk : chunk + 1, :]
        sums += turned(part, block, False)
    return sums


def row_kernel(exp_ref, factor_ref, col_ref, row_ref):
    weight = 1.0 / jnp.sum(col_ref[...], axis=0)
    sums = weighted_rows(exp_ref, weight) * factor_ref[...]
    row_ref[...] = jnp.broadcast_to(sums[None], row_ref.shape)


def student_kernel(*refs):
    place_ref, *line_refs = refs[: ROWS + 1]
    slot_ref, protos_ref, stud_ref, row_ref, pay_ref, exp_ref = refs[ROWS + 1 :]
    arrived = in_order(place_ref[2], line_refs, pay_ref)
    onehot = place_onehot(slot_ref[:1, :], stud_ref.shape[0])
    stud_ref[...] = dot_nn(onehot, arrived).astype(BF16)
    tops, totals = exps_below_top(stud_ref, protos_ref, STUDENT_SCALE, None, exp_ref)
    row_ref[...] = tops + jnp.log(jnp.where(totals > 0.0, totals, 1.0))


def last_row_kernel(exp_ref, factor_ref, col_ref, stud_row_ref, row_ref):
    weight = 1.0 / jnp.sum(col_ref[...], axis=0)
    sums = weighted_rows(exp_ref, weight) * factor_ref[...]
    both = jnp.concatenate([sums, stud_row_ref[...]], axis=0)
    row_ref[...] = jnp.broadcast_to(both[None], row_ref.shape)


def gradient_kernel(
    exp_ref, factor_ref, valid_ref, col_ref, row_ref, stud_ref, protos_ref, slot_ref,
    tok_ref, grad_ref, scale_ref, lse_ref,
):
    tokens, width = stud_ref.shape
    weights = 1.0 / jnp.sum(col_ref[...], axis=0)
    sums = jnp.sum(row_ref[:, :8, :], axis=0)
    scale = row_scale(valid_ref, sums) * (factor_ref[...] * STUDENT_SCALE)
    lses = lse_over_first(row_ref[:, 8:, :]) - math.log(STUDENT_SCALE)
    lses = jnp.where(valid_ref[...] > 0.0, lses, -FAR_BELOW)
    for block, rows in blocks(tokens):
        size = rows.stop - rows.start
        scale_ref[rows, :] = column(scale, block, size)
        lse_ref[rows, :] = column(lses, block, size)
    step = 2 * LANES
    for chunk in range(protos_ref.shape[0] // step):
        scores = dot_nt(stud_ref[...], protos_ref[chunk * step : (chunk + 1) * step, :])
        for half in range(2):
            index = 2 * chunk + half
            lanes = slice(index * LANES, (index + 1) * LANES)
            part = scores[:, half * LANES : (half + 1) * LANES] * STUDENT_SCALE
            student = jnp.exp(part - lse_ref[...])
            target = exp_ref[:, lanes] * scale_ref[...] * weights[index : index + 1, :]
            grad_ref[:, lanes] = (student - target).astype(BF16)
    total = dot_nn(grad_ref[...], protos_ref[...])
    onehot = place_onehot(slot_ref[:1, :], tokens)
    slots = dot_tn(onehot, total.astype(BF16)).astype(BF16)
    tok_ref[...] = slots.reshape(tok_ref.shape)


def proto_kernel(place_ref, grad_ref, stud_ref, near_ref, far_ref):
    share = near_ref.shape[1]
    group = place_ref[0]
    for away in range(PROTO // 2):
        x = lax.rem(group // 2 + away, PROTO // 2)
        core = lax.rem(group, 2)
        start = pl.multiple_of((2 * x + 1 - core) * share, share)
        far_ref[away, :, :] = dot_tn(grad_ref[:, pl.ds(start, share)], stud_ref[...])
        start = pl.multiple_of((2 * x + core) * share, share)
        near_ref[away, :, :] = dot_tn(grad_ref[:, pl.ds(start, share)], stud_ref[...])


def sum_kernel(parts_ref, near_ref, *refs):
    *far_refs, out_ref, proto_ref = refs
    total = jnp.sum(parts_ref[...].astype(F32), axis=0)
    out_ref[...] = jnp.broadcast_to(total[None], out_ref.shape)
    total = near_ref[0]
    for far_ref in far_refs:
        total = total + far_ref[...]
    proto_ref[...] = total


def patch_kernel(place_ref, count_ref, mask_ref, onehot_ref):
    patches = onehot_ref.shape[0]
    device = place_ref[1]
    wanted = iota((patches, CAP), 1)
    rank = (wanted % SLOTS) * PROTO + row_offset(wanted // SLOTS, device)
    at = (iota((patches, CAP), 0) == rank).astype(F32)
    mask = jnp.broadcast_to(mask_ref[...].astype(F32), (8, patches))
    chosen = (dot_nn(mask, at, HIGH)[:1] + 0.5).astype(jnp.int32)
    chosen = jnp.where(rank[:1, :] < count_ref[0], chosen, -1)
    onehot_ref[...] = (iota((patches, CAP), 0) == chosen).astype(BF16)


def spread_kernel(onehot_ref, rows_ref, out_ref):
    rest = rows_ref[...].reshape(CAP, out_ref.shape[1])
    total = None
    for _ in range(3):
        part = rest.astype(BF16)
        rest = rest - part.astype(F32)
        moved = dot_nn(onehot_ref[...], part)
        total = moved if total is None else total + moved
    out_ref[...] = total


def call(kernel, outs, inputs, scalars=0, scratch=(), cost=None):
    smem = [pl.BlockSpec(memory_space=pltpu.SMEM)] * scalars
    arrays = [pl.BlockSpec(memory_space=pltpu.VMEM)] * (len(inputs) - scalars)
    return pl.pallas_call(
        kernel,
        out_shape=[jax.ShapeDtypeStruct(shape, dtype) for shape, dtype in outs],
        in_specs=smem + arrays,
        out_specs=[pl.BlockSpec(memory_space=pltpu.VMEM)] * len(outs),
        scratch_shapes=list(scratch),
        compiler_params=pltpu.CompilerParams(vmem_limit_bytes=VMEM),
        cost_estimate=cost,
    )(*inputs)


def most_tokens(devices):
    slack = sum((PROTO - 1 - device % PROTO) for device in range(devices))
    return -(-((BAL * devices + slack) // PROTO) // 16) * 16


def exchange(parts, axis):
    return lax.all_to_all(parts, axis, 0, 0, tiled=True)


def on_device(devices, teacher_patches, student_patches, prototypes, mask_index, counts):
    patches, width = teacher_patches.shape
    share = prototypes.shape[0]
    protos_held = PROTO * share
    chunks = protos_held // LANES
    tokens = most_tokens(devices)
    line = devices // ROWS
    group = lax.axis_index("proto")
    y = lax.axis_index("y")
    device = y * line + lax.axis_index("z")
    place = jnp.stack([group, device, y]).astype(jnp.int32)

    half = PROTO // 2
    swap = [(p, p ^ 1) for p in range(PROTO)]
    routes = [[(p, (p + 2 * away) % PROTO) for p in range(PROTO)] for away in range(half)]
    pay, own = pl.pallas_call(
        pick_kernel,
        out_shape=[
            jax.ShapeDtypeStruct((line, 2 * SLOTS, width), BF16),
            jax.ShapeDtypeStruct((share, width), BF16),
        ],
        in_specs=[
            pl.BlockSpec(memory_space=pltpu.SMEM),
            pl.BlockSpec(memory_space=pltpu.SMEM),
            pl.BlockSpec(memory_space=pltpu.VMEM),
            pl.BlockSpec(memory_space=pl.ANY),
            pl.BlockSpec(memory_space=pl.ANY),
            pl.BlockSpec(memory_space=pl.ANY),
        ],
        out_specs=[pl.BlockSpec(memory_space=pltpu.VMEM)] * 2,
        scratch_shapes=[pltpu.VMEM((2, patches, width), BF16), pltpu.SemaphoreType.DMA((3,))],
        compiler_params=pltpu.CompilerParams(vmem_limit_bytes=60 * 1024 * 1024),
    )(place, counts, mask_index, teacher_patches, student_patches, prototypes)
    pay = exchange(pay, "z")
    lines = []
    for half_pay in (pay[:, :SLOTS], pay[:, SLOTS:]):
        lines.append([half_pay])
        for away in range(1, ROWS):
            route = [(i, (i - away) % ROWS) for i in range(ROWS)]
            lines[-1].append(lax.ppermute(half_pay, "y", route))
    teach_lines, stud_lines = lines
    near = [lax.ppermute(own, "proto", routes[-away % half]) for away in range(1, half)]
    near = jnp.stack([own] + near)
    far = lax.ppermute(near, "proto", swap)
    (protos,) = call(
        prototypes_kernel, [((protos_held, width), BF16)], (place, near, far), scalars=1
    )
    (onehot,) = call(
        patch_kernel, [((patches, CAP), BF16)], (place, counts, mask_index), scalars=2
    )

    packed = ((8, LANES), F32)
    col_out = ((PROTO, chunks, LANES), F32)
    row_out = ((devices, 8, LANES), F32)
    pay_scratch = pltpu.VMEM((devices, SLOTS, width), BF16)
    pairs = tokens * protos_held
    work = pl.CostEstimate(
        flops=2 * pairs * width, bytes_accessed=8 * pairs, transcendentals=pairs
    )
    teach, slots, valid, col = call(
        first_kernel,
        [((tokens, width), BF16), ((8, devices * SLOTS), F32), packed, col_out],
        (place, *teach_lines, protos),
        scalars=1,
        scratch=(pay_scratch,),
        cost=work,
    )
    col = exchange(col, "proto")
    stud, stud_row = call(
        student_kernel,
        [((tokens, width), BF16), packed],
        (place, *stud_lines, slots, protos),
        scalars=1,
        scratch=(pay_scratch, pltpu.VMEM((tokens, protos_held), F32)),
        cost=work,
    )
    exps, top, row, stud_row = call(
        second_kernel,
        [((tokens, protos_held), F32), packed, row_out, packed],
        (teach, protos, col, stud_row),
        cost=work,
    )
    row = exchange(row, TOK)
    factor, col = call(third_kernel, [packed, col_out], (exps, top, valid, row))
    col = exchange(col, "proto")
    (row,) = call(row_kernel, [row_out], (exps, factor, col))
    row = exchange(row, TOK)
    (col,) = call(column_kernel, [col_out], (exps, factor, valid, row))
    col = exchange(col, "proto")
    (row,) = call(
        last_row_kernel, [((devices, 16, LANES), F32)], (exps, factor, col, stud_row)
    )
    row = exchange(row, TOK)
    grad_slots, grads = call(
        gradient_kernel,
        [((devices, SLOTS, width), BF16), ((tokens, protos_held), BF16)],
        (exps, factor, valid, col, row, stud, protos, slots),
        scratch=(pltpu.VMEM((tokens, LANES), F32), pltpu.VMEM((tokens, LANES), F32)),
        cost=work,
    )
    near, far = call(
        proto_kernel,
        [((half, share, width), F32), ((half, share, width), F32)],
        (place, grads, stud),
        scalars=1,
        cost=work,
    )
    mine = near + lax.ppermute(far, "proto", swap)
    arrived = [lax.ppermute(mine[away], "proto", routes[away]) for away in range(1, half)]
    rows, grad_prototypes = call(
        sum_kernel,
        [((PROTO, SLOTS, width), F32), ((share, width), F32)],
        (exchange(grad_slots, TOK), mine, *arrived),
    )
    rows = exchange(rows, "proto")
    (grad_patches,) = call(spread_kernel, [((patches, width), F32)], (onehot, rows))
    return (grad_patches, grad_prototypes)


def solution(mesh):
    devices, protos = mesh.devices.shape
    shape = (ROWS, devices // ROWS, protos)
    mesh = Mesh(mesh.devices.reshape(shape), (*TOK, "proto"))
    return jax.shard_map(
        functools.partial(on_device, devices),
        mesh=mesh,
        in_specs=(
            P(TOK, None),
            P(TOK, None),
            P(("proto", *TOK), None),
            P(TOK, None),
            P(TOK),
        ),
        out_specs=(P(TOK, None), P(("proto", *TOK), None)),
        check_vma=False,
    )
```

```python
import functools
import math

import jax
import jax.numpy as jnp
from jax import lax
from jax.experimental import pallas as pl
from jax.experimental.pallas import tpu as pltpu
from jax.sharding import Mesh, PartitionSpec as P

CAP = 256
BAL = 128
PROTO = 8
SLOTS = CAP // PROTO
ROWS = 4
TOK = ("y", "z")
LANES = 128
TEACHER_SCALE = 1.0 / 0.07
STUDENT_SCALE = 1.0 / 0.1
FAR_BELOW = -1e30
VMEM = 24 * 1024 * 1024
F32 = jnp.float32
BF16 = jnp.bfloat16
HIGH = lax.Precision.HIGHEST


def iota(shape, dim):
    return lax.broadcasted_iota(jnp.int32, shape, dim)


def dot_nt(a, b, precision=None):
    return lax.dot_general(
        a, b, (((1,), (1,)), ((), ())), precision=precision, preferred_element_type=F32
    )


def dot_tn(a, b, precision=None):
    return lax.dot_general(
        a, b, (((0,), (0,)), ((), ())), precision=precision, preferred_element_type=F32
    )


def dot_nn(a, b, precision=None):
    return jnp.dot(a, b, precision=precision, preferred_element_type=F32)


def blocks(tokens):
    return [(at // LANES, slice(at, min(at + LANES, tokens))) for at in range(0, tokens, LANES)]


def turned(rows, block, first_lane_only):
    at = iota((8, LANES), 0) == block
    if first_lane_only:
        at = at & (iota((8, LANES), 1) == 0)
    short = LANES - rows.shape[0]
    if short:
        rows = jnp.concatenate([rows, jnp.zeros((short, LANES), F32)], axis=0)
    return dot_nt(at.astype(F32), rows, HIGH)


def column(packed, block, size):
    at = (iota((8, LANES), 0) == block).astype(F32)
    return dot_tn(packed, at, HIGH)[:size]


def lse_over_first(values):
    top = jnp.max(values, axis=0)
    return top + jnp.log(jnp.sum(jnp.exp(values - top[None]), axis=0))


def row_offset(group, device):
    return lax.rem(group + device, PROTO)


def pick_kernel(
    count_ref, mask_ref, teacher_ref, student_ref, protos_ref,
    pay_ref, own_ref, patch_ref, sem_ref,
):
    sources = (teacher_ref, student_ref, protos_ref)
    targets = (patch_ref.at[0], patch_ref.at[1], own_ref)
    copies = [
        pltpu.make_async_copy(source, target, sem_ref.at[which])
        for which, (source, target) in enumerate(zip(sources, targets))
    ]
    for copy in copies:
        copy.start()
    patches, width = teacher_ref.shape
    device = lax.axis_index("y") * pay_ref.shape[0] + lax.axis_index("z")
    offset = row_offset(lax.axis_index("proto"), device)
    at = (iota((SLOTS, patches), 1) == iota((SLOTS, patches), 0) * PROTO + offset).astype(BF16)
    mask = jnp.broadcast_to(mask_ref[...], (LANES, patches))
    high = dot_nt(at, (mask // 256).astype(F32).astype(BF16))
    low = dot_nt(at, (mask % 256).astype(F32).astype(BF16))
    chosen = (high * 256.0 + low + 0.5).astype(jnp.int32)
    lane = iota((SLOTS, LANES), 1)
    onehot = jnp.concatenate(
        [(lane + start == chosen).astype(F32).astype(BF16) for start in range(0, patches, LANES)],
        axis=1,
    )
    held = iota((SLOTS, width), 0) * PROTO + offset < count_ref[0]
    copies[0].wait()
    teach = jnp.where(held, dot_nn(onehot, patch_ref[0]), jnp.inf).astype(BF16)
    copies[1].wait()
    stud = dot_nn(onehot, patch_ref[1]).astype(BF16)
    both = jnp.concatenate([teach, stud], axis=0)
    pay_ref[...] = jnp.broadcast_to(both[None], pay_ref.shape)
    copies[2].wait()


def place_onehot(place, tokens):
    return (iota((tokens, place.shape[1]), 0).astype(F32) == place).astype(BF16)


def stack_kernel(own_ref, *refs):
    out_ref = refs[-1]
    out_ref[0, :, :] = own_ref[...]
    for away in range(1, PROTO // 2):
        out_ref[away, :, :] = refs[away - 1][...]


def prototypes_kernel(place_ref, near_ref, far_ref, protos_ref):
    share = near_ref.shape[1]
    group = place_ref[0]
    for away in range(PROTO // 2):
        x = lax.rem(group // 2 + away, PROTO // 2)
        core = lax.rem(group, 2)
        start = pl.multiple_of((2 * x + core) * share, share)
        protos_ref[pl.ds(start, share), :] = near_ref[away]
        start = pl.multiple_of((2 * x + 1 - core) * share, share)
        protos_ref[pl.ds(start, share), :] = far_ref[away]


def in_order(y, line_refs, pay_ref, first_slot):
    line = line_refs[0].shape[0]
    for away in range(ROWS):
        start = lax.rem(y + away, ROWS) * line
        pay_ref[pl.ds(start, line), :, :] = line_refs[away][:, first_slot : first_slot + SLOTS, :]
    devices, slots, width = pay_ref.shape
    return pay_ref[...].reshape(devices * slots, width)


def first_kernel(*refs):
    place_ref, *line_refs = refs[: ROWS + 1]
    protos_ref, teach_ref, place_out_ref, valid_ref, base_ref, col_ref, pay_ref = refs[ROWS + 1 :]
    arrived = in_order(place_ref[2], line_refs, pay_ref, 0).astype(F32)
    tokens = teach_ref.shape[0]
    slots, width = arrived.shape
    real = arrived < jnp.inf
    pick = (iota((8, width), 1) == 0).astype(BF16)
    flags = dot_nt(pick, real.astype(F32).astype(BF16))
    held = dot_nn(
        flags.astype(BF16), (iota((slots, LANES), 0) // SLOTS == iota((slots, LANES), 1)).astype(BF16)
    )
    before = dot_nn(
        held.astype(BF16), (iota((LANES, slots), 0) < iota((LANES, slots), 1) // SLOTS).astype(BF16)
    )[:1]
    bases = dot_nn(
        held.astype(BF16), (iota((LANES, LANES), 0) < iota((LANES, LANES), 1)).astype(BF16)
    )
    base_ref[...] = (bases + 0.5).astype(jnp.int32)
    inner = (iota((1, slots), 1) % SLOTS).astype(F32)
    place = jnp.where(flags[:1] > 0.5, before + inner, -1.0)
    place_out_ref[...] = jnp.broadcast_to(place, place_out_ref.shape)
    total = jnp.max(place, axis=1, keepdims=True) + 1.0
    order = iota((8, LANES), 0) * LANES + iota((8, LANES), 1)
    valid_ref[...] = (order.astype(F32) < total).astype(F32)
    onehot = place_onehot(place, tokens)
    teach = dot_nn(onehot, jnp.where(real, arrived, 0.0).astype(BF16)).astype(BF16)
    teach_ref[...] = teach
    step = 2 * LANES
    alive = iota((tokens, step), 0).astype(F32) < total
    rows = []
    for start in range(0, protos_ref.shape[0], step):
        scores = dot_nt(teach, protos_ref[start : start + step, :]) * TEACHER_SCALE
        scores = jnp.where(alive, scores, FAR_BELOW)
        top = jnp.max(scores, axis=0, keepdims=True)
        lse = top + jnp.log(jnp.sum(jnp.exp(scores - top), axis=0, keepdims=True))
        rows += [lse[:, :LANES], lse[:, LANES:]]
    col_ref[...] = jnp.broadcast_to(jnp.concatenate(rows, axis=0)[None], col_ref.shape)


def wide(packed):
    return jnp.concatenate([packed[i : i + 1, :] for i in range(packed.shape[0])], axis=1)


def exps_below_top(left_ref, protos_ref, scale, shift, out_ref):
    step = 2 * LANES
    for start in range(0, protos_ref.shape[0], step):
        scores = dot_nt(left_ref[...], protos_ref[start : start + step, :]) * scale
        if shift is not None:
            scores = scores + shift[:, start : start + step]
        out_ref[:, start : start + step] = scores
    tops = jnp.zeros((8, LANES), F32)
    totals = jnp.zeros((8, LANES), F32)
    starts = range(0, protos_ref.shape[0], LANES)
    for block, rows in blocks(left_ref.shape[0]):
        top = out_ref[rows, :LANES]
        for start in starts[1:]:
            top = jnp.maximum(top, out_ref[rows, start : start + LANES])
        top = jnp.broadcast_to(jnp.max(top, axis=1, keepdims=True), top.shape)
        sums = jnp.zeros_like(top)
        for start in starts:
            exps = jnp.exp(out_ref[rows, start : start + LANES] - top)
            out_ref[rows, start : start + LANES] = exps
            sums += exps
        tops += turned(top, block, True)
        totals += turned(sums, block, False)
    return tops, totals


def second_kernel(teach_ref, protos_ref, col_ref, stud_row_ref, exp_ref, top_ref, row_ref, stud_out_ref):
    col_pot = -wide(lse_over_first(col_ref[...]))
    tops, totals = exps_below_top(teach_ref, protos_ref, TEACHER_SCALE, col_pot, exp_ref)
    top_ref[...] = tops
    lses = tops + jnp.log(jnp.where(totals > 0.0, totals, 1.0))
    row_ref[...] = jnp.broadcast_to(lses[None], row_ref.shape)
    stud_out_ref[...] = stud_row_ref[...]


def weighted_columns(exp_ref, weight):
    chunks = exp_ref.shape[1] // LANES
    sums = [jnp.zeros((8, LANES), F32) for _ in range(chunks)]
    for block, rows in blocks(exp_ref.shape[0]):
        size = rows.stop - rows.start
        factor = column(weight, block, size)
        for chunk in range(chunks):
            part = exp_ref[rows, chunk * LANES : (chunk + 1) * LANES] * factor
            sums[chunk] += jnp.sum(part.reshape(size // 8, 8, LANES), axis=0)
    return jnp.concatenate([jnp.sum(part, axis=0, keepdims=True) for part in sums], axis=0)


def third_kernel(exp_ref, top_ref, valid_ref, row_ref, factor_ref, col_ref):
    row_pot = -lse_over_first(row_ref[...])
    factor = jnp.where(valid_ref[...] > 0.0, jnp.exp(top_ref[...] + row_pot), 0.0)
    factor_ref[...] = factor
    col_ref[...] = jnp.broadcast_to(weighted_columns(exp_ref, factor)[None], col_ref.shape)


def row_scale(valid_ref, sums):
    alive = valid_ref[...] > 0.0
    return jnp.where(alive, 1.0 / jnp.where(alive, sums, 1.0), 0.0)


def column_kernel(exp_ref, factor_ref, valid_ref, row_ref, col_ref):
    weight = row_scale(valid_ref, jnp.sum(row_ref[...], axis=0)) * factor_ref[...]
    col_ref[...] = jnp.broadcast_to(weighted_columns(exp_ref, weight)[None], col_ref.shape)


def weighted_rows(exp_ref, weight):
    sums = jnp.zeros((8, LANES), F32)
    for block, rows in blocks(exp_ref.shape[0]):
        part = jnp.zeros((rows.stop - rows.start, LANES), F32)
        for chunk in range(weight.shape[0]):
            values = exp_ref[rows, chunk * LANES : (chunk + 1) * LANES]
            part += values * weight[chunk : chunk + 1, :]
        sums += turned(part, block, False)
    return sums


def row_kernel(exp_ref, factor_ref, col_ref, row_ref):
    weight = 1.0 / jnp.sum(col_ref[...], axis=0)
    sums = weighted_rows(exp_ref, weight) * factor_ref[...]
    row_ref[...] = jnp.broadcast_to(sums[None], row_ref.shape)


def student_kernel(*refs):
    place_ref, *line_refs = refs[: ROWS + 1]
    slot_ref, protos_ref, stud_ref, row_ref, pay_ref, exp_ref = refs[ROWS + 1 :]
    arrived = in_order(place_ref[2], line_refs, pay_ref, SLOTS)
    onehot = place_onehot(slot_ref[:1, :], stud_ref.shape[0])
    stud_ref[...] = dot_nn(onehot, arrived).astype(BF16)
    tops, totals = exps_below_top(stud_ref, protos_ref, STUDENT_SCALE, None, exp_ref)
    row_ref[...] = tops + jnp.log(jnp.where(totals > 0.0, totals, 1.0))


def last_row_kernel(exp_ref, factor_ref, col_ref, stud_row_ref, row_ref):
    weight = 1.0 / jnp.sum(col_ref[...], axis=0)
    sums = weighted_rows(exp_ref, weight) * factor_ref[...]
    both = jnp.concatenate([sums, stud_row_ref[...]], axis=0)
    row_ref[...] = jnp.broadcast_to(both[None], row_ref.shape)


def gradient_kernel(
    base_ref, exp_ref, factor_ref, valid_ref, col_ref, row_ref, stud_ref, protos_ref,
    tok_ref, grad_ref, scale_ref, lse_ref, total_ref,
):
    tokens, width = stud_ref.shape
    weights = 1.0 / jnp.sum(col_ref[...], axis=0)
    sums = jnp.sum(row_ref[:, :8, :], axis=0)
    scale = row_scale(valid_ref, sums) * (factor_ref[...] * STUDENT_SCALE)
    lses = lse_over_first(row_ref[:, 8:, :]) - math.log(STUDENT_SCALE)
    lses = jnp.where(valid_ref[...] > 0.0, lses, -FAR_BELOW)
    for block, rows in blocks(tokens):
        size = rows.stop - rows.start
        scale_ref[rows, :] = column(scale, block, size)
        lse_ref[rows, :] = column(lses, block, size)
    step = 2 * LANES
    for chunk in range(protos_ref.shape[0] // step):
        scores = dot_nt(stud_ref[...], protos_ref[chunk * step : (chunk + 1) * step, :])
        for half in range(2):
            index = 2 * chunk + half
            lanes = slice(index * LANES, (index + 1) * LANES)
            part = scores[:, half * LANES : (half + 1) * LANES] * STUDENT_SCALE
            student = jnp.exp(part - lse_ref[...])
            target = exp_ref[:, lanes] * scale_ref[...] * weights[index : index + 1, :]
            grad_ref[:, lanes] = (student - target).astype(BF16)
    total_ref[:tokens, :] = dot_nn(grad_ref[...], protos_ref[...])
    total_ref[tokens:, :] = jnp.zeros((SLOTS, width), F32)
    for device in range(tok_ref.shape[0]):
        base = base_ref[0, device]
        start = pl.multiple_of(base // 8 * 8, 8)
        rows = pltpu.roll(total_ref[pl.ds(start, SLOTS + 8), :], SLOTS + 8 - base % 8, 0)
        tok_ref[device, :, :] = rows[:SLOTS, :].astype(BF16)


def proto_kernel(place_ref, grad_ref, stud_ref, near_ref, far_ref):
    share = near_ref.shape[1]
    group = place_ref[0]
    for away in range(PROTO // 2):
        x = lax.rem(group // 2 + away, PROTO // 2)
        core = lax.rem(group, 2)
        start = pl.multiple_of((2 * x + 1 - core) * share, share)
        far_ref[away, :, :] = dot_tn(grad_ref[:, pl.ds(start, share)], stud_ref[...])
        start = pl.multiple_of((2 * x + core) * share, share)
        near_ref[away, :, :] = dot_tn(grad_ref[:, pl.ds(start, share)], stud_ref[...])


def sum_kernel(parts_ref, near_ref, *refs):
    *far_refs, out_ref, proto_ref = refs
    total = jnp.sum(parts_ref[...].astype(F32), axis=0)
    out_ref[...] = jnp.broadcast_to(total[None], out_ref.shape)
    total = near_ref[0]
    for far_ref in far_refs:
        total = total + far_ref[...]
    proto_ref[...] = total


def patch_kernel(place_ref, count_ref, mask_ref, onehot_ref):
    patches = onehot_ref.shape[0]
    device = place_ref[1]
    wanted = iota((patches, CAP), 1)
    rank = (wanted % SLOTS) * PROTO + row_offset(wanted // SLOTS, device)
    at = (iota((patches, CAP), 0) == rank).astype(F32)
    mask = jnp.broadcast_to(mask_ref[...].astype(F32), (8, patches))
    chosen = (dot_nn(mask, at, HIGH)[:1] + 0.5).astype(jnp.int32)
    chosen = jnp.where(rank[:1, :] < count_ref[0], chosen, -1)
    onehot_ref[...] = (iota((patches, CAP), 0) == chosen).astype(BF16)


def spread_kernel(onehot_ref, rows_ref, out_ref):
    rest = rows_ref[...].reshape(CAP, out_ref.shape[1])
    total = None
    for _ in range(3):
        part = rest.astype(BF16)
        rest = rest - part.astype(F32)
        moved = dot_nn(onehot_ref[...], part)
        total = moved if total is None else total + moved
    out_ref[...] = total


def call(kernel, outs, inputs, scalars=0, scratch=(), cost=None):
    smem = [pl.BlockSpec(memory_space=pltpu.SMEM)] * scalars
    arrays = [pl.BlockSpec(memory_space=pltpu.VMEM)] * (len(inputs) - scalars)
    return pl.pallas_call(
        kernel,
        out_shape=[jax.ShapeDtypeStruct(shape, dtype) for shape, dtype in outs],
        in_specs=smem + arrays,
        out_specs=[pl.BlockSpec(memory_space=pltpu.VMEM)] * len(outs),
        scratch_shapes=list(scratch),
        compiler_params=pltpu.CompilerParams(vmem_limit_bytes=VMEM),
        cost_estimate=cost,
    )(*inputs)


def most_tokens(devices):
    slack = sum((PROTO - 1 - device % PROTO) for device in range(devices))
    return -(-((BAL * devices + slack) // PROTO) // 16) * 16


def exchange(parts, axis):
    return lax.all_to_all(parts, axis, 0, 0, tiled=True)


def on_device(devices, teacher_patches, student_patches, prototypes, mask_index, counts):
    patches, width = teacher_patches.shape
    share = prototypes.shape[0]
    protos_held = PROTO * share
    chunks = protos_held // LANES
    tokens = most_tokens(devices)
    line = devices // ROWS
    group = lax.axis_index("proto")
    y = lax.axis_index("y")
    device = y * line + lax.axis_index("z")
    place = jnp.stack([group, device, y]).astype(jnp.int32)

    half = PROTO // 2
    swap = [(p, p ^ 1) for p in range(PROTO)]
    routes = [[(p, (p + 2 * away) % PROTO) for p in range(PROTO)] for away in range(half)]
    pay, own = pl.pallas_call(
        pick_kernel,
        out_shape=[
            jax.ShapeDtypeStruct((line, 2 * SLOTS, width), BF16),
            jax.ShapeDtypeStruct((share, width), BF16),
        ],
        in_specs=[
            pl.BlockSpec(memory_space=pltpu.SMEM),
            pl.BlockSpec(memory_space=pltpu.VMEM),
            pl.BlockSpec(memory_space=pl.ANY),
            pl.BlockSpec(memory_space=pl.ANY),
            pl.BlockSpec(memory_space=pl.ANY),
        ],
        out_specs=[pl.BlockSpec(memory_space=pltpu.VMEM)] * 2,
        scratch_shapes=[pltpu.VMEM((2, patches, width), BF16), pltpu.SemaphoreType.DMA((3,))],
        compiler_params=pltpu.CompilerParams(vmem_limit_bytes=60 * 1024 * 1024),
    )(counts, mask_index, teacher_patches, student_patches, prototypes)
    pay = exchange(pay, "z")
    lines = [pay]
    for away in range(1, ROWS):
        route = [(i, (i - away) % ROWS) for i in range(ROWS)]
        lines.append(lax.ppermute(pay, "y", route))
    near = [lax.ppermute(own, "proto", routes[-away % half]) for away in range(1, half)]
    (near,) = pl.pallas_call(
        stack_kernel,
        out_shape=[jax.ShapeDtypeStruct((half, share, width), BF16)],
        in_specs=[pl.BlockSpec(memory_space=pltpu.VMEM)] * half
        + [pl.BlockSpec(memory_space=pl.ANY)],
        out_specs=[pl.BlockSpec(memory_space=pltpu.VMEM)],
        compiler_params=pltpu.CompilerParams(vmem_limit_bytes=VMEM),
    )(own, *near, pay)
    far = lax.ppermute(near, "proto", swap)
    (protos,) = call(
        prototypes_kernel, [((protos_held, width), BF16)], (place, near, far), scalars=1
    )
    (onehot,) = call(
        patch_kernel, [((patches, CAP), BF16)], (place, counts, mask_index), scalars=2
    )

    packed = ((8, LANES), F32)
    col_out = ((PROTO, chunks, LANES), F32)
    row_out = ((devices, 8, LANES), F32)
    pay_scratch = pltpu.VMEM((devices, SLOTS, width), BF16)
    pairs = tokens * protos_held
    work = pl.CostEstimate(
        flops=2 * pairs * width, bytes_accessed=8 * pairs, transcendentals=pairs
    )
    teach, slots, valid, base, col = call(
        first_kernel,
        [
            ((tokens, width), BF16),
            ((8, devices * SLOTS), F32),
            packed,
            ((8, LANES), jnp.int32),
            col_out,
        ],
        (place, *lines, protos),
        scalars=1,
        scratch=(pay_scratch,),
        cost=work,
    )
    col = exchange(col, "proto")
    stud, stud_row = call(
        student_kernel,
        [((tokens, width), BF16), packed],
        (place, *lines, slots, protos),
        scalars=1,
        scratch=(pay_scratch, pltpu.VMEM((tokens, protos_held), F32)),
        cost=work,
    )
    exps, top, row, stud_row = call(
        second_kernel,
        [((tokens, protos_held), F32), packed, row_out, packed],
        (teach, protos, col, stud_row),
        cost=work,
    )
    row = exchange(row, TOK)
    factor, col = call(third_kernel, [packed, col_out], (exps, top, valid, row))
    col = exchange(col, "proto")
    (row,) = call(row_kernel, [row_out], (exps, factor, col))
    row = exchange(row, TOK)
    (col,) = call(column_kernel, [col_out], (exps, factor, valid, row))
    col = exchange(col, "proto")
    (row,) = call(
        last_row_kernel, [((devices, 16, LANES), F32)], (exps, factor, col, stud_row)
    )
    row = exchange(row, TOK)
    grad_slots, grads = call(
        gradient_kernel,
        [((devices, SLOTS, width), BF16), ((tokens, protos_held), BF16)],
        (base, exps, factor, valid, col, row, stud, protos),
        scalars=1,
        scratch=(
            pltpu.VMEM((tokens, LANES), F32),
            pltpu.VMEM((tokens, LANES), F32),
            pltpu.VMEM((tokens + SLOTS, width), F32),
        ),
        cost=work,
    )
    near, far = call(
        proto_kernel,
        [((half, share, width), F32), ((half, share, width), F32)],
        (place, grads, stud),
        scalars=1,
        cost=work,
    )
    mine = near + lax.ppermute(far, "proto", swap)
    arrived = [lax.ppermute(mine[away], "proto", routes[away]) for away in range(1, half)]
    rows, grad_prototypes = call(
        sum_kernel,
        [((PROTO, SLOTS, width), F32), ((share, width), F32)],
        (exchange(grad_slots, TOK), mine, *arrived),
    )
    rows = exchange(rows, "proto")
    (grad_patches,) = call(spread_kernel, [((patches, width), F32)], (onehot, rows))
    return (grad_patches, grad_prototypes)


def solution(mesh):
    devices, protos = mesh.devices.shape
    shape = (ROWS, devices // ROWS, protos)
    mesh = Mesh(mesh.devices.reshape(shape), (*TOK, "proto"))
    return jax.shard_map(
        functools.partial(on_device, devices),
        mesh=mesh,
        in_specs=(
            P(TOK, None),
            P(TOK, None),
            P(("proto", *TOK), None),
            P(TOK, None),
            P(TOK),
        ),
        out_specs=(P(TOK, None), P(("proto", *TOK), None)),
        check_vma=False,
    )
```

```python
import functools
import math

import jax
import jax.numpy as jnp
from jax import lax
from jax.experimental import pallas as pl
from jax.experimental.pallas import tpu as pltpu
from jax.sharding import Mesh, PartitionSpec as P

CAP = 256
BAL = 128
PROTO = 8
SLOTS = CAP // PROTO
ROWS = 4
TOK = ("y", "z")
LANES = 128
TEACHER_SCALE = 1.0 / 0.07
STUDENT_SCALE = 1.0 / 0.1
FAR_BELOW = -1e30
VMEM = 24 * 1024 * 1024
F32 = jnp.float32
BF16 = jnp.bfloat16
HIGH = lax.Precision.HIGHEST


def iota(shape, dim):
    return lax.broadcasted_iota(jnp.int32, shape, dim)


def dot_nt(a, b, precision=None):
    return lax.dot_general(
        a, b, (((1,), (1,)), ((), ())), precision=precision, preferred_element_type=F32
    )


def dot_tn(a, b, precision=None):
    return lax.dot_general(
        a, b, (((0,), (0,)), ((), ())), precision=precision, preferred_element_type=F32
    )


def dot_nn(a, b, precision=None):
    return jnp.dot(a, b, precision=precision, preferred_element_type=F32)


def blocks(tokens):
    return [(at // LANES, slice(at, min(at + LANES, tokens))) for at in range(0, tokens, LANES)]


def turned(rows, block, first_lane_only):
    at = iota((8, LANES), 0) == block
    if first_lane_only:
        at = at & (iota((8, LANES), 1) == 0)
    short = LANES - rows.shape[0]
    if short:
        rows = jnp.concatenate([rows, jnp.zeros((short, LANES), F32)], axis=0)
    return dot_nt(at.astype(F32), rows, HIGH)


def column(packed, block, size):
    at = (iota((8, LANES), 0) == block).astype(F32)
    return dot_tn(packed, at, HIGH)[:size]


def lse_over_first(values):
    top = jnp.max(values, axis=0)
    return top + jnp.log(jnp.sum(jnp.exp(values - top[None]), axis=0))


def row_offset(group, device):
    return lax.rem(group + device, PROTO)


def pick_kernel(
    count_ref, mask_ref, teacher_ref, student_ref, pay_ref, patch_ref, sem_ref,
):
    copies = [
        pltpu.make_async_copy(source, patch_ref.at[which], sem_ref.at[which])
        for which, source in enumerate((teacher_ref, student_ref))
    ]
    for copy in copies:
        copy.start()
    patches, width = teacher_ref.shape
    device = lax.axis_index("y") * pay_ref.shape[0] + lax.axis_index("z")
    offset = row_offset(lax.axis_index("proto"), device)
    at = (iota((SLOTS, patches), 1) == iota((SLOTS, patches), 0) * PROTO + offset).astype(BF16)
    mask = jnp.broadcast_to(mask_ref[...], (LANES, patches))
    high = dot_nt(at, (mask // 256).astype(F32).astype(BF16))
    low = dot_nt(at, (mask % 256).astype(F32).astype(BF16))
    chosen = (high * 256.0 + low + 0.5).astype(jnp.int32)
    lane = iota((SLOTS, LANES), 1)
    onehot = jnp.concatenate(
        [(lane + start == chosen).astype(F32).astype(BF16) for start in range(0, patches, LANES)],
        axis=1,
    )
    held = iota((SLOTS, width), 0) * PROTO + offset < count_ref[0]
    copies[0].wait()
    teach = jnp.where(held, dot_nn(onehot, patch_ref[0]), jnp.inf).astype(BF16)
    copies[1].wait()
    stud = dot_nn(onehot, patch_ref[1]).astype(BF16)
    both = jnp.concatenate([teach, stud], axis=0)
    pay_ref[...] = jnp.broadcast_to(both[None], pay_ref.shape)


def place_onehot(place, tokens):
    return (iota((tokens, place.shape[1]), 0).astype(F32) == place).astype(BF16)


def prototypes_kernel(place_ref, *refs):
    *pair_refs, protos_ref = refs
    share = pair_refs[0].shape[1]
    group = place_ref[0]
    core = lax.rem(group, 2)
    for away, pair_ref in enumerate(pair_refs):
        x = lax.rem(group // 2 + away, PROTO // 2)
        for other in range(2):
            start = pl.multiple_of((2 * x + (core + other) % 2) * share, share)
            protos_ref[pl.ds(start, share), :] = pair_ref[other]


def in_order(y, line_refs, pay_ref, first_slot):
    line = line_refs[0].shape[0]
    for away in range(ROWS):
        start = lax.rem(y + away, ROWS) * line
        pay_ref[pl.ds(start, line), :, :] = line_refs[away][:, first_slot : first_slot + SLOTS, :]
    devices, slots, width = pay_ref.shape
    return pay_ref[...].reshape(devices * slots, width)


def first_kernel(*refs):
    place_ref, *line_refs = refs[: ROWS + 1]
    protos_ref, teach_ref, place_out_ref, valid_ref, base_ref, col_ref, pay_ref = refs[ROWS + 1 :]
    arrived = in_order(place_ref[2], line_refs, pay_ref, 0).astype(F32)
    tokens = teach_ref.shape[0]
    slots, width = arrived.shape
    real = arrived < jnp.inf
    pick = (iota((8, width), 1) == 0).astype(BF16)
    flags = dot_nt(pick, real.astype(F32).astype(BF16))
    held = dot_nn(
        flags.astype(BF16), (iota((slots, LANES), 0) // SLOTS == iota((slots, LANES), 1)).astype(BF16)
    )
    before = dot_nn(
        held.astype(BF16), (iota((LANES, slots), 0) < iota((LANES, slots), 1) // SLOTS).astype(BF16)
    )[:1]
    bases = dot_nn(
        held.astype(BF16), (iota((LANES, LANES), 0) < iota((LANES, LANES), 1)).astype(BF16)
    )
    base_ref[...] = (bases + 0.5).astype(jnp.int32)
    inner = (iota((1, slots), 1) % SLOTS).astype(F32)
    place = jnp.where(flags[:1] > 0.5, before + inner, -1.0)
    place_out_ref[...] = jnp.broadcast_to(place, place_out_ref.shape)
    total = jnp.max(place, axis=1, keepdims=True) + 1.0
    order = iota((8, LANES), 0) * LANES + iota((8, LANES), 1)
    valid_ref[...] = (order.astype(F32) < total).astype(F32)
    onehot = place_onehot(place, tokens)
    teach = dot_nn(onehot, jnp.where(real, arrived, 0.0).astype(BF16)).astype(BF16)
    teach_ref[...] = teach
    step = 2 * LANES
    alive = iota((tokens, step), 0).astype(F32) < total
    rows = []
    for start in range(0, protos_ref.shape[0], step):
        scores = dot_nt(teach, protos_ref[start : start + step, :]) * TEACHER_SCALE
        scores = jnp.where(alive, scores, FAR_BELOW)
        top = jnp.max(scores, axis=0, keepdims=True)
        lse = top + jnp.log(jnp.sum(jnp.exp(scores - top), axis=0, keepdims=True))
        rows += [lse[:, :LANES], lse[:, LANES:]]
    col_ref[...] = jnp.broadcast_to(jnp.concatenate(rows, axis=0)[None], col_ref.shape)


def wide(packed):
    return jnp.concatenate([packed[i : i + 1, :] for i in range(packed.shape[0])], axis=1)


def exps_below_top(left_ref, protos_ref, scale, shift, out_ref):
    step = 2 * LANES
    for start in range(0, protos_ref.shape[0], step):
        scores = dot_nt(left_ref[...], protos_ref[start : start + step, :]) * scale
        if shift is not None:
            scores = scores + shift[:, start : start + step]
        out_ref[:, start : start + step] = scores
    tops = jnp.zeros((8, LANES), F32)
    totals = jnp.zeros((8, LANES), F32)
    starts = range(0, protos_ref.shape[0], LANES)
    for block, rows in blocks(left_ref.shape[0]):
        top = out_ref[rows, :LANES]
        for start in starts[1:]:
            top = jnp.maximum(top, out_ref[rows, start : start + LANES])
        top = jnp.broadcast_to(jnp.max(top, axis=1, keepdims=True), top.shape)
        sums = jnp.zeros_like(top)
        for start in starts:
            exps = jnp.exp(out_ref[rows, start : start + LANES] - top)
            out_ref[rows, start : start + LANES] = exps
            sums += exps
        tops += turned(top, block, True)
        totals += turned(sums, block, False)
    return tops, totals


def second_kernel(teach_ref, protos_ref, col_ref, stud_row_ref, exp_ref, top_ref, row_ref, stud_out_ref):
    col_pot = -wide(lse_over_first(col_ref[...]))
    tops, totals = exps_below_top(teach_ref, protos_ref, TEACHER_SCALE, col_pot, exp_ref)
    top_ref[...] = tops
    lses = tops + jnp.log(jnp.where(totals > 0.0, totals, 1.0))
    row_ref[...] = jnp.broadcast_to(lses[None], row_ref.shape)
    stud_out_ref[...] = stud_row_ref[...]


def weighted_columns(exp_ref, weight):
    chunks = exp_ref.shape[1] // LANES
    sums = [jnp.zeros((8, LANES), F32) for _ in range(chunks)]
    for block, rows in blocks(exp_ref.shape[0]):
        size = rows.stop - rows.start
        factor = column(weight, block, size)
        for chunk in range(chunks):
            part = exp_ref[rows, chunk * LANES : (chunk + 1) * LANES] * factor
            sums[chunk] += jnp.sum(part.reshape(size // 8, 8, LANES), axis=0)
    return jnp.concatenate([jnp.sum(part, axis=0, keepdims=True) for part in sums], axis=0)


def third_kernel(exp_ref, top_ref, valid_ref, row_ref, factor_ref, col_ref):
    row_pot = -lse_over_first(row_ref[...])
    factor = jnp.where(valid_ref[...] > 0.0, jnp.exp(top_ref[...] + row_pot), 0.0)
    factor_ref[...] = factor
    col_ref[...] = jnp.broadcast_to(weighted_columns(exp_ref, factor)[None], col_ref.shape)


def row_scale(valid_ref, sums):
    alive = valid_ref[...] > 0.0
    return jnp.where(alive, 1.0 / jnp.where(alive, sums, 1.0), 0.0)


def column_kernel(exp_ref, factor_ref, valid_ref, row_ref, col_ref):
    weight = row_scale(valid_ref, jnp.sum(row_ref[...], axis=0)) * factor_ref[...]
    col_ref[...] = jnp.broadcast_to(weighted_columns(exp_ref, weight)[None], col_ref.shape)


def weighted_rows(exp_ref, weight):
    sums = jnp.zeros((8, LANES), F32)
    for block, rows in blocks(exp_ref.shape[0]):
        part = jnp.zeros((rows.stop - rows.start, LANES), F32)
        for chunk in range(weight.shape[0]):
            values = exp_ref[rows, chunk * LANES : (chunk + 1) * LANES]
            part += values * weight[chunk : chunk + 1, :]
        sums += turned(part, block, False)
    return sums


def row_kernel(exp_ref, factor_ref, col_ref, row_ref):
    weight = 1.0 / jnp.sum(col_ref[...], axis=0)
    sums = weighted_rows(exp_ref, weight) * factor_ref[...]
    row_ref[...] = jnp.broadcast_to(sums[None], row_ref.shape)


def student_kernel(*refs):
    place_ref, *line_refs = refs[: ROWS + 1]
    slot_ref, protos_ref, stud_ref, row_ref, pay_ref, exp_ref = refs[ROWS + 1 :]
    arrived = in_order(place_ref[2], line_refs, pay_ref, SLOTS)
    onehot = place_onehot(slot_ref[:1, :], stud_ref.shape[0])
    stud_ref[...] = dot_nn(onehot, arrived).astype(BF16)
    tops, totals = exps_below_top(stud_ref, protos_ref, STUDENT_SCALE, None, exp_ref)
    row_ref[...] = tops + jnp.log(jnp.where(totals > 0.0, totals, 1.0))


def last_row_kernel(exp_ref, factor_ref, col_ref, stud_row_ref, row_ref):
    weight = 1.0 / jnp.sum(col_ref[...], axis=0)
    sums = weighted_rows(exp_ref, weight) * factor_ref[...]
    both = jnp.concatenate([sums, stud_row_ref[...]], axis=0)
    row_ref[...] = jnp.broadcast_to(both[None], row_ref.shape)


def gradient_kernel(
    base_ref, exp_ref, factor_ref, valid_ref, col_ref, row_ref, stud_ref, protos_ref,
    tok_ref, grad_ref, scale_ref, lse_ref, total_ref,
):
    tokens, width = stud_ref.shape
    weights = 1.0 / jnp.sum(col_ref[...], axis=0)
    sums = jnp.sum(row_ref[:, :8, :], axis=0)
    scale = row_scale(valid_ref, sums) * (factor_ref[...] * STUDENT_SCALE)
    lses = lse_over_first(row_ref[:, 8:, :]) - math.log(STUDENT_SCALE)
    lses = jnp.where(valid_ref[...] > 0.0, lses, -FAR_BELOW)
    for block, rows in blocks(tokens):
        size = rows.stop - rows.start
        scale_ref[rows, :] = column(scale, block, size)
        lse_ref[rows, :] = column(lses, block, size)
    step = 2 * LANES
    for chunk in range(protos_ref.shape[0] // step):
        scores = dot_nt(stud_ref[...], protos_ref[chunk * step : (chunk + 1) * step, :])
        for half in range(2):
            index = 2 * chunk + half
            lanes = slice(index * LANES, (index + 1) * LANES)
            part = scores[:, half * LANES : (half + 1) * LANES] * STUDENT_SCALE
            student = jnp.exp(part - lse_ref[...])
            target = exp_ref[:, lanes] * scale_ref[...] * weights[index : index + 1, :]
            grad_ref[:, lanes] = (student - target).astype(BF16)
    total_ref[:tokens, :] = dot_nn(grad_ref[...], protos_ref[...])
    total_ref[tokens:, :] = jnp.zeros((SLOTS, width), F32)
    for device in range(tok_ref.shape[0]):
        base = base_ref[0, device]
        start = pl.multiple_of(base // 8 * 8, 8)
        rows = pltpu.roll(total_ref[pl.ds(start, SLOTS + 8), :], SLOTS + 8 - base % 8, 0)
        tok_ref[device, :, :] = rows[:SLOTS, :].astype(BF16)


def proto_kernel(place_ref, grad_ref, stud_ref, near_ref, far_ref):
    share = near_ref.shape[1]
    group = place_ref[0]
    for away in range(PROTO // 2):
        x = lax.rem(group // 2 + away, PROTO // 2)
        core = lax.rem(group, 2)
        start = pl.multiple_of((2 * x + 1 - core) * share, share)
        far_ref[away, :, :] = dot_tn(grad_ref[:, pl.ds(start, share)], stud_ref[...])
        start = pl.multiple_of((2 * x + core) * share, share)
        near_ref[away, :, :] = dot_tn(grad_ref[:, pl.ds(start, share)], stud_ref[...])


def sum_kernel(parts_ref, near_ref, *refs):
    *far_refs, out_ref, proto_ref = refs
    total = jnp.sum(parts_ref[...].astype(F32), axis=0)
    out_ref[...] = jnp.broadcast_to(total[None], out_ref.shape)
    total = near_ref[0]
    for far_ref in far_refs:
        total = total + far_ref[...]
    proto_ref[...] = total


def patch_kernel(place_ref, count_ref, mask_ref, onehot_ref):
    patches = onehot_ref.shape[0]
    device = place_ref[1]
    wanted = iota((patches, CAP), 1)
    rank = (wanted % SLOTS) * PROTO + row_offset(wanted // SLOTS, device)
    at = (iota((patches, CAP), 0) == rank).astype(F32)
    mask = jnp.broadcast_to(mask_ref[...].astype(F32), (8, patches))
    chosen = (dot_nn(mask, at, HIGH)[:1] + 0.5).astype(jnp.int32)
    chosen = jnp.where(rank[:1, :] < count_ref[0], chosen, -1)
    onehot_ref[...] = (iota((patches, CAP), 0) == chosen).astype(BF16)


def spread_kernel(onehot_ref, rows_ref, out_ref):
    rest = rows_ref[...].reshape(CAP, out_ref.shape[1])
    total = None
    for _ in range(3):
        part = rest.astype(BF16)
        rest = rest - part.astype(F32)
        moved = dot_nn(onehot_ref[...], part)
        total = moved if total is None else total + moved
    out_ref[...] = total


def call(kernel, outs, inputs, scalars=0, scratch=(), cost=None):
    smem = [pl.BlockSpec(memory_space=pltpu.SMEM)] * scalars
    arrays = [pl.BlockSpec(memory_space=pltpu.VMEM)] * (len(inputs) - scalars)
    return pl.pallas_call(
        kernel,
        out_shape=[jax.ShapeDtypeStruct(shape, dtype) for shape, dtype in outs],
        in_specs=smem + arrays,
        out_specs=[pl.BlockSpec(memory_space=pltpu.VMEM)] * len(outs),
        scratch_shapes=list(scratch),
        compiler_params=pltpu.CompilerParams(vmem_limit_bytes=VMEM),
        cost_estimate=cost,
    )(*inputs)


def most_tokens(devices):
    slack = sum((PROTO - 1 - device % PROTO) for device in range(devices))
    return -(-((BAL * devices + slack) // PROTO) // 16) * 16


def exchange(parts, axis):
    return lax.all_to_all(parts, axis, 0, 0, tiled=True)


def on_device(devices, teacher_patches, student_patches, prototypes, mask_index, counts):
    patches, width = teacher_patches.shape
    share = prototypes.shape[0]
    protos_held = PROTO * share
    chunks = protos_held // LANES
    tokens = most_tokens(devices)
    line = devices // ROWS
    group = lax.axis_index("proto")
    y = lax.axis_index("y")
    device = y * line + lax.axis_index("z")
    place = jnp.stack([group, device, y]).astype(jnp.int32)

    half = PROTO // 2
    swap = [(p, p ^ 1) for p in range(PROTO)]
    routes = [[(p, (p + 2 * away) % PROTO) for p in range(PROTO)] for away in range(half)]
    (pay,) = pl.pallas_call(
        pick_kernel,
        out_shape=[
            jax.ShapeDtypeStruct((line, 2 * SLOTS, width), BF16),
        ],
        in_specs=[
            pl.BlockSpec(memory_space=pltpu.SMEM),
            pl.BlockSpec(memory_space=pltpu.VMEM),
            pl.BlockSpec(memory_space=pl.ANY),
            pl.BlockSpec(memory_space=pl.ANY),
        ],
        out_specs=[pl.BlockSpec(memory_space=pltpu.VMEM)],
        scratch_shapes=[pltpu.VMEM((2, patches, width), BF16), pltpu.SemaphoreType.DMA((2,))],
        compiler_params=pltpu.CompilerParams(vmem_limit_bytes=60 * 1024 * 1024),
    )(counts, mask_index, teacher_patches, student_patches)
    pay = exchange(pay, "z")
    lines = [pay]
    for away in range(1, ROWS):
        route = [(i, (i - away) % ROWS) for i in range(ROWS)]
        lines.append(lax.ppermute(pay, "y", route))
    pair = jnp.stack([prototypes, lax.ppermute(prototypes, "proto", swap)])
    pairs_held = [pair]
    for away in range(1, half):
        pairs_held.append(lax.ppermute(pair, "proto", routes[-away % half]))
    (protos,) = call(
        prototypes_kernel, [((protos_held, width), BF16)], (place, *pairs_held), scalars=1
    )
    (onehot,) = call(
        patch_kernel, [((patches, CAP), BF16)], (place, counts, mask_index), scalars=2
    )

    packed = ((8, LANES), F32)
    col_out = ((PROTO, chunks, LANES), F32)
    row_out = ((devices, 8, LANES), F32)
    pay_scratch = pltpu.VMEM((devices, SLOTS, width), BF16)
    pairs = tokens * protos_held
    work = pl.CostEstimate(
        flops=2 * pairs * width, bytes_accessed=8 * pairs, transcendentals=pairs
    )
    teach, slots, valid, base, col = call(
        first_kernel,
        [
            ((tokens, width), BF16),
            ((8, devices * SLOTS), F32),
            packed,
            ((8, LANES), jnp.int32),
            col_out,
        ],
        (place, *lines, protos),
        scalars=1,
        scratch=(pay_scratch,),
        cost=work,
    )
    col = exchange(col, "proto")
    stud, stud_row = call(
        student_kernel,
        [((tokens, width), BF16), packed],
        (place, *lines, slots, protos),
        scalars=1,
        scratch=(pay_scratch, pltpu.VMEM((tokens, protos_held), F32)),
        cost=work,
    )
    exps, top, row, stud_row = call(
        second_kernel,
        [((tokens, protos_held), F32), packed, row_out, packed],
        (teach, protos, col, stud_row),
        cost=work,
    )
    row = exchange(row, TOK)
    factor, col = call(third_kernel, [packed, col_out], (exps, top, valid, row))
    col = exchange(col, "proto")
    (row,) = call(row_kernel, [row_out], (exps, factor, col))
    row = exchange(row, TOK)
    (col,) = call(column_kernel, [col_out], (exps, factor, valid, row))
    col = exchange(col, "proto")
    (row,) = call(
        last_row_kernel, [((devices, 16, LANES), F32)], (exps, factor, col, stud_row)
    )
    row = exchange(row, TOK)
    grad_slots, grads = call(
        gradient_kernel,
        [((devices, SLOTS, width), BF16), ((tokens, protos_held), BF16)],
        (base, exps, factor, valid, col, row, stud, protos),
        scalars=1,
        scratch=(
            pltpu.VMEM((tokens, LANES), F32),
            pltpu.VMEM((tokens, LANES), F32),
            pltpu.VMEM((tokens + SLOTS, width), F32),
        ),
        cost=work,
    )
    near, far = call(
        proto_kernel,
        [((half, share, width), F32), ((half, share, width), F32)],
        (place, grads, stud),
        scalars=1,
        cost=work,
    )
    mine = near + lax.ppermute(far, "proto", swap)
    arrived = [lax.ppermute(mine[away], "proto", routes[away]) for away in range(1, half)]
    rows, grad_prototypes = call(
        sum_kernel,
        [((PROTO, SLOTS, width), F32), ((share, width), F32)],
        (exchange(grad_slots, TOK), mine, *arrived),
    )
    rows = exchange(rows, "proto")
    (grad_patches,) = call(spread_kernel, [((patches, width), F32)], (onehot, rows))
    return (grad_patches, grad_prototypes)


def solution(mesh):
    devices, protos = mesh.devices.shape
    shape = (ROWS, devices // ROWS, protos)
    mesh = Mesh(mesh.devices.reshape(shape), (*TOK, "proto"))
    return jax.shard_map(
        functools.partial(on_device, devices),
        mesh=mesh,
        in_specs=(
            P(TOK, None),
            P(TOK, None),
            P(("proto", *TOK), None),
            P(TOK, None),
            P(TOK),
        ),
        out_specs=(P(TOK, None), P(("proto", *TOK), None)),
        check_vma=False,
    )
```

```python
import functools
import math

import jax
import jax.numpy as jnp
from jax import lax
from jax.experimental import pallas as pl
from jax.experimental.pallas import tpu as pltpu
from jax.sharding import Mesh, PartitionSpec as P

CAP = 256
BAL = 128
PROTO = 8
SLOTS = CAP // PROTO
ROWS = 4
TOK = ("y", "z")
LANES = 128
TEACHER_SCALE = 1.0 / 0.07
STUDENT_SCALE = 1.0 / 0.1
FAR_BELOW = -1e30
VMEM = 24 * 1024 * 1024
F32 = jnp.float32
BF16 = jnp.bfloat16
HIGH = lax.Precision.HIGHEST


def iota(shape, dim):
    return lax.broadcasted_iota(jnp.int32, shape, dim)


def dot_nt(a, b, precision=None):
    return lax.dot_general(
        a, b, (((1,), (1,)), ((), ())), precision=precision, preferred_element_type=F32
    )


def dot_tn(a, b, precision=None):
    return lax.dot_general(
        a, b, (((0,), (0,)), ((), ())), precision=precision, preferred_element_type=F32
    )


def dot_nn(a, b, precision=None):
    return jnp.dot(a, b, precision=precision, preferred_element_type=F32)


def blocks(tokens):
    return [(at // LANES, slice(at, min(at + LANES, tokens))) for at in range(0, tokens, LANES)]


def turned(rows, block, first_lane_only):
    at = iota((8, LANES), 0) == block
    if first_lane_only:
        at = at & (iota((8, LANES), 1) == 0)
    short = LANES - rows.shape[0]
    if short:
        rows = jnp.concatenate([rows, jnp.zeros((short, LANES), F32)], axis=0)
    return dot_nt(at.astype(F32), rows, HIGH)


def column(packed, block, size):
    at = (iota((8, LANES), 0) == block).astype(F32)
    return dot_tn(packed, at, HIGH)[:size]


def lse_over_first(values):
    top = jnp.max(values, axis=0)
    return top + jnp.log(jnp.sum(jnp.exp(values - top[None]), axis=0))


def row_offset(group, device):
    return lax.rem(group + device, PROTO)


def pick_kernel(
    count_ref, mask_ref, teacher_ref, student_ref, pay_ref, patch_ref, sem_ref,
):
    copies = [
        pltpu.make_async_copy(source, patch_ref.at[which], sem_ref.at[which])
        for which, source in enumerate((teacher_ref, student_ref))
    ]
    for copy in copies:
        copy.start()
    patches, width = teacher_ref.shape
    device = lax.axis_index("y") * pay_ref.shape[0] + lax.axis_index("z")
    offset = row_offset(lax.axis_index("proto"), device)
    at = (iota((SLOTS, patches), 1) == iota((SLOTS, patches), 0) * PROTO + offset).astype(BF16)
    mask = jnp.broadcast_to(mask_ref[...], (LANES, patches))
    high = dot_nt(at, (mask // 256).astype(F32).astype(BF16))
    low = dot_nt(at, (mask % 256).astype(F32).astype(BF16))
    chosen = (high * 256.0 + low + 0.5).astype(jnp.int32)
    lane = iota((SLOTS, LANES), 1)
    onehot = jnp.concatenate(
        [(lane + start == chosen).astype(F32).astype(BF16) for start in range(0, patches, LANES)],
        axis=1,
    )
    held = iota((SLOTS, width), 0) * PROTO + offset < count_ref[0]
    copies[0].wait()
    teach = jnp.where(held, dot_nn(onehot, patch_ref[0]), jnp.inf).astype(BF16)
    copies[1].wait()
    stud = dot_nn(onehot, patch_ref[1]).astype(BF16)
    both = jnp.concatenate([teach, stud], axis=0)
    pay_ref[...] = jnp.broadcast_to(both[None], pay_ref.shape)


def place_onehot(place, tokens):
    return (iota((tokens, place.shape[1]), 0).astype(F32) == place).astype(BF16)


def prototypes_kernel(place_ref, *refs):
    *pair_refs, protos_ref = refs
    share = pair_refs[0].shape[1]
    for away, pair_ref in enumerate(pair_refs):
        x = lax.rem(place_ref[0] // 2 + away, PROTO // 2)
        for other in range(2):
            start = pl.multiple_of((other * (PROTO // 2) + x) * share, share)
            protos_ref[pl.ds(start, share), :] = pair_ref[other]


def by_core(sums):
    half = sums.shape[0] // 2
    core = lax.rem(lax.axis_index("proto"), 2)
    return jnp.where(core == 0, sums, jnp.concatenate([sums[half:], sums[:half]], axis=0))


def in_order(y, line_refs, pay_ref, first_slot):
    line = line_refs[0].shape[0]
    for away in range(ROWS):
        start = lax.rem(y + away, ROWS) * line
        pay_ref[pl.ds(start, line), :, :] = line_refs[away][:, first_slot : first_slot + SLOTS, :]
    devices, slots, width = pay_ref.shape
    return pay_ref[...].reshape(devices * slots, width)


def first_kernel(*refs):
    place_ref, *line_refs = refs[: ROWS + 1]
    protos_ref, teach_ref, place_out_ref, valid_ref, base_ref, col_ref, pay_ref = refs[ROWS + 1 :]
    arrived = in_order(place_ref[2], line_refs, pay_ref, 0).astype(F32)
    tokens = teach_ref.shape[0]
    slots, width = arrived.shape
    real = arrived < jnp.inf
    pick = (iota((8, width), 1) == 0).astype(BF16)
    flags = dot_nt(pick, real.astype(F32).astype(BF16))
    held = dot_nn(
        flags.astype(BF16), (iota((slots, LANES), 0) // SLOTS == iota((slots, LANES), 1)).astype(BF16)
    )
    before = dot_nn(
        held.astype(BF16), (iota((LANES, slots), 0) < iota((LANES, slots), 1) // SLOTS).astype(BF16)
    )[:1]
    bases = dot_nn(
        held.astype(BF16), (iota((LANES, LANES), 0) < iota((LANES, LANES), 1)).astype(BF16)
    )
    base_ref[...] = (bases + 0.5).astype(jnp.int32)
    inner = (iota((1, slots), 1) % SLOTS).astype(F32)
    place = jnp.where(flags[:1] > 0.5, before + inner, -1.0)
    place_out_ref[...] = jnp.broadcast_to(place, place_out_ref.shape)
    total = jnp.max(place, axis=1, keepdims=True) + 1.0
    order = iota((8, LANES), 0) * LANES + iota((8, LANES), 1)
    valid_ref[...] = (order.astype(F32) < total).astype(F32)
    onehot = place_onehot(place, tokens)
    teach = dot_nn(onehot, jnp.where(real, arrived, 0.0).astype(BF16)).astype(BF16)
    teach_ref[...] = teach
    step = 2 * LANES
    alive = iota((tokens, step), 0).astype(F32) < total
    rows = []
    for start in range(0, protos_ref.shape[0], step):
        scores = dot_nt(teach, protos_ref[start : start + step, :]) * TEACHER_SCALE
        scores = jnp.where(alive, scores, FAR_BELOW)
        top = jnp.max(scores, axis=0, keepdims=True)
        lse = top + jnp.log(jnp.sum(jnp.exp(scores - top), axis=0, keepdims=True))
        rows += [lse[:, :LANES], lse[:, LANES:]]
    col_ref[...] = jnp.broadcast_to(by_core(jnp.concatenate(rows, axis=0))[None], col_ref.shape)


def wide(packed):
    return jnp.concatenate([packed[i : i + 1, :] for i in range(packed.shape[0])], axis=1)


def exps_below_top(left_ref, protos_ref, scale, shift, out_ref):
    step = 2 * LANES
    for start in range(0, protos_ref.shape[0], step):
        scores = dot_nt(left_ref[...], protos_ref[start : start + step, :]) * scale
        if shift is not None:
            scores = scores + shift[:, start : start + step]
        out_ref[:, start : start + step] = scores
    tops = jnp.zeros((8, LANES), F32)
    totals = jnp.zeros((8, LANES), F32)
    starts = range(0, protos_ref.shape[0], LANES)
    for block, rows in blocks(left_ref.shape[0]):
        top = out_ref[rows, :LANES]
        for start in starts[1:]:
            top = jnp.maximum(top, out_ref[rows, start : start + LANES])
        top = jnp.broadcast_to(jnp.max(top, axis=1, keepdims=True), top.shape)
        sums = jnp.zeros_like(top)
        for start in starts:
            exps = jnp.exp(out_ref[rows, start : start + LANES] - top)
            out_ref[rows, start : start + LANES] = exps
            sums += exps
        tops += turned(top, block, True)
        totals += turned(sums, block, False)
    return tops, totals


def second_kernel(teach_ref, protos_ref, col_ref, stud_row_ref, exp_ref, top_ref, row_ref, stud_out_ref):
    col_pot = -wide(by_core(lse_over_first(col_ref[...])))
    tops, totals = exps_below_top(teach_ref, protos_ref, TEACHER_SCALE, col_pot, exp_ref)
    top_ref[...] = tops
    lses = tops + jnp.log(jnp.where(totals > 0.0, totals, 1.0))
    row_ref[...] = jnp.broadcast_to(lses[None], row_ref.shape)
    stud_out_ref[...] = stud_row_ref[...]


def weighted_columns(exp_ref, weight):
    chunks = exp_ref.shape[1] // LANES
    sums = [jnp.zeros((8, LANES), F32) for _ in range(chunks)]
    for block, rows in blocks(exp_ref.shape[0]):
        size = rows.stop - rows.start
        factor = column(weight, block, size)
        for chunk in range(chunks):
            part = exp_ref[rows, chunk * LANES : (chunk + 1) * LANES] * factor
            sums[chunk] += jnp.sum(part.reshape(size // 8, 8, LANES), axis=0)
    return jnp.concatenate([jnp.sum(part, axis=0, keepdims=True) for part in sums], axis=0)


def third_kernel(exp_ref, top_ref, valid_ref, row_ref, factor_ref, col_ref):
    row_pot = -lse_over_first(row_ref[...])
    factor = jnp.where(valid_ref[...] > 0.0, jnp.exp(top_ref[...] + row_pot), 0.0)
    factor_ref[...] = factor
    col_ref[...] = jnp.broadcast_to(by_core(weighted_columns(exp_ref, factor))[None], col_ref.shape)


def row_scale(valid_ref, sums):
    alive = valid_ref[...] > 0.0
    return jnp.where(alive, 1.0 / jnp.where(alive, sums, 1.0), 0.0)


def column_kernel(exp_ref, factor_ref, valid_ref, row_ref, col_ref):
    weight = row_scale(valid_ref, jnp.sum(row_ref[...], axis=0)) * factor_ref[...]
    col_ref[...] = jnp.broadcast_to(by_core(weighted_columns(exp_ref, weight))[None], col_ref.shape)


def weighted_rows(exp_ref, weight):
    sums = jnp.zeros((8, LANES), F32)
    for block, rows in blocks(exp_ref.shape[0]):
        part = jnp.zeros((rows.stop - rows.start, LANES), F32)
        for chunk in range(weight.shape[0]):
            values = exp_ref[rows, chunk * LANES : (chunk + 1) * LANES]
            part += values * weight[chunk : chunk + 1, :]
        sums += turned(part, block, False)
    return sums


def row_kernel(exp_ref, factor_ref, col_ref, row_ref):
    weight = 1.0 / by_core(jnp.sum(col_ref[...], axis=0))
    sums = weighted_rows(exp_ref, weight) * factor_ref[...]
    row_ref[...] = jnp.broadcast_to(sums[None], row_ref.shape)


def student_kernel(*refs):
    place_ref, *line_refs = refs[: ROWS + 1]
    slot_ref, protos_ref, stud_ref, row_ref, pay_ref, exp_ref = refs[ROWS + 1 :]
    arrived = in_order(place_ref[2], line_refs, pay_ref, SLOTS)
    onehot = place_onehot(slot_ref[:1, :], stud_ref.shape[0])
    stud_ref[...] = dot_nn(onehot, arrived).astype(BF16)
    tops, totals = exps_below_top(stud_ref, protos_ref, STUDENT_SCALE, None, exp_ref)
    row_ref[...] = tops + jnp.log(jnp.where(totals > 0.0, totals, 1.0))


def last_row_kernel(exp_ref, factor_ref, col_ref, stud_row_ref, row_ref):
    weight = 1.0 / by_core(jnp.sum(col_ref[...], axis=0))
    sums = weighted_rows(exp_ref, weight) * factor_ref[...]
    both = jnp.concatenate([sums, stud_row_ref[...]], axis=0)
    row_ref[...] = jnp.broadcast_to(both[None], row_ref.shape)


def gradient_kernel(
    base_ref, exp_ref, factor_ref, valid_ref, col_ref, row_ref, stud_ref, protos_ref,
    tok_ref, near_ref, far_ref, scale_ref, lse_ref, total_ref,
):
    tokens, width = stud_ref.shape
    weights = 1.0 / by_core(jnp.sum(col_ref[...], axis=0))
    sums = jnp.sum(row_ref[:, :8, :], axis=0)
    scale = row_scale(valid_ref, sums) * (factor_ref[...] * STUDENT_SCALE)
    lses = lse_over_first(row_ref[:, 8:, :]) - math.log(STUDENT_SCALE)
    lses = jnp.where(valid_ref[...] > 0.0, lses, -FAR_BELOW)
    for block, rows in blocks(tokens):
        size = rows.stop - rows.start
        scale_ref[rows, :] = column(scale, block, size)
        lse_ref[rows, :] = column(lses, block, size)
    step = 2 * LANES
    for chunk in range(protos_ref.shape[0] // step):
        scores = dot_nt(stud_ref[...], protos_ref[chunk * step : (chunk + 1) * step, :])
        for half in range(2):
            index = 2 * chunk + half
            lanes = slice(index * LANES, (index + 1) * LANES)
            part = scores[:, half * LANES : (half + 1) * LANES] * STUDENT_SCALE
            student = jnp.exp(part - lse_ref[...])
            target = exp_ref[:, lanes] * scale_ref[...] * weights[index : index + 1, :]
            grads_ref, at = (near_ref, index) if 2 * index < weights.shape[0] else (far_ref, index - weights.shape[0] // 2)
            grads_ref[:, at * LANES : (at + 1) * LANES] = (student - target).astype(BF16)
    held = near_ref.shape[1]
    total_ref[:tokens, :] = dot_nn(near_ref[...], protos_ref[:held, :]) + dot_nn(
        far_ref[:, :held], protos_ref[held:, :]
    )
    far_ref[:, held:] = stud_ref[...]
    total_ref[tokens:, :] = jnp.zeros((SLOTS, width), F32)
    for device in range(tok_ref.shape[0]):
        base = base_ref[0, device]
        start = pl.multiple_of(base // 8 * 8, 8)
        rows = pltpu.roll(total_ref[pl.ds(start, SLOTS + 8), :], SLOTS + 8 - base % 8, 0)
        tok_ref[device, :, :] = rows[:SLOTS, :].astype(BF16)


def proto_kernel(place_ref, near_ref, far_ref, stud_ref, out_ref):
    _, share, width = out_ref.shape
    other = far_ref[:, near_ref.shape[1] :]
    for away in range(PROTO // 2):
        start = pl.multiple_of(lax.rem(place_ref[0] // 2 + away, PROTO // 2) * share, share)
        part = pl.ds(start, share)
        out_ref[away, :, :] = dot_tn(near_ref[:, part], stud_ref[...]) + dot_tn(far_ref[:, part], other)


def sum_kernel(parts_ref, near_ref, *refs):
    *far_refs, out_ref, proto_ref = refs
    total = jnp.sum(parts_ref[...].astype(F32), axis=0)
    out_ref[...] = jnp.broadcast_to(total[None], out_ref.shape)
    total = near_ref[0]
    for far_ref in far_refs:
        total = total + far_ref[...]
    proto_ref[...] = total


def patch_kernel(place_ref, count_ref, mask_ref, onehot_ref):
    patches = onehot_ref.shape[0]
    device = place_ref[1]
    wanted = iota((patches, CAP), 1)
    rank = (wanted % SLOTS) * PROTO + row_offset(wanted // SLOTS, device)
    at = (iota((patches, CAP), 0) == rank).astype(F32)
    mask = jnp.broadcast_to(mask_ref[...].astype(F32), (8, patches))
    chosen = (dot_nn(mask, at, HIGH)[:1] + 0.5).astype(jnp.int32)
    chosen = jnp.where(rank[:1, :] < count_ref[0], chosen, -1)
    onehot_ref[...] = (iota((patches, CAP), 0) == chosen).astype(BF16)


def spread_kernel(onehot_ref, rows_ref, out_ref):
    rest = rows_ref[...].reshape(CAP, out_ref.shape[1])
    total = None
    for _ in range(3):
        part = rest.astype(BF16)
        rest = rest - part.astype(F32)
        moved = dot_nn(onehot_ref[...], part)
        total = moved if total is None else total + moved
    out_ref[...] = total


def call(kernel, outs, inputs, scalars=0, scratch=(), cost=None):
    smem = [pl.BlockSpec(memory_space=pltpu.SMEM)] * scalars
    arrays = [pl.BlockSpec(memory_space=pltpu.VMEM)] * (len(inputs) - scalars)
    return pl.pallas_call(
        kernel,
        out_shape=[jax.ShapeDtypeStruct(shape, dtype) for shape, dtype in outs],
        in_specs=smem + arrays,
        out_specs=[pl.BlockSpec(memory_space=pltpu.VMEM)] * len(outs),
        scratch_shapes=list(scratch),
        compiler_params=pltpu.CompilerParams(vmem_limit_bytes=VMEM),
        cost_estimate=cost,
    )(*inputs)


def most_tokens(devices):
    slack = sum((PROTO - 1 - device % PROTO) for device in range(devices))
    return -(-((BAL * devices + slack) // PROTO) // 16) * 16


def exchange(parts, axis):
    return lax.all_to_all(parts, axis, 0, 0, tiled=True)


def on_device(devices, teacher_patches, student_patches, prototypes, mask_index, counts):
    patches, width = teacher_patches.shape
    share = prototypes.shape[0]
    protos_held = PROTO * share
    chunks = protos_held // LANES
    tokens = most_tokens(devices)
    line = devices // ROWS
    group = lax.axis_index("proto")
    y = lax.axis_index("y")
    device = y * line + lax.axis_index("z")
    place = jnp.stack([group, device, y]).astype(jnp.int32)

    half = PROTO // 2
    swap = [(p, p ^ 1) for p in range(PROTO)]
    routes = [[(p, (p + 2 * away) % PROTO) for p in range(PROTO)] for away in range(half)]
    (pay,) = pl.pallas_call(
        pick_kernel,
        out_shape=[
            jax.ShapeDtypeStruct((line, 2 * SLOTS, width), BF16),
        ],
        in_specs=[
            pl.BlockSpec(memory_space=pltpu.SMEM),
            pl.BlockSpec(memory_space=pltpu.VMEM),
            pl.BlockSpec(memory_space=pl.ANY),
            pl.BlockSpec(memory_space=pl.ANY),
        ],
        out_specs=[pl.BlockSpec(memory_space=pltpu.VMEM)],
        scratch_shapes=[pltpu.VMEM((2, patches, width), BF16), pltpu.SemaphoreType.DMA((2,))],
        compiler_params=pltpu.CompilerParams(vmem_limit_bytes=60 * 1024 * 1024),
    )(counts, mask_index, teacher_patches, student_patches)
    pay = exchange(pay, "z")
    lines = [pay]
    for away in range(1, ROWS):
        route = [(i, (i - away) % ROWS) for i in range(ROWS)]
        lines.append(lax.ppermute(pay, "y", route))
    pair = jnp.stack([prototypes, lax.ppermute(prototypes, "proto", swap)])
    pairs_held = [pair]
    for away in range(1, half):
        pairs_held.append(lax.ppermute(pair, "proto", routes[-away % half]))
    (protos,) = call(
        prototypes_kernel, [((protos_held, width), BF16)], (place, *pairs_held), scalars=1
    )
    (onehot,) = call(
        patch_kernel, [((patches, CAP), BF16)], (place, counts, mask_index), scalars=2
    )

    packed = ((8, LANES), F32)
    col_out = ((PROTO, chunks, LANES), F32)
    row_out = ((devices, 8, LANES), F32)
    pay_scratch = pltpu.VMEM((devices, SLOTS, width), BF16)
    pairs = tokens * protos_held
    work = pl.CostEstimate(
        flops=2 * pairs * width, bytes_accessed=8 * pairs, transcendentals=pairs
    )
    teach, slots, valid, base, col = call(
        first_kernel,
        [
            ((tokens, width), BF16),
            ((8, devices * SLOTS), F32),
            packed,
            ((8, LANES), jnp.int32),
            col_out,
        ],
        (place, *lines, protos),
        scalars=1,
        scratch=(pay_scratch,),
        cost=work,
    )
    col = exchange(col, "proto")
    stud, stud_row = call(
        student_kernel,
        [((tokens, width), BF16), packed],
        (place, *lines, slots, protos),
        scalars=1,
        scratch=(pay_scratch, pltpu.VMEM((tokens, protos_held), F32)),
        cost=work,
    )
    exps, top, row, stud_row = call(
        second_kernel,
        [((tokens, protos_held), F32), packed, row_out, packed],
        (teach, protos, col, stud_row),
        cost=work,
    )
    row = exchange(row, TOK)
    factor, col = call(third_kernel, [packed, col_out], (exps, top, valid, row))
    col = exchange(col, "proto")
    (row,) = call(row_kernel, [row_out], (exps, factor, col))
    row = exchange(row, TOK)
    (col,) = call(column_kernel, [col_out], (exps, factor, valid, row))
    col = exchange(col, "proto")
    (row,) = call(
        last_row_kernel, [((devices, 16, LANES), F32)], (exps, factor, col, stud_row)
    )
    row = exchange(row, TOK)
    grad_slots, near, far = call(
        gradient_kernel,
        [
            ((devices, SLOTS, width), BF16),
            ((tokens, protos_held // 2), BF16),
            ((tokens, protos_held // 2 + width), BF16),
        ],
        (base, exps, factor, valid, col, row, stud, protos),
        scalars=1,
        scratch=(
            pltpu.VMEM((tokens, LANES), F32),
            pltpu.VMEM((tokens, LANES), F32),
            pltpu.VMEM((tokens + SLOTS, width), F32),
        ),
        cost=work,
    )
    (mine,) = call(
        proto_kernel,
        [((half, share, width), F32)],
        (place, near, lax.ppermute(far, "proto", swap), stud),
        scalars=1,
        cost=work,
    )
    arrived = [lax.ppermute(mine[away], "proto", routes[away]) for away in range(1, half)]
    rows, grad_prototypes = call(
        sum_kernel,
        [((PROTO, SLOTS, width), F32), ((share, width), F32)],
        (exchange(grad_slots, TOK), mine, *arrived),
    )
    rows = exchange(rows, "proto")
    (grad_patches,) = call(spread_kernel, [((patches, width), F32)], (onehot, rows))
    return (grad_patches, grad_prototypes)


def solution(mesh):
    devices, protos = mesh.devices.shape
    shape = (ROWS, devices // ROWS, protos)
    mesh = Mesh(mesh.devices.reshape(shape), (*TOK, "proto"))
    return jax.shard_map(
        functools.partial(on_device, devices),
        mesh=mesh,
        in_specs=(
            P(TOK, None),
            P(TOK, None),
            P(("proto", *TOK), None),
            P(TOK, None),
            P(TOK),
        ),
        out_specs=(P(TOK, None), P(("proto", *TOK), None)),
        check_vma=False,
    )
```

```python
import functools
import math

import jax
import jax.numpy as jnp
from jax import lax
from jax.experimental import pallas as pl
from jax.experimental.pallas import tpu as pltpu
from jax.sharding import Mesh, PartitionSpec as P

CAP = 256
BAL = 128
PROTO = 8
SLOTS = CAP // PROTO
ROWS = 4
TOK = ("y", "z")
USED = 5
LANES = 128
TEACHER_SCALE = 1.0 / 0.07
STUDENT_SCALE = 1.0 / 0.1
FAR_BELOW = -1e30
VMEM = 24 * 1024 * 1024
F32 = jnp.float32
BF16 = jnp.bfloat16
HIGH = lax.Precision.HIGHEST


def iota(shape, dim):
    return lax.broadcasted_iota(jnp.int32, shape, dim)


def dot_nt(a, b, precision=None):
    return lax.dot_general(
        a, b, (((1,), (1,)), ((), ())), precision=precision, preferred_element_type=F32
    )


def dot_tn(a, b, precision=None):
    return lax.dot_general(
        a, b, (((0,), (0,)), ((), ())), precision=precision, preferred_element_type=F32
    )


def dot_nn(a, b, precision=None):
    return jnp.dot(a, b, precision=precision, preferred_element_type=F32)


def blocks(tokens):
    return [(at // LANES, slice(at, min(at + LANES, tokens))) for at in range(0, tokens, LANES)]


def turned(rows, block, first_lane_only):
    at = iota((8, LANES), 0) == block
    if first_lane_only:
        at = at & (iota((8, LANES), 1) == 0)
    short = LANES - rows.shape[0]
    if short:
        rows = jnp.concatenate([rows, jnp.zeros((short, LANES), F32)], axis=0)
    return dot_nt(at.astype(F32), rows, HIGH)


def column(packed, block, size):
    at = (iota((8, LANES), 0) == block).astype(F32)
    return dot_tn(packed, at, HIGH)[:size]


def lse_over_first(values):
    top = jnp.max(values, axis=0)
    return top + jnp.log(jnp.sum(jnp.exp(values - top[None]), axis=0))


def row_offset(group, device):
    return lax.rem(group + device, PROTO)


def pick_kernel(
    count_ref, mask_ref, teacher_ref, student_ref, pay_ref, patch_ref, sem_ref,
):
    copies = [
        pltpu.make_async_copy(source, patch_ref.at[which], sem_ref.at[which])
        for which, source in enumerate((teacher_ref, student_ref))
    ]
    for copy in copies:
        copy.start()
    patches, width = teacher_ref.shape
    device = lax.axis_index("y") * pay_ref.shape[0] + lax.axis_index("z")
    offset = row_offset(lax.axis_index("proto"), device)
    at = (iota((SLOTS, patches), 1) == iota((SLOTS, patches), 0) * PROTO + offset).astype(BF16)
    mask = jnp.broadcast_to(mask_ref[...], (LANES, patches))
    high = dot_nt(at, (mask // 256).astype(F32).astype(BF16))
    low = dot_nt(at, (mask % 256).astype(F32).astype(BF16))
    chosen = (high * 256.0 + low + 0.5).astype(jnp.int32)
    lane = iota((SLOTS, LANES), 1)
    onehot = jnp.concatenate(
        [(lane + start == chosen).astype(F32).astype(BF16) for start in range(0, patches, LANES)],
        axis=1,
    )
    held = iota((SLOTS, width), 0) * PROTO + offset < count_ref[0]
    copies[0].wait()
    teach = jnp.where(held, dot_nn(onehot, patch_ref[0]), jnp.inf).astype(BF16)
    copies[1].wait()
    stud = dot_nn(onehot, patch_ref[1]).astype(BF16)
    both = jnp.concatenate([teach, stud], axis=0)
    pay_ref[...] = jnp.broadcast_to(both[None], pay_ref.shape)


def place_onehot(place, tokens):
    return (iota((tokens, place.shape[1]), 0).astype(F32) == place).astype(BF16)


def prototypes_kernel(place_ref, *refs):
    *pair_refs, protos_ref = refs
    share = pair_refs[0].shape[1]
    group = place_ref[0]
    core = lax.rem(group, 2)
    for away, pair_ref in enumerate(pair_refs):
        x = lax.rem(group // 2 + away, PROTO // 2)
        for other in range(2):
            start = pl.multiple_of((2 * x + (core + other) % 2) * share, share)
            protos_ref[pl.ds(start, share), :] = pair_ref[other]


def in_order(y, line_refs, pay_ref, first_slot):
    line = line_refs[0].shape[0]
    for away in range(ROWS):
        start = lax.rem(y + away, ROWS) * line
        pay_ref[pl.ds(start, line), :, :] = line_refs[away][:, first_slot : first_slot + SLOTS, :]
    devices, slots, width = pay_ref.shape
    return pay_ref[...].reshape(devices * slots, width)


def first_kernel(*refs):
    place_ref, *line_refs = refs[: ROWS + 1]
    protos_ref, teach_ref, place_out_ref, valid_ref, base_ref, col_ref, pay_ref = refs[ROWS + 1 :]
    arrived = in_order(place_ref[2], line_refs, pay_ref, 0).astype(F32)
    tokens = teach_ref.shape[0]
    slots, width = arrived.shape
    real = arrived < jnp.inf
    pick = (iota((8, width), 1) == 0).astype(BF16)
    flags = dot_nt(pick, real.astype(F32).astype(BF16))
    held = dot_nn(
        flags.astype(BF16), (iota((slots, LANES), 0) // SLOTS == iota((slots, LANES), 1)).astype(BF16)
    )
    before = dot_nn(
        held.astype(BF16), (iota((LANES, slots), 0) < iota((LANES, slots), 1) // SLOTS).astype(BF16)
    )[:1]
    bases = dot_nn(
        held.astype(BF16), (iota((LANES, LANES), 0) < iota((LANES, LANES), 1)).astype(BF16)
    )
    base_ref[...] = (bases + 0.5).astype(jnp.int32)
    inner = (iota((1, slots), 1) % SLOTS).astype(F32)
    place = jnp.where(flags[:1] > 0.5, before + inner, -1.0)
    place_out_ref[...] = jnp.broadcast_to(place, place_out_ref.shape)
    total = jnp.max(place, axis=1, keepdims=True) + 1.0
    order = iota((8, LANES), 0) * LANES + iota((8, LANES), 1)
    valid_ref[...] = (order.astype(F32) < total).astype(F32)
    onehot = place_onehot(place, tokens)
    teach = dot_nn(onehot, jnp.where(real, arrived, 0.0).astype(BF16)).astype(BF16)
    teach_ref[...] = teach
    step = 2 * LANES
    alive = iota((tokens, step), 0).astype(F32) < total
    rows = []
    for start in range(0, protos_ref.shape[0], step):
        scores = dot_nt(teach, protos_ref[start : start + step, :]) * TEACHER_SCALE
        scores = jnp.where(alive, scores, FAR_BELOW)
        top = jnp.max(scores, axis=0, keepdims=True)
        lse = top + jnp.log(jnp.sum(jnp.exp(scores - top), axis=0, keepdims=True))
        rows += [lse[:, :LANES], lse[:, LANES:]]
    col_ref[...] = jnp.broadcast_to(jnp.concatenate(rows, axis=0)[None], col_ref.shape)


def wide(packed):
    return jnp.concatenate([packed[i : i + 1, :] for i in range(packed.shape[0])], axis=1)


def exps_below_top(left_ref, protos_ref, scale, shift, out_ref):
    step = 2 * LANES
    for start in range(0, protos_ref.shape[0], step):
        scores = dot_nt(left_ref[...], protos_ref[start : start + step, :]) * scale
        if shift is not None:
            scores = scores + shift[:, start : start + step]
        out_ref[:, start : start + step] = scores
    tops = jnp.zeros((8, LANES), F32)
    totals = jnp.zeros((8, LANES), F32)
    starts = range(0, protos_ref.shape[0], LANES)
    for block, rows in blocks(left_ref.shape[0]):
        top = out_ref[rows, :LANES]
        for start in starts[1:]:
            top = jnp.maximum(top, out_ref[rows, start : start + LANES])
        top = jnp.broadcast_to(jnp.max(top, axis=1, keepdims=True), top.shape)
        sums = jnp.zeros_like(top)
        for start in starts:
            exps = jnp.exp(out_ref[rows, start : start + LANES] - top)
            out_ref[rows, start : start + LANES] = exps
            sums += exps
        tops += turned(top, block, True)
        totals += turned(sums, block, False)
    return tops, totals


def second_kernel(teach_ref, protos_ref, col_ref, stud_row_ref, exp_ref, top_ref, row_ref, stud_out_ref):
    col_pot = -wide(lse_over_first(col_ref[...]))
    tops, totals = exps_below_top(teach_ref, protos_ref, TEACHER_SCALE, col_pot, exp_ref)
    top_ref[...] = tops
    lses = tops + jnp.log(jnp.where(totals > 0.0, totals, 1.0))
    row_ref[...] = jnp.broadcast_to(lses[None], row_ref.shape)
    stud_out_ref[...] = stud_row_ref[...]


def weighted_columns(exp_ref, weight):
    chunks = exp_ref.shape[1] // LANES
    sums = [jnp.zeros((8, LANES), F32) for _ in range(chunks)]
    for block, rows in blocks(exp_ref.shape[0]):
        size = rows.stop - rows.start
        factor = column(weight, block, size)
        for chunk in range(chunks):
            part = exp_ref[rows, chunk * LANES : (chunk + 1) * LANES] * factor
            sums[chunk] += jnp.sum(part.reshape(size // 8, 8, LANES), axis=0)
    return jnp.concatenate([jnp.sum(part, axis=0, keepdims=True) for part in sums], axis=0)


def third_kernel(exp_ref, top_ref, valid_ref, row_ref, factor_ref, col_ref):
    row_pot = -lse_over_first(row_ref[...])
    factor = jnp.where(valid_ref[...] > 0.0, jnp.exp(top_ref[...] + row_pot), 0.0)
    factor_ref[...] = factor
    col_ref[...] = jnp.broadcast_to(weighted_columns(exp_ref, factor)[None], col_ref.shape)


def row_scale(valid_ref, sums):
    alive = valid_ref[...] > 0.0
    return jnp.where(alive, 1.0 / jnp.where(alive, sums, 1.0), 0.0)


def column_kernel(exp_ref, factor_ref, valid_ref, row_ref, col_ref):
    weight = row_scale(valid_ref, jnp.sum(row_ref[...], axis=0)) * factor_ref[...]
    col_ref[...] = jnp.broadcast_to(weighted_columns(exp_ref, weight)[None], col_ref.shape)


def weighted_rows(exp_ref, weight):
    sums = jnp.zeros((8, LANES), F32)
    for block, rows in blocks(exp_ref.shape[0]):
        part = jnp.zeros((rows.stop - rows.start, LANES), F32)
        for chunk in range(weight.shape[0]):
            values = exp_ref[rows, chunk * LANES : (chunk + 1) * LANES]
            part += values * weight[chunk : chunk + 1, :]
        sums += turned(part, block, False)
    return sums


def row_kernel(first, exp_ref, factor_ref, col_ref, stud_row_ref, row_ref):
    weight = 1.0 / jnp.sum(col_ref[...], axis=0)
    sums = weighted_rows(exp_ref, weight) * factor_ref[...]
    free = 8 - USED
    both = jnp.concatenate([sums[:USED], stud_row_ref[first : first + free, :]], axis=0)
    row_ref[...] = jnp.broadcast_to(both[None], row_ref.shape)


def student_kernel(*refs):
    place_ref, *line_refs = refs[: ROWS + 1]
    slot_ref, protos_ref, stud_ref, row_ref, pay_ref, exp_ref = refs[ROWS + 1 :]
    arrived = in_order(place_ref[2], line_refs, pay_ref, SLOTS)
    onehot = place_onehot(slot_ref[:1, :], stud_ref.shape[0])
    stud_ref[...] = dot_nn(onehot, arrived).astype(BF16)
    tops, totals = exps_below_top(stud_ref, protos_ref, STUDENT_SCALE, None, exp_ref)
    row_ref[...] = tops + jnp.log(jnp.where(totals > 0.0, totals, 1.0))


def gradient_kernel(
    base_ref, exp_ref, factor_ref, valid_ref, col_ref, early_ref, row_ref, stud_ref, protos_ref,
    tok_ref, grad_ref, score_ref, scale_ref, lse_ref, total_ref,
):
    tokens, width = stud_ref.shape
    weights = 1.0 / jnp.sum(col_ref[...], axis=0)
    sums = jnp.sum(row_ref[...], axis=0)
    scale = row_scale(valid_ref, sums) * (factor_ref[...] * STUDENT_SCALE)
    early, late = lse_over_first(early_ref[...]), lse_over_first(row_ref[...])
    lses = jnp.concatenate([early[USED:], late[USED:], jnp.zeros((2, LANES), F32)], axis=0)
    lses = lses - math.log(STUDENT_SCALE)
    lses = jnp.where(valid_ref[...] > 0.0, lses, -FAR_BELOW)
    for block, rows in blocks(tokens):
        size = rows.stop - rows.start
        scale_ref[rows, :] = column(scale, block, size)
        lse_ref[rows, :] = column(lses, block, size)
    step = 2 * LANES
    for chunk in range(protos_ref.shape[0] // step):
        slot = chunk % 2
        score_ref[slot] = dot_nt(stud_ref[...], protos_ref[chunk * step : (chunk + 1) * step, :])
        for half in range(2):
            index = 2 * chunk + half
            lanes = slice(index * LANES, (index + 1) * LANES)
            for _, rows in blocks(tokens):
                part = score_ref[slot, rows, half * LANES : (half + 1) * LANES] * STUDENT_SCALE
                student = jnp.exp(part - lse_ref[rows, :])
                target = exp_ref[rows, lanes] * scale_ref[rows, :] * weights[index : index + 1, :]
                grad_ref[rows, lanes] = (student - target).astype(BF16)
    total_ref[:tokens, :] = dot_nn(grad_ref[...], protos_ref[...])
    total_ref[tokens:, :] = jnp.zeros((SLOTS, width), F32)
    for device in range(tok_ref.shape[0]):
        base = base_ref[0, device]
        start = pl.multiple_of(base // 8 * 8, 8)
        rows = pltpu.roll(total_ref[pl.ds(start, SLOTS + 8), :], SLOTS + 8 - base % 8, 0)
        tok_ref[device, :, :] = rows[:SLOTS, :].astype(BF16)


def proto_kernel(place_ref, grad_ref, stud_ref, near_ref, far_ref):
    share = near_ref.shape[1]
    group = place_ref[0]
    for away in range(PROTO // 2):
        x = lax.rem(group // 2 + away, PROTO // 2)
        core = lax.rem(group, 2)
        start = pl.multiple_of((2 * x + 1 - core) * share, share)
        far_ref[away, :, :] = dot_tn(grad_ref[:, pl.ds(start, share)], stud_ref[...])
        start = pl.multiple_of((2 * x + core) * share, share)
        near_ref[away, :, :] = dot_tn(grad_ref[:, pl.ds(start, share)], stud_ref[...])


def sum_kernel(parts_ref, near_ref, *refs):
    *far_refs, out_ref, proto_ref = refs
    total = jnp.sum(parts_ref[...].astype(F32), axis=0)
    out_ref[...] = jnp.broadcast_to(total[None], out_ref.shape)
    total = near_ref[0]
    for far_ref in far_refs:
        total = total + far_ref[...]
    proto_ref[...] = total


def patch_kernel(place_ref, count_ref, mask_ref, onehot_ref):
    patches = onehot_ref.shape[0]
    device = place_ref[1]
    wanted = iota((patches, CAP), 1)
    rank = (wanted % SLOTS) * PROTO + row_offset(wanted // SLOTS, device)
    at = (iota((patches, CAP), 0) == rank).astype(F32)
    mask = jnp.broadcast_to(mask_ref[...].astype(F32), (8, patches))
    chosen = (dot_nn(mask, at, HIGH)[:1] + 0.5).astype(jnp.int32)
    chosen = jnp.where(rank[:1, :] < count_ref[0], chosen, -1)
    onehot_ref[...] = (iota((patches, CAP), 0) == chosen).astype(BF16)


def spread_kernel(onehot_ref, rows_ref, out_ref):
    rest = rows_ref[...].reshape(CAP, out_ref.shape[1])
    total = None
    for _ in range(3):
        part = rest.astype(BF16)
        rest = rest - part.astype(F32)
        moved = dot_nn(onehot_ref[...], part)
        total = moved if total is None else total + moved
    out_ref[...] = total


def call(kernel, outs, inputs, scalars=0, scratch=(), cost=None):
    smem = [pl.BlockSpec(memory_space=pltpu.SMEM)] * scalars
    arrays = [pl.BlockSpec(memory_space=pltpu.VMEM)] * (len(inputs) - scalars)
    return pl.pallas_call(
        kernel,
        out_shape=[jax.ShapeDtypeStruct(shape, dtype) for shape, dtype in outs],
        in_specs=smem + arrays,
        out_specs=[pl.BlockSpec(memory_space=pltpu.VMEM)] * len(outs),
        scratch_shapes=list(scratch),
        compiler_params=pltpu.CompilerParams(vmem_limit_bytes=VMEM),
        cost_estimate=cost,
    )(*inputs)


def most_tokens(devices):
    slack = sum((PROTO - 1 - device % PROTO) for device in range(devices))
    return -(-((BAL * devices + slack) // PROTO) // 16) * 16


def exchange(parts, axis):
    return lax.all_to_all(parts, axis, 0, 0, tiled=True)


def on_device(devices, teacher_patches, student_patches, prototypes, mask_index, counts):
    patches, width = teacher_patches.shape
    share = prototypes.shape[0]
    protos_held = PROTO * share
    chunks = protos_held // LANES
    tokens = most_tokens(devices)
    line = devices // ROWS
    group = lax.axis_index("proto")
    y = lax.axis_index("y")
    device = y * line + lax.axis_index("z")
    place = jnp.stack([group, device, y]).astype(jnp.int32)

    half = PROTO // 2
    swap = [(p, p ^ 1) for p in range(PROTO)]
    routes = [[(p, (p + 2 * away) % PROTO) for p in range(PROTO)] for away in range(half)]
    (pay,) = pl.pallas_call(
        pick_kernel,
        out_shape=[
            jax.ShapeDtypeStruct((line, 2 * SLOTS, width), BF16),
        ],
        in_specs=[
            pl.BlockSpec(memory_space=pltpu.SMEM),
            pl.BlockSpec(memory_space=pltpu.VMEM),
            pl.BlockSpec(memory_space=pl.ANY),
            pl.BlockSpec(memory_space=pl.ANY),
        ],
        out_specs=[pl.BlockSpec(memory_space=pltpu.VMEM)],
        scratch_shapes=[pltpu.VMEM((2, patches, width), BF16), pltpu.SemaphoreType.DMA((2,))],
        compiler_params=pltpu.CompilerParams(vmem_limit_bytes=60 * 1024 * 1024),
    )(counts, mask_index, teacher_patches, student_patches)
    pay = exchange(pay, "z")
    lines = [pay]
    for away in range(1, ROWS):
        route = [(i, (i - away) % ROWS) for i in range(ROWS)]
        lines.append(lax.ppermute(pay, "y", route))
    pair = jnp.stack([prototypes, lax.ppermute(prototypes, "proto", swap)])
    pairs_held = [pair]
    for away in range(1, half):
        pairs_held.append(lax.ppermute(pair, "proto", routes[-away % half]))
    (protos,) = call(
        prototypes_kernel, [((protos_held, width), BF16)], (place, *pairs_held), scalars=1
    )
    (onehot,) = call(
        patch_kernel, [((patches, CAP), BF16)], (place, counts, mask_index), scalars=2
    )

    packed = ((8, LANES), F32)
    col_out = ((PROTO, chunks, LANES), F32)
    row_out = ((devices, 8, LANES), F32)
    pay_scratch = pltpu.VMEM((devices, SLOTS, width), BF16)
    pairs = tokens * protos_held
    work = pl.CostEstimate(
        flops=2 * pairs * width, bytes_accessed=8 * pairs, transcendentals=pairs
    )
    teach, slots, valid, base, col = call(
        first_kernel,
        [
            ((tokens, width), BF16),
            ((8, devices * SLOTS), F32),
            packed,
            ((8, LANES), jnp.int32),
            col_out,
        ],
        (place, *lines, protos),
        scalars=1,
        scratch=(pay_scratch,),
        cost=work,
    )
    col = exchange(col, "proto")
    stud, stud_row = call(
        student_kernel,
        [((tokens, width), BF16), packed],
        (place, *lines, slots, protos),
        scalars=1,
        scratch=(pay_scratch, pltpu.VMEM((tokens, protos_held), F32)),
        cost=work,
    )
    exps, top, row, stud_row = call(
        second_kernel,
        [((tokens, protos_held), F32), packed, row_out, packed],
        (teach, protos, col, stud_row),
        cost=work,
    )
    row = exchange(row, TOK)
    factor, col = call(third_kernel, [packed, col_out], (exps, top, valid, row))
    col = exchange(col, "proto")
    (row,) = call(functools.partial(row_kernel, 0), [row_out], (exps, factor, col, stud_row))
    row = exchange(row, TOK)
    early = row
    (col,) = call(column_kernel, [col_out], (exps, factor, valid, row))
    col = exchange(col, "proto")
    (row,) = call(
        functools.partial(row_kernel, 8 - USED), [row_out], (exps, factor, col, stud_row)
    )
    row = exchange(row, TOK)
    grad_slots, grads = call(
        gradient_kernel,
        [((devices, SLOTS, width), BF16), ((tokens, protos_held), BF16)],
        (base, exps, factor, valid, col, early, row, stud, protos),
        scalars=1,
        scratch=(
            pltpu.VMEM((2, tokens, 2 * LANES), F32),
            pltpu.VMEM((tokens, LANES), F32),
            pltpu.VMEM((tokens, LANES), F32),
            pltpu.VMEM((tokens + SLOTS, width), F32),
        ),
        cost=work,
    )
    near, far = call(
        proto_kernel,
        [((half, share, width), F32), ((half, share, width), F32)],
        (place, grads, stud),
        scalars=1,
        cost=work,
    )
    mine = near + lax.ppermute(far, "proto", swap)
    arrived = [lax.ppermute(mine[away], "proto", routes[away]) for away in range(1, half)]
    rows, grad_prototypes = call(
        sum_kernel,
        [((PROTO, SLOTS, width), F32), ((share, width), F32)],
        (exchange(grad_slots, TOK), mine, *arrived),
    )
    rows = exchange(rows, "proto")
    (grad_patches,) = call(spread_kernel, [((patches, width), F32)], (onehot, rows))
    return (grad_patches, grad_prototypes)


def solution(mesh):
    devices, protos = mesh.devices.shape
    shape = (ROWS, devices // ROWS, protos)
    mesh = Mesh(mesh.devices.reshape(shape), (*TOK, "proto"))
    return jax.shard_map(
        functools.partial(on_device, devices),
        mesh=mesh,
        in_specs=(
            P(TOK, None),
            P(TOK, None),
            P(("proto", *TOK), None),
            P(TOK, None),
            P(TOK),
        ),
        out_specs=(P(TOK, None), P(("proto", *TOK), None)),
        check_vma=False,
    )
```

```python
import functools
import math

import jax
import jax.numpy as jnp
from jax import lax
from jax.experimental import pallas as pl
from jax.experimental.pallas import tpu as pltpu
from jax.sharding import Mesh, PartitionSpec as P

CAP = 256
BAL = 128
PROTO = 8
SLOTS = CAP // PROTO
ROWS = 4
TOK = ("y", "z")
USED = 5
LANES = 128
TEACHER_SCALE = 1.0 / 0.07
STUDENT_SCALE = 1.0 / 0.1
FAR_BELOW = -1e30
VMEM = 24 * 1024 * 1024
F32 = jnp.float32
BF16 = jnp.bfloat16
HIGH = lax.Precision.HIGHEST


def iota(shape, dim):
    return lax.broadcasted_iota(jnp.int32, shape, dim)


def dot_nt(a, b, precision=None):
    return lax.dot_general(
        a, b, (((1,), (1,)), ((), ())), precision=precision, preferred_element_type=F32
    )


def dot_tn(a, b, precision=None):
    return lax.dot_general(
        a, b, (((0,), (0,)), ((), ())), precision=precision, preferred_element_type=F32
    )


def dot_nn(a, b, precision=None):
    return jnp.dot(a, b, precision=precision, preferred_element_type=F32)


def blocks(tokens):
    return [(at // LANES, slice(at, min(at + LANES, tokens))) for at in range(0, tokens, LANES)]


def turned(rows, block, first_lane_only):
    at = iota((8, LANES), 0) == block
    if first_lane_only:
        at = at & (iota((8, LANES), 1) == 0)
    short = LANES - rows.shape[0]
    if short:
        rows = jnp.concatenate([rows, jnp.zeros((short, LANES), F32)], axis=0)
    return dot_nt(at.astype(F32), rows, HIGH)


def column(packed, block, size):
    at = (iota((8, LANES), 0) == block).astype(F32)
    return dot_tn(packed, at, HIGH)[:size]


def lse_over_first(values):
    top = jnp.max(values, axis=0)
    return top + jnp.log(jnp.sum(jnp.exp(values - top[None]), axis=0))


def row_offset(group, device):
    return lax.rem(group + device, PROTO)


def pick_kernel(
    count_ref, mask_ref, teacher_ref, student_ref, pay_ref, patch_ref, sem_ref,
):
    copies = [
        pltpu.make_async_copy(source, patch_ref.at[which], sem_ref.at[which])
        for which, source in enumerate((teacher_ref, student_ref))
    ]
    for copy in copies:
        copy.start()
    patches, width = teacher_ref.shape
    device = lax.axis_index("y") * pay_ref.shape[0] + lax.axis_index("z")
    offset = row_offset(lax.axis_index("proto"), device)
    at = (iota((SLOTS, patches), 1) == iota((SLOTS, patches), 0) * PROTO + offset).astype(BF16)
    mask = jnp.broadcast_to(mask_ref[...], (LANES, patches))
    high = dot_nt(at, (mask // 256).astype(F32).astype(BF16))
    low = dot_nt(at, (mask % 256).astype(F32).astype(BF16))
    chosen = (high * 256.0 + low + 0.5).astype(jnp.int32)
    lane = iota((SLOTS, LANES), 1)
    onehot = jnp.concatenate(
        [(lane + start == chosen).astype(F32).astype(BF16) for start in range(0, patches, LANES)],
        axis=1,
    )
    held = iota((SLOTS, width), 0) * PROTO + offset < count_ref[0]
    copies[0].wait()
    teach = jnp.where(held, dot_nn(onehot, patch_ref[0]), jnp.inf).astype(BF16)
    copies[1].wait()
    stud = dot_nn(onehot, patch_ref[1]).astype(BF16)
    both = jnp.concatenate([teach, stud], axis=0)
    pay_ref[...] = jnp.broadcast_to(both[None], pay_ref.shape)


def place_onehot(place, tokens):
    return (iota((tokens, place.shape[1]), 0).astype(F32) == place).astype(BF16)


def prototypes_kernel(place_ref, *refs):
    *pair_refs, protos_ref = refs
    share = pair_refs[0].shape[1]
    group = place_ref[0]
    core = lax.rem(group, 2)
    for away, pair_ref in enumerate(pair_refs):
        x = lax.rem(group // 2 + away, PROTO // 2)
        for other in range(2):
            start = pl.multiple_of((2 * x + (core + other) % 2) * share, share)
            protos_ref[pl.ds(start, share), :] = pair_ref[other]


def in_order(y, line_refs, pay_ref, first_slot):
    line = line_refs[0].shape[0]
    for away in range(ROWS):
        start = lax.rem(y + away, ROWS) * line
        pay_ref[pl.ds(start, line), :, :] = line_refs[away][:, first_slot : first_slot + SLOTS, :]
    devices, slots, width = pay_ref.shape
    return pay_ref[...].reshape(devices * slots, width)


def first_kernel(*refs):
    place_ref, *line_refs = refs[: ROWS + 1]
    protos_ref, teach_ref, place_out_ref, valid_ref, base_ref, col_ref, pay_ref = refs[ROWS + 1 :]
    arrived = in_order(place_ref[2], line_refs, pay_ref, 0).astype(F32)
    tokens = teach_ref.shape[0]
    slots, width = arrived.shape
    real = arrived < jnp.inf
    pick = (iota((8, width), 1) == 0).astype(BF16)
    flags = dot_nt(pick, real.astype(F32).astype(BF16))
    held = dot_nn(
        flags.astype(BF16), (iota((slots, LANES), 0) // SLOTS == iota((slots, LANES), 1)).astype(BF16)
    )
    before = dot_nn(
        held.astype(BF16), (iota((LANES, slots), 0) < iota((LANES, slots), 1) // SLOTS).astype(BF16)
    )[:1]
    bases = dot_nn(
        held.astype(BF16), (iota((LANES, LANES), 0) < iota((LANES, LANES), 1)).astype(BF16)
    )
    base_ref[...] = (bases + 0.5).astype(jnp.int32)
    inner = (iota((1, slots), 1) % SLOTS).astype(F32)
    place = jnp.where(flags[:1] > 0.5, before + inner, -1.0)
    place_out_ref[...] = jnp.broadcast_to(place, place_out_ref.shape)
    total = jnp.max(place, axis=1, keepdims=True) + 1.0
    order = iota((8, LANES), 0) * LANES + iota((8, LANES), 1)
    valid_ref[...] = (order.astype(F32) < total).astype(F32)
    onehot = place_onehot(place, tokens)
    teach = dot_nn(onehot, jnp.where(real, arrived, 0.0).astype(BF16)).astype(BF16)
    teach_ref[...] = teach
    step = 2 * LANES
    alive = iota((tokens, step), 0).astype(F32) < total
    rows = []
    for start in range(0, protos_ref.shape[0], step):
        scores = dot_nt(teach, protos_ref[start : start + step, :]) * TEACHER_SCALE
        scores = jnp.where(alive, scores, FAR_BELOW)
        top = jnp.max(scores, axis=0, keepdims=True)
        lse = top + jnp.log(jnp.sum(jnp.exp(scores - top), axis=0, keepdims=True))
        rows += [lse[:, :LANES], lse[:, LANES:]]
    col_ref[...] = jnp.broadcast_to(jnp.concatenate(rows, axis=0)[None], col_ref.shape)


def wide(packed):
    return jnp.concatenate([packed[i : i + 1, :] for i in range(packed.shape[0])], axis=1)


def exps_below_top(left_ref, protos_ref, scale, shift, out_ref):
    step = 2 * LANES
    for start in range(0, protos_ref.shape[0], step):
        scores = dot_nt(left_ref[...], protos_ref[start : start + step, :]) * scale
        if shift is not None:
            scores = scores + shift[:, start : start + step]
        out_ref[:, start : start + step] = scores
    tops = jnp.zeros((8, LANES), F32)
    totals = jnp.zeros((8, LANES), F32)
    starts = range(0, protos_ref.shape[0], LANES)
    for block, rows in blocks(left_ref.shape[0]):
        top = out_ref[rows, :LANES]
        for start in starts[1:]:
            top = jnp.maximum(top, out_ref[rows, start : start + LANES])
        top = jnp.broadcast_to(jnp.max(top, axis=1, keepdims=True), top.shape)
        sums = jnp.zeros_like(top)
        for start in starts:
            exps = jnp.exp(out_ref[rows, start : start + LANES] - top)
            out_ref[rows, start : start + LANES] = exps
            sums += exps
        tops += turned(top, block, True)
        totals += turned(sums, block, False)
    return tops, totals


def second_kernel(teach_ref, protos_ref, col_ref, stud_row_ref, exp_ref, top_ref, row_ref, stud_out_ref):
    col_pot = -wide(lse_over_first(col_ref[...]))
    tops, totals = exps_below_top(teach_ref, protos_ref, TEACHER_SCALE, col_pot, exp_ref)
    top_ref[...] = tops
    lses = tops + jnp.log(jnp.where(totals > 0.0, totals, 1.0))
    row_ref[...] = jnp.broadcast_to(lses[None], row_ref.shape)
    stud_out_ref[...] = stud_row_ref[...]


def weighted_columns(exp_ref, weight):
    chunks = exp_ref.shape[1] // LANES
    sums = [jnp.zeros((8, LANES), F32) for _ in range(chunks)]
    for block, rows in blocks(exp_ref.shape[0]):
        size = rows.stop - rows.start
        factor = column(weight, block, size)
        for chunk in range(chunks):
            part = exp_ref[rows, chunk * LANES : (chunk + 1) * LANES] * factor
            sums[chunk] += jnp.sum(part.reshape(size // 8, 8, LANES), axis=0)
    return jnp.concatenate([jnp.sum(part, axis=0, keepdims=True) for part in sums], axis=0)


def third_kernel(exp_ref, top_ref, valid_ref, row_ref, factor_ref, col_ref):
    row_pot = -lse_over_first(row_ref[...])
    factor = jnp.where(valid_ref[...] > 0.0, jnp.exp(top_ref[...] + row_pot), 0.0)
    factor_ref[...] = factor
    col_ref[...] = jnp.broadcast_to(weighted_columns(exp_ref, factor)[None], col_ref.shape)


def row_scale(valid_ref, sums):
    alive = valid_ref[...] > 0.0
    return jnp.where(alive, 1.0 / jnp.where(alive, sums, 1.0), 0.0)


def column_kernel(exp_ref, factor_ref, valid_ref, row_ref, col_ref):
    weight = row_scale(valid_ref, jnp.sum(row_ref[...], axis=0)) * factor_ref[...]
    col_ref[...] = jnp.broadcast_to(weighted_columns(exp_ref, weight)[None], col_ref.shape)


def weighted_rows(exp_ref, weight):
    sums = jnp.zeros((8, LANES), F32)
    for block, rows in blocks(exp_ref.shape[0]):
        part = jnp.zeros((rows.stop - rows.start, LANES), F32)
        for chunk in range(weight.shape[0]):
            values = exp_ref[rows, chunk * LANES : (chunk + 1) * LANES]
            part += values * weight[chunk : chunk + 1, :]
        sums += turned(part, block, False)
    return sums


def row_kernel(first, exp_ref, factor_ref, col_ref, stud_row_ref, row_ref):
    weight = 1.0 / jnp.sum(col_ref[...], axis=0)
    sums = weighted_rows(exp_ref, weight) * factor_ref[...]
    free = 8 - USED
    both = jnp.concatenate([sums[:USED], stud_row_ref[first : first + free, :]], axis=0)
    row_ref[...] = jnp.broadcast_to(both[None], row_ref.shape)


def student_kernel(*refs):
    place_ref, *line_refs = refs[: ROWS + 1]
    slot_ref, protos_ref, stud_ref, row_ref, pay_ref, exp_ref = refs[ROWS + 1 :]
    arrived = in_order(place_ref[2], line_refs, pay_ref, SLOTS)
    onehot = place_onehot(slot_ref[:1, :], stud_ref.shape[0])
    stud_ref[...] = dot_nn(onehot, arrived).astype(BF16)
    tops, totals = exps_below_top(stud_ref, protos_ref, STUDENT_SCALE, None, exp_ref)
    row_ref[...] = tops + jnp.log(jnp.where(totals > 0.0, totals, 1.0))


def gradient_kernel(
    base_ref, exp_ref, factor_ref, valid_ref, col_ref, early_ref, row_ref, stud_ref, protos_ref,
    tok_ref, grad_ref, score_ref, scale_ref, lse_ref, total_ref,
):
    tokens, width = stud_ref.shape
    weights = 1.0 / jnp.sum(col_ref[...], axis=0)
    sums = jnp.sum(row_ref[...], axis=0)
    scale = row_scale(valid_ref, sums) * (factor_ref[...] * STUDENT_SCALE)
    early, late = lse_over_first(early_ref[...]), lse_over_first(row_ref[...])
    lses = jnp.concatenate([early[USED:], late[USED:], jnp.zeros((2, LANES), F32)], axis=0)
    lses = lses - math.log(STUDENT_SCALE)
    lses = jnp.where(valid_ref[...] > 0.0, lses, -FAR_BELOW)
    for block, rows in blocks(tokens):
        size = rows.stop - rows.start
        scale_ref[rows, :] = column(scale, block, size)
        lse_ref[rows, :] = column(lses, block, size)
    step = 2 * LANES
    for chunk in range(protos_ref.shape[0] // step):
        slot = chunk % 2
        score_ref[slot] = dot_nt(stud_ref[...], protos_ref[chunk * step : (chunk + 1) * step, :])
        for half in range(2):
            index = 2 * chunk + half
            lanes = slice(index * LANES, (index + 1) * LANES)
            for _, rows in blocks(tokens):
                part = score_ref[slot, rows, half * LANES : (half + 1) * LANES] * STUDENT_SCALE
                student = jnp.exp(part - lse_ref[rows, :])
                target = exp_ref[rows, lanes] * scale_ref[rows, :] * weights[index : index + 1, :]
                grad_ref[rows, lanes] = (student - target).astype(BF16)
    total_ref[:tokens, :] = dot_nn(grad_ref[...], protos_ref[...])
    total_ref[tokens:, :] = jnp.zeros((SLOTS, width), F32)
    for device in range(tok_ref.shape[0]):
        base = base_ref[0, device]
        start = pl.multiple_of(base // 8 * 8, 8)
        rows = pltpu.roll(total_ref[pl.ds(start, SLOTS + 8), :], SLOTS + 8 - base % 8, 0)
        tok_ref[device, :, :] = rows[:SLOTS, :].astype(BF16)


def proto_kernel(place_ref, grad_ref, stud_ref, near_ref, far_ref):
    share = near_ref.shape[1]
    group = place_ref[0]
    for away in range(PROTO // 2):
        x = lax.rem(group // 2 + away, PROTO // 2)
        core = lax.rem(group, 2)
        start = pl.multiple_of((2 * x + 1 - core) * share, share)
        far_ref[away, :, :] = dot_tn(grad_ref[:, pl.ds(start, share)], stud_ref[...])
        start = pl.multiple_of((2 * x + core) * share, share)
        near_ref[away, :, :] = dot_tn(grad_ref[:, pl.ds(start, share)], stud_ref[...])


def sum_kernel(parts_ref, out_ref):
    out_ref[...] = jnp.sum(parts_ref[...].astype(F32), axis=0)


def patch_kernel(place_ref, count_ref, mask_ref, near_ref, *refs):
    *far_refs, onehot_ref, proto_ref = refs
    patches = onehot_ref.shape[0]
    group, device = place_ref[0], place_ref[1]
    wanted = iota((patches, CAP), 1)
    block = wanted // SLOTS
    source = (group // 2 + block // 2) % (PROTO // 2) * 2 + (group + block) % 2
    rank = (wanted % SLOTS) * PROTO + row_offset(source, device)
    at = (iota((patches, CAP), 0) == rank).astype(F32)
    mask = jnp.broadcast_to(mask_ref[...].astype(F32), (8, patches))
    chosen = (dot_nn(mask, at, HIGH)[:1] + 0.5).astype(jnp.int32)
    chosen = jnp.where(rank[:1, :] < count_ref[0], chosen, -1)
    onehot_ref[...] = (iota((patches, CAP), 0) == chosen).astype(BF16)
    total = near_ref[0]
    for far_ref in far_refs:
        total = total + far_ref[...]
    proto_ref[...] = total


def spread_kernel(onehot_ref, *refs):
    *row_refs, out_ref = refs
    rest = jnp.concatenate([ref[i] for ref in row_refs for i in range(2)], axis=0)
    total = None
    for _ in range(3):
        part = rest.astype(BF16)
        rest = rest - part.astype(F32)
        moved = dot_nn(onehot_ref[...], part)
        total = moved if total is None else total + moved
    out_ref[...] = total


def call(kernel, outs, inputs, scalars=0, scratch=(), cost=None):
    smem = [pl.BlockSpec(memory_space=pltpu.SMEM)] * scalars
    arrays = [pl.BlockSpec(memory_space=pltpu.VMEM)] * (len(inputs) - scalars)
    return pl.pallas_call(
        kernel,
        out_shape=[jax.ShapeDtypeStruct(shape, dtype) for shape, dtype in outs],
        in_specs=smem + arrays,
        out_specs=[pl.BlockSpec(memory_space=pltpu.VMEM)] * len(outs),
        scratch_shapes=list(scratch),
        compiler_params=pltpu.CompilerParams(vmem_limit_bytes=VMEM),
        cost_estimate=cost,
    )(*inputs)


def most_tokens(devices):
    slack = sum((PROTO - 1 - device % PROTO) for device in range(devices))
    return -(-((BAL * devices + slack) // PROTO) // 16) * 16


def exchange(parts, axis):
    return lax.all_to_all(parts, axis, 0, 0, tiled=True)


def on_device(devices, teacher_patches, student_patches, prototypes, mask_index, counts):
    patches, width = teacher_patches.shape
    share = prototypes.shape[0]
    protos_held = PROTO * share
    chunks = protos_held // LANES
    tokens = most_tokens(devices)
    line = devices // ROWS
    group = lax.axis_index("proto")
    y = lax.axis_index("y")
    device = y * line + lax.axis_index("z")
    place = jnp.stack([group, device, y]).astype(jnp.int32)

    half = PROTO // 2
    swap = [(p, p ^ 1) for p in range(PROTO)]
    routes = [[(p, (p + 2 * away) % PROTO) for p in range(PROTO)] for away in range(half)]
    (pay,) = pl.pallas_call(
        pick_kernel,
        out_shape=[
            jax.ShapeDtypeStruct((line, 2 * SLOTS, width), BF16),
        ],
        in_specs=[
            pl.BlockSpec(memory_space=pltpu.SMEM),
            pl.BlockSpec(memory_space=pltpu.VMEM),
            pl.BlockSpec(memory_space=pl.ANY),
            pl.BlockSpec(memory_space=pl.ANY),
        ],
        out_specs=[pl.BlockSpec(memory_space=pltpu.VMEM)],
        scratch_shapes=[pltpu.VMEM((2, patches, width), BF16), pltpu.SemaphoreType.DMA((2,))],
        compiler_params=pltpu.CompilerParams(vmem_limit_bytes=60 * 1024 * 1024),
    )(counts, mask_index, teacher_patches, student_patches)
    pay = exchange(pay, "z")
    lines = [pay]
    for away in range(1, ROWS):
        route = [(i, (i - away) % ROWS) for i in range(ROWS)]
        lines.append(lax.ppermute(pay, "y", route))
    pair = jnp.stack([prototypes, lax.ppermute(prototypes, "proto", swap)])
    pairs_held = [pair]
    for away in range(1, half):
        pairs_held.append(lax.ppermute(pair, "proto", routes[-away % half]))
    (protos,) = call(
        prototypes_kernel, [((protos_held, width), BF16)], (place, *pairs_held), scalars=1
    )
    packed = ((8, LANES), F32)
    col_out = ((PROTO, chunks, LANES), F32)
    row_out = ((devices, 8, LANES), F32)
    pay_scratch = pltpu.VMEM((devices, SLOTS, width), BF16)
    pairs = tokens * protos_held
    work = pl.CostEstimate(
        flops=2 * pairs * width, bytes_accessed=8 * pairs, transcendentals=pairs
    )
    teach, slots, valid, base, col = call(
        first_kernel,
        [
            ((tokens, width), BF16),
            ((8, devices * SLOTS), F32),
            packed,
            ((8, LANES), jnp.int32),
            col_out,
        ],
        (place, *lines, protos),
        scalars=1,
        scratch=(pay_scratch,),
        cost=work,
    )
    col = exchange(col, "proto")
    stud, stud_row = call(
        student_kernel,
        [((tokens, width), BF16), packed],
        (place, *lines, slots, protos),
        scalars=1,
        scratch=(pay_scratch, pltpu.VMEM((tokens, protos_held), F32)),
        cost=work,
    )
    exps, top, row, stud_row = call(
        second_kernel,
        [((tokens, protos_held), F32), packed, row_out, packed],
        (teach, protos, col, stud_row),
        cost=work,
    )
    row = exchange(row, TOK)
    factor, col = call(third_kernel, [packed, col_out], (exps, top, valid, row))
    col = exchange(col, "proto")
    (row,) = call(functools.partial(row_kernel, 0), [row_out], (exps, factor, col, stud_row))
    row = exchange(row, TOK)
    early = row
    (col,) = call(column_kernel, [col_out], (exps, factor, valid, row))
    col = exchange(col, "proto")
    (row,) = call(
        functools.partial(row_kernel, 8 - USED), [row_out], (exps, factor, col, stud_row)
    )
    row = exchange(row, TOK)
    grad_slots, grads = call(
        gradient_kernel,
        [((devices, SLOTS, width), BF16), ((tokens, protos_held), BF16)],
        (base, exps, factor, valid, col, early, row, stud, protos),
        scalars=1,
        scratch=(
            pltpu.VMEM((2, tokens, 2 * LANES), F32),
            pltpu.VMEM((tokens, LANES), F32),
            pltpu.VMEM((tokens, LANES), F32),
            pltpu.VMEM((tokens + SLOTS, width), F32),
        ),
        cost=work,
    )
    near, far = call(
        proto_kernel,
        [((half, share, width), F32), ((half, share, width), F32)],
        (place, grads, stud),
        scalars=1,
        cost=work,
    )
    mine = near + lax.ppermute(far, "proto", swap)
    arrived = [lax.ppermute(mine[away], "proto", routes[away]) for away in range(1, half)]
    (rows,) = call(sum_kernel, [((SLOTS, width), F32)], (exchange(grad_slots, TOK),))
    rows = jnp.stack([rows, lax.ppermute(rows, "proto", swap)])
    all_rows = [rows]
    for away in range(1, half):
        all_rows.append(lax.ppermute(rows, "proto", routes[-away % half]))
    onehot, grad_prototypes = call(
        patch_kernel,
        [((patches, CAP), BF16), ((share, width), F32)],
        (place, counts, mask_index, mine, *arrived),
        scalars=2,
    )
    (grad_patches,) = call(spread_kernel, [((patches, width), F32)], (onehot, *all_rows))
    return (grad_patches, grad_prototypes)


def solution(mesh):
    devices, protos = mesh.devices.shape
    shape = (ROWS, devices // ROWS, protos)
    mesh = Mesh(mesh.devices.reshape(shape), (*TOK, "proto"))
    return jax.shard_map(
        functools.partial(on_device, devices),
        mesh=mesh,
        in_specs=(
            P(TOK, None),
            P(TOK, None),
            P(("proto", *TOK), None),
            P(TOK, None),
            P(TOK),
        ),
        out_specs=(P(TOK, None), P(("proto", *TOK), None)),
        check_vma=False,
    )
```

```python
import functools
import math

import jax
import jax.numpy as jnp
from jax import lax
from jax.experimental import pallas as pl
from jax.experimental.pallas import tpu as pltpu
from jax.sharding import Mesh, PartitionSpec as P

CAP = 256
BAL = 128
PROTO = 8
SLOTS = CAP // PROTO
ROWS = 4
TOK = ("y", "z")
USED = 5
LANES = 128
TEACHER_SCALE = 1.0 / 0.07
STUDENT_SCALE = 1.0 / 0.1
FAR_BELOW = -1e30
VMEM = 24 * 1024 * 1024
F32 = jnp.float32
BF16 = jnp.bfloat16
HIGH = lax.Precision.HIGHEST


def iota(shape, dim):
    return lax.broadcasted_iota(jnp.int32, shape, dim)


def dot_nt(a, b, precision=None):
    return lax.dot_general(
        a, b, (((1,), (1,)), ((), ())), precision=precision, preferred_element_type=F32
    )


def dot_tn(a, b, precision=None):
    return lax.dot_general(
        a, b, (((0,), (0,)), ((), ())), precision=precision, preferred_element_type=F32
    )


def dot_nn(a, b, precision=None):
    return jnp.dot(a, b, precision=precision, preferred_element_type=F32)


def blocks(tokens):
    return [(at // LANES, slice(at, min(at + LANES, tokens))) for at in range(0, tokens, LANES)]


def turned(parts, first_lane_only):
    count = len(parts)
    short = LANES - parts[-1].shape[0]
    if short:
        parts = parts + [jnp.zeros((short, LANES), F32)]
    at = jnp.ones((8, LANES), F32)
    if first_lane_only:
        at = (iota((8, LANES), 1) == 0).astype(F32)
    values = dot_nt(at, jnp.concatenate(parts, axis=0), HIGH)
    rows = [values[:1, block * LANES : (block + 1) * LANES] for block in range(count)]
    return jnp.concatenate(rows + [jnp.zeros((8 - count, LANES), F32)], axis=0)


def in_parts(packed):
    parts = []
    for _ in range(3):
        part = packed.astype(BF16).astype(F32)
        packed = packed - part
        parts.append(part)
    return jnp.concatenate(parts + [jnp.zeros((8, LANES), F32)], axis=0).astype(BF16)


def column(parts, block, size):
    at = (iota((32, LANES), 0) % 8 == block).astype(F32).astype(BF16)
    return dot_tn(parts, at)[:size]


def lse_over_first(values):
    top = jnp.max(values, axis=0)
    return top + jnp.log(jnp.sum(jnp.exp(values - top[None]), axis=0))


def row_offset(group, device):
    return lax.rem(group + device, PROTO)


def pick_kernel(
    count_ref, mask_ref, teacher_ref, student_ref, pay_ref, patch_ref, sem_ref,
):
    copies = [
        pltpu.make_async_copy(source, patch_ref.at[which], sem_ref.at[which])
        for which, source in enumerate((teacher_ref, student_ref))
    ]
    for copy in copies:
        copy.start()
    patches, width = teacher_ref.shape
    device = lax.axis_index("y") * pay_ref.shape[0] + lax.axis_index("z")
    offset = row_offset(lax.axis_index("proto"), device)
    at = (iota((SLOTS, patches), 1) == iota((SLOTS, patches), 0) * PROTO + offset).astype(BF16)
    mask = jnp.broadcast_to(mask_ref[...], (LANES, patches))
    high = dot_nt(at, (mask // 256).astype(F32).astype(BF16))
    low = dot_nt(at, (mask % 256).astype(F32).astype(BF16))
    chosen = (high * 256.0 + low + 0.5).astype(jnp.int32)
    lane = iota((SLOTS, LANES), 1)
    onehot = jnp.concatenate(
        [(lane + start == chosen).astype(F32).astype(BF16) for start in range(0, patches, LANES)],
        axis=1,
    )
    held = iota((SLOTS, width), 0) * PROTO + offset < count_ref[0]
    copies[0].wait()
    teach = jnp.where(held, dot_nn(onehot, patch_ref[0]), jnp.inf).astype(BF16)
    copies[1].wait()
    stud = dot_nn(onehot, patch_ref[1]).astype(BF16)
    both = jnp.concatenate([teach, stud], axis=0)
    pay_ref[...] = jnp.broadcast_to(both[None], pay_ref.shape)


def place_onehot(place, tokens):
    return (iota((tokens, place.shape[1]), 0).astype(F32) == place).astype(BF16)


def prototypes_kernel(place_ref, *refs):
    *pair_refs, protos_ref = refs
    share = pair_refs[0].shape[1]
    group = place_ref[0]
    core = lax.rem(group, 2)
    for away, pair_ref in enumerate(pair_refs):
        x = lax.rem(group // 2 + away, PROTO // 2)
        for other in range(2):
            start = pl.multiple_of((2 * x + (core + other) % 2) * share, share)
            protos_ref[pl.ds(start, share), :] = pair_ref[other]


def in_order(y, line_refs, pay_ref, first_slot):
    line = line_refs[0].shape[0]
    for away in range(ROWS):
        start = lax.rem(y + away, ROWS) * line
        pay_ref[pl.ds(start, line), :, :] = line_refs[away][:, first_slot : first_slot + SLOTS, :]
    devices, slots, width = pay_ref.shape
    return pay_ref[...].reshape(devices * slots, width)


def first_kernel(*refs):
    place_ref, *line_refs = refs[: ROWS + 1]
    protos_ref, teach_ref, place_out_ref, valid_ref, base_ref, col_ref, pay_ref = refs[ROWS + 1 :]
    arrived = in_order(place_ref[2], line_refs, pay_ref, 0).astype(F32)
    tokens = teach_ref.shape[0]
    slots, width = arrived.shape
    real = arrived < jnp.inf
    pick = (iota((8, width), 1) == 0).astype(BF16)
    flags = dot_nt(pick, real.astype(F32).astype(BF16))
    held = dot_nn(
        flags.astype(BF16), (iota((slots, LANES), 0) // SLOTS == iota((slots, LANES), 1)).astype(BF16)
    )
    before = dot_nn(
        held.astype(BF16), (iota((LANES, slots), 0) < iota((LANES, slots), 1) // SLOTS).astype(BF16)
    )[:1]
    bases = dot_nn(
        held.astype(BF16), (iota((LANES, LANES), 0) < iota((LANES, LANES), 1)).astype(BF16)
    )
    base_ref[...] = (bases + 0.5).astype(jnp.int32)
    inner = (iota((1, slots), 1) % SLOTS).astype(F32)
    place = jnp.where(flags[:1] > 0.5, before + inner, -1.0)
    place_out_ref[...] = jnp.broadcast_to(place, place_out_ref.shape)
    total = jnp.max(place, axis=1, keepdims=True) + 1.0
    order = iota((8, LANES), 0) * LANES + iota((8, LANES), 1)
    valid_ref[...] = (order.astype(F32) < total).astype(F32)
    onehot = place_onehot(place, tokens)
    teach = dot_nn(onehot, jnp.where(real, arrived, 0.0).astype(BF16)).astype(BF16)
    teach_ref[...] = teach
    step = 2 * LANES
    alive = iota((tokens, step), 0).astype(F32) < total
    rows = []
    for start in range(0, protos_ref.shape[0], step):
        scores = dot_nt(teach, protos_ref[start : start + step, :]) * TEACHER_SCALE
        scores = jnp.where(alive, scores, FAR_BELOW)
        top = jnp.max(scores, axis=0, keepdims=True)
        lse = top + jnp.log(jnp.sum(jnp.exp(scores - top), axis=0, keepdims=True))
        rows += [lse[:, :LANES], lse[:, LANES:]]
    col_ref[...] = jnp.broadcast_to(jnp.concatenate(rows, axis=0)[None], col_ref.shape)


def wide(packed):
    return jnp.concatenate([packed[i : i + 1, :] for i in range(packed.shape[0])], axis=1)


def exps_below_top(left_ref, protos_ref, scale, shift, out_ref):
    step = 2 * LANES
    for start in range(0, protos_ref.shape[0], step):
        scores = dot_nt(left_ref[...], protos_ref[start : start + step, :]) * scale
        if shift is not None:
            scores = scores + shift[:, start : start + step]
        out_ref[:, start : start + step] = scores
    tops, totals = [], []
    starts = range(0, protos_ref.shape[0], LANES)
    for block, rows in blocks(left_ref.shape[0]):
        top = out_ref[rows, :LANES]
        for start in starts[1:]:
            top = jnp.maximum(top, out_ref[rows, start : start + LANES])
        top = jnp.broadcast_to(jnp.max(top, axis=1, keepdims=True), top.shape)
        sums = jnp.zeros_like(top)
        for start in starts:
            exps = jnp.exp(out_ref[rows, start : start + LANES] - top)
            out_ref[rows, start : start + LANES] = exps
            sums += exps
        tops.append(top)
        totals.append(sums)
    return turned(tops, True), turned(totals, False)


def second_kernel(teach_ref, protos_ref, col_ref, stud_row_ref, exp_ref, top_ref, row_ref, stud_out_ref):
    col_pot = -wide(lse_over_first(col_ref[...]))
    tops, totals = exps_below_top(teach_ref, protos_ref, TEACHER_SCALE, col_pot, exp_ref)
    top_ref[...] = tops
    lses = tops + jnp.log(jnp.where(totals > 0.0, totals, 1.0))
    row_ref[...] = jnp.broadcast_to(lses[None], row_ref.shape)
    stud_out_ref[...] = stud_row_ref[...]


def weighted_columns(exp_ref, weight):
    chunks = exp_ref.shape[1] // LANES
    sums = [jnp.zeros((8, LANES), F32) for _ in range(chunks)]
    weight = in_parts(weight)
    for block, rows in blocks(exp_ref.shape[0]):
        size = rows.stop - rows.start
        factor = column(weight, block, size)
        for chunk in range(chunks):
            part = exp_ref[rows, chunk * LANES : (chunk + 1) * LANES] * factor
            sums[chunk] += jnp.sum(part.reshape(size // 8, 8, LANES), axis=0)
    return jnp.concatenate([jnp.sum(part, axis=0, keepdims=True) for part in sums], axis=0)


def third_kernel(exp_ref, top_ref, valid_ref, row_ref, factor_ref, col_ref):
    row_pot = -lse_over_first(row_ref[...])
    factor = jnp.where(valid_ref[...] > 0.0, jnp.exp(top_ref[...] + row_pot), 0.0)
    factor_ref[...] = factor
    col_ref[...] = jnp.broadcast_to(weighted_columns(exp_ref, factor)[None], col_ref.shape)


def row_scale(valid_ref, sums):
    alive = valid_ref[...] > 0.0
    return jnp.where(alive, 1.0 / jnp.where(alive, sums, 1.0), 0.0)


def column_kernel(exp_ref, factor_ref, valid_ref, row_ref, col_ref):
    weight = row_scale(valid_ref, jnp.sum(row_ref[...], axis=0)) * factor_ref[...]
    col_ref[...] = jnp.broadcast_to(weighted_columns(exp_ref, weight)[None], col_ref.shape)


def weighted_rows(exp_ref, weight):
    sums = []
    for block, rows in blocks(exp_ref.shape[0]):
        part = jnp.zeros((rows.stop - rows.start, LANES), F32)
        for chunk in range(weight.shape[0]):
            values = exp_ref[rows, chunk * LANES : (chunk + 1) * LANES]
            part += values * weight[chunk : chunk + 1, :]
        sums.append(part)
    return turned(sums, False)


def row_kernel(first, exp_ref, factor_ref, col_ref, stud_row_ref, row_ref):
    weight = 1.0 / jnp.sum(col_ref[...], axis=0)
    sums = weighted_rows(exp_ref, weight) * factor_ref[...]
    free = 8 - USED
    both = jnp.concatenate([sums[:USED], stud_row_ref[first : first + free, :]], axis=0)
    row_ref[...] = jnp.broadcast_to(both[None], row_ref.shape)


def student_kernel(*refs):
    place_ref, *line_refs = refs[: ROWS + 1]
    slot_ref, protos_ref, stud_ref, row_ref, pay_ref, exp_ref = refs[ROWS + 1 :]
    arrived = in_order(place_ref[2], line_refs, pay_ref, SLOTS)
    onehot = place_onehot(slot_ref[:1, :], stud_ref.shape[0])
    stud_ref[...] = dot_nn(onehot, arrived).astype(BF16)
    tops, totals = exps_below_top(stud_ref, protos_ref, STUDENT_SCALE, None, exp_ref)
    row_ref[...] = tops + jnp.log(jnp.where(totals > 0.0, totals, 1.0))


def gradient_kernel(
    base_ref, exp_ref, factor_ref, valid_ref, col_ref, early_ref, row_ref, stud_ref, protos_ref,
    tok_ref, grad_ref, score_ref, scale_ref, lse_ref, total_ref,
):
    tokens, width = stud_ref.shape
    weights = 1.0 / jnp.sum(col_ref[...], axis=0)
    sums = jnp.sum(row_ref[...], axis=0)
    scale = row_scale(valid_ref, sums) * (factor_ref[...] * STUDENT_SCALE)
    early, late = lse_over_first(early_ref[...]), lse_over_first(row_ref[...])
    lses = jnp.concatenate([early[USED:], late[USED:], jnp.zeros((2, LANES), F32)], axis=0)
    lses = lses - math.log(STUDENT_SCALE)
    lses = jnp.where(valid_ref[...] > 0.0, lses, -FAR_BELOW)
    scale, lses = in_parts(scale), in_parts(lses)
    for block, rows in blocks(tokens):
        size = rows.stop - rows.start
        scale_ref[rows, :] = column(scale, block, size)
        lse_ref[rows, :] = column(lses, block, size)
    step = 2 * LANES
    for chunk in range(protos_ref.shape[0] // step):
        slot = chunk % 2
        score_ref[slot] = dot_nt(stud_ref[...], protos_ref[chunk * step : (chunk + 1) * step, :])
        for half in range(2):
            index = 2 * chunk + half
            lanes = slice(index * LANES, (index + 1) * LANES)
            for _, rows in blocks(tokens):
                part = score_ref[slot, rows, half * LANES : (half + 1) * LANES] * STUDENT_SCALE
                student = jnp.exp(part - lse_ref[rows, :])
                target = exp_ref[rows, lanes] * scale_ref[rows, :] * weights[index : index + 1, :]
                grad_ref[rows, lanes] = (student - target).astype(BF16)
    total_ref[:tokens, :] = dot_nn(grad_ref[...], protos_ref[...])
    total_ref[tokens:, :] = jnp.zeros((SLOTS, width), F32)
    for device in range(tok_ref.shape[0]):
        base = base_ref[0, device]
        start = pl.multiple_of(base // 8 * 8, 8)
        rows = pltpu.roll(total_ref[pl.ds(start, SLOTS + 8), :], SLOTS + 8 - base % 8, 0)
        tok_ref[device, :, :] = rows[:SLOTS, :].astype(BF16)


def proto_kernel(place_ref, grad_ref, stud_ref, near_ref, far_ref):
    share = near_ref.shape[1]
    group = place_ref[0]
    for away in range(PROTO // 2):
        x = lax.rem(group // 2 + away, PROTO // 2)
        core = lax.rem(group, 2)
        start = pl.multiple_of((2 * x + 1 - core) * share, share)
        far_ref[away, :, :] = dot_tn(grad_ref[:, pl.ds(start, share)], stud_ref[...])
        start = pl.multiple_of((2 * x + core) * share, share)
        near_ref[away, :, :] = dot_tn(grad_ref[:, pl.ds(start, share)], stud_ref[...])


def sum_kernel(parts_ref, out_ref):
    out_ref[...] = jnp.sum(parts_ref[...].astype(F32), axis=0)


def patch_kernel(place_ref, count_ref, mask_ref, near_ref, *refs):
    *far_refs, onehot_ref, proto_ref = refs
    patches = onehot_ref.shape[0]
    group, device = place_ref[0], place_ref[1]
    wanted = iota((patches, CAP), 1)
    block = wanted // SLOTS
    source = (group // 2 + block // 2) % (PROTO // 2) * 2 + (group + block) % 2
    rank = (wanted % SLOTS) * PROTO + row_offset(source, device)
    at = (iota((patches, CAP), 0) == rank).astype(F32)
    mask = jnp.broadcast_to(mask_ref[...].astype(F32), (8, patches))
    chosen = (dot_nn(mask, at, HIGH)[:1] + 0.5).astype(jnp.int32)
    chosen = jnp.where(rank[:1, :] < count_ref[0], chosen, -1)
    onehot_ref[...] = (iota((patches, CAP), 0) == chosen).astype(BF16)
    total = near_ref[0]
    for far_ref in far_refs:
        total = total + far_ref[...]
    proto_ref[...] = total


def spread_kernel(onehot_ref, *refs):
    *row_refs, out_ref = refs
    rest = jnp.concatenate([ref[i] for ref in row_refs for i in range(2)], axis=0)
    total = None
    for _ in range(3):
        part = rest.astype(BF16)
        rest = rest - part.astype(F32)
        moved = dot_nn(onehot_ref[...], part)
        total = moved if total is None else total + moved
    out_ref[...] = total


def call(kernel, outs, inputs, scalars=0, scratch=(), cost=None):
    smem = [pl.BlockSpec(memory_space=pltpu.SMEM)] * scalars
    arrays = [pl.BlockSpec(memory_space=pltpu.VMEM)] * (len(inputs) - scalars)
    return pl.pallas_call(
        kernel,
        out_shape=[jax.ShapeDtypeStruct(shape, dtype) for shape, dtype in outs],
        in_specs=smem + arrays,
        out_specs=[pl.BlockSpec(memory_space=pltpu.VMEM)] * len(outs),
        scratch_shapes=list(scratch),
        compiler_params=pltpu.CompilerParams(vmem_limit_bytes=VMEM),
        cost_estimate=cost,
    )(*inputs)


def most_tokens(devices):
    slack = sum((PROTO - 1 - device % PROTO) for device in range(devices))
    return -(-((BAL * devices + slack) // PROTO) // 16) * 16


def exchange(parts, axis):
    return lax.all_to_all(parts, axis, 0, 0, tiled=True)


def on_device(devices, teacher_patches, student_patches, prototypes, mask_index, counts):
    patches, width = teacher_patches.shape
    share = prototypes.shape[0]
    protos_held = PROTO * share
    chunks = protos_held // LANES
    tokens = most_tokens(devices)
    line = devices // ROWS
    group = lax.axis_index("proto")
    y = lax.axis_index("y")
    device = y * line + lax.axis_index("z")
    place = jnp.stack([group, device, y]).astype(jnp.int32)

    half = PROTO // 2
    swap = [(p, p ^ 1) for p in range(PROTO)]
    routes = [[(p, (p + 2 * away) % PROTO) for p in range(PROTO)] for away in range(half)]
    (pay,) = pl.pallas_call(
        pick_kernel,
        out_shape=[
            jax.ShapeDtypeStruct((line, 2 * SLOTS, width), BF16),
        ],
        in_specs=[
            pl.BlockSpec(memory_space=pltpu.SMEM),
            pl.BlockSpec(memory_space=pltpu.VMEM),
            pl.BlockSpec(memory_space=pl.ANY),
            pl.BlockSpec(memory_space=pl.ANY),
        ],
        out_specs=[pl.BlockSpec(memory_space=pltpu.VMEM)],
        scratch_shapes=[pltpu.VMEM((2, patches, width), BF16), pltpu.SemaphoreType.DMA((2,))],
        compiler_params=pltpu.CompilerParams(vmem_limit_bytes=60 * 1024 * 1024),
    )(counts, mask_index, teacher_patches, student_patches)
    pay = exchange(pay, "z")
    lines = [pay]
    for away in range(1, ROWS):
        route = [(i, (i - away) % ROWS) for i in range(ROWS)]
        lines.append(lax.ppermute(pay, "y", route))
    pair = jnp.stack([prototypes, lax.ppermute(prototypes, "proto", swap)])
    pairs_held = [pair]
    for away in range(1, half):
        pairs_held.append(lax.ppermute(pair, "proto", routes[-away % half]))
    (protos,) = call(
        prototypes_kernel, [((protos_held, width), BF16)], (place, *pairs_held), scalars=1
    )
    packed = ((8, LANES), F32)
    col_out = ((PROTO, chunks, LANES), F32)
    row_out = ((devices, 8, LANES), F32)
    pay_scratch = pltpu.VMEM((devices, SLOTS, width), BF16)
    pairs = tokens * protos_held
    work = pl.CostEstimate(
        flops=2 * pairs * width, bytes_accessed=8 * pairs, transcendentals=pairs
    )
    teach, slots, valid, base, col = call(
        first_kernel,
        [
            ((tokens, width), BF16),
            ((8, devices * SLOTS), F32),
            packed,
            ((8, LANES), jnp.int32),
            col_out,
        ],
        (place, *lines, protos),
        scalars=1,
        scratch=(pay_scratch,),
        cost=work,
    )
    col = exchange(col, "proto")
    stud, stud_row = call(
        student_kernel,
        [((tokens, width), BF16), packed],
        (place, *lines, slots, protos),
        scalars=1,
        scratch=(pay_scratch, pltpu.VMEM((tokens, protos_held), F32)),
        cost=work,
    )
    exps, top, row, stud_row = call(
        second_kernel,
        [((tokens, protos_held), F32), packed, row_out, packed],
        (teach, protos, col, stud_row),
        cost=work,
    )
    row = exchange(row, TOK)
    factor, col = call(third_kernel, [packed, col_out], (exps, top, valid, row))
    col = exchange(col, "proto")
    (row,) = call(functools.partial(row_kernel, 0), [row_out], (exps, factor, col, stud_row))
    row = exchange(row, TOK)
    early = row
    (col,) = call(column_kernel, [col_out], (exps, factor, valid, row))
    col = exchange(col, "proto")
    (row,) = call(
        functools.partial(row_kernel, 8 - USED), [row_out], (exps, factor, col, stud_row)
    )
    row = exchange(row, TOK)
    grad_slots, grads = call(
        gradient_kernel,
        [((devices, SLOTS, width), BF16), ((tokens, protos_held), BF16)],
        (base, exps, factor, valid, col, early, row, stud, protos),
        scalars=1,
        scratch=(
            pltpu.VMEM((2, tokens, 2 * LANES), F32),
            pltpu.VMEM((tokens, LANES), F32),
            pltpu.VMEM((tokens, LANES), F32),
            pltpu.VMEM((tokens + SLOTS, width), F32),
        ),
        cost=work,
    )
    near, far = call(
        proto_kernel,
        [((half, share, width), F32), ((half, share, width), F32)],
        (place, grads, stud),
        scalars=1,
        cost=work,
    )
    mine = near + lax.ppermute(far, "proto", swap)
    arrived = [lax.ppermute(mine[away], "proto", routes[away]) for away in range(1, half)]
    (rows,) = call(sum_kernel, [((SLOTS, width), F32)], (exchange(grad_slots, TOK),))
    rows = jnp.stack([rows, lax.ppermute(rows, "proto", swap)])
    all_rows = [rows]
    for away in range(1, half):
        all_rows.append(lax.ppermute(rows, "proto", routes[-away % half]))
    onehot, grad_prototypes = call(
        patch_kernel,
        [((patches, CAP), BF16), ((share, width), F32)],
        (place, counts, mask_index, mine, *arrived),
        scalars=2,
    )
    (grad_patches,) = call(spread_kernel, [((patches, width), F32)], (onehot, *all_rows))
    return (grad_patches, grad_prototypes)


def solution(mesh):
    devices, protos = mesh.devices.shape
    shape = (ROWS, devices // ROWS, protos)
    mesh = Mesh(mesh.devices.reshape(shape), (*TOK, "proto"))
    return jax.shard_map(
        functools.partial(on_device, devices),
        mesh=mesh,
        in_specs=(
            P(TOK, None),
            P(TOK, None),
            P(("proto", *TOK), None),
            P(TOK, None),
            P(TOK),
        ),
        out_specs=(P(TOK, None), P(("proto", *TOK), None)),
        check_vma=False,
    )
```

```python
import functools
import math

import jax
import jax.numpy as jnp
from jax import lax
from jax.experimental import pallas as pl
from jax.experimental.pallas import tpu as pltpu
from jax.sharding import Mesh, PartitionSpec as P

CAP = 256
BAL = 128
PROTO = 8
SLOTS = CAP // PROTO
ROWS = 4
TOK = ("y", "z")
USED = 5
LANES = 128
TEACHER_SCALE = 1.0 / 0.07
STUDENT_SCALE = 1.0 / 0.1
FAR_BELOW = -1e30
VMEM = 24 * 1024 * 1024
F32 = jnp.float32
BF16 = jnp.bfloat16
HIGH = lax.Precision.HIGHEST


def iota(shape, dim):
    return lax.broadcasted_iota(jnp.int32, shape, dim)


def dot_nt(a, b, precision=None):
    return lax.dot_general(
        a, b, (((1,), (1,)), ((), ())), precision=precision, preferred_element_type=F32
    )


def dot_tn(a, b, precision=None):
    return lax.dot_general(
        a, b, (((0,), (0,)), ((), ())), precision=precision, preferred_element_type=F32
    )


def dot_nn(a, b, precision=None):
    return jnp.dot(a, b, precision=precision, preferred_element_type=F32)


def blocks(tokens):
    return [(at // LANES, slice(at, min(at + LANES, tokens))) for at in range(0, tokens, LANES)]


def turned(parts, first_lane_only):
    count = len(parts)
    short = LANES - parts[-1].shape[0]
    if short:
        parts = parts + [jnp.zeros((short, LANES), F32)]
    at = jnp.ones((8, LANES), F32)
    if first_lane_only:
        at = (iota((8, LANES), 1) == 0).astype(F32)
    values = dot_nt(at, jnp.concatenate(parts, axis=0), HIGH)
    rows = [values[:1, block * LANES : (block + 1) * LANES] for block in range(count)]
    return jnp.concatenate(rows + [jnp.zeros((8 - count, LANES), F32)], axis=0)


def in_parts(packed):
    parts = []
    for _ in range(3):
        part = packed.astype(BF16).astype(F32)
        packed = packed - part
        parts.append(part)
    return jnp.concatenate(parts + [jnp.zeros((8, LANES), F32)], axis=0).astype(BF16)


def column(parts, block, size):
    at = (iota((32, LANES), 0) % 8 == block).astype(F32).astype(BF16)
    return dot_tn(parts, at)[:size]


def lse_over_first(values):
    top = jnp.max(values, axis=0)
    return top + jnp.log(jnp.sum(jnp.exp(values - top[None]), axis=0))


def row_offset(group, device):
    return lax.rem(group + device, PROTO)


def pick_kernel(
    count_ref, mask_ref, teacher_ref, student_ref, pay_ref, patch_ref, sem_ref,
):
    copies = [
        pltpu.make_async_copy(source, patch_ref.at[which], sem_ref.at[which])
        for which, source in enumerate((teacher_ref, student_ref))
    ]
    for copy in copies:
        copy.start()
    patches, width = teacher_ref.shape
    device = lax.axis_index("y") * pay_ref.shape[0] + lax.axis_index("z")
    offset = row_offset(lax.axis_index("proto"), device)
    at = (iota((SLOTS, patches), 1) == iota((SLOTS, patches), 0) * PROTO + offset).astype(BF16)
    mask = jnp.broadcast_to(mask_ref[...], (LANES, patches))
    high = dot_nt(at, (mask // 256).astype(F32).astype(BF16))
    low = dot_nt(at, (mask % 256).astype(F32).astype(BF16))
    chosen = (high * 256.0 + low + 0.5).astype(jnp.int32)
    lane = iota((SLOTS, LANES), 1)
    onehot = jnp.concatenate(
        [(lane + start == chosen).astype(F32).astype(BF16) for start in range(0, patches, LANES)],
        axis=1,
    )
    held = iota((SLOTS, width), 0) * PROTO + offset < count_ref[0]
    copies[0].wait()
    teach = jnp.where(held, dot_nn(onehot, patch_ref[0]), jnp.inf).astype(BF16)
    copies[1].wait()
    stud = dot_nn(onehot, patch_ref[1]).astype(BF16)
    both = jnp.concatenate([teach, stud], axis=0)
    pay_ref[...] = jnp.broadcast_to(both[None], pay_ref.shape)


def place_onehot(place, tokens):
    return (iota((tokens, place.shape[1]), 0).astype(F32) == place).astype(BF16)


def prototypes_kernel(place_ref, *refs):
    *pair_refs, protos_ref = refs
    share = pair_refs[0].shape[1]
    group = place_ref[0]
    core = lax.rem(group, 2)
    for away, pair_ref in enumerate(pair_refs):
        x = lax.rem(group // 2 + away, PROTO // 2)
        for other in range(2):
            start = pl.multiple_of((2 * x + (core + other) % 2) * share, share)
            protos_ref[pl.ds(start, share), :] = pair_ref[other]


def in_order(y, line_refs, pay_ref, first_slot):
    line = line_refs[0].shape[0]
    for away in range(ROWS):
        start = lax.rem(y + away, ROWS) * line
        pay_ref[pl.ds(start, line), :, :] = line_refs[away][:, first_slot : first_slot + SLOTS, :]
    devices, slots, width = pay_ref.shape
    return pay_ref[...].reshape(devices * slots, width)


def first_kernel(*refs):
    place_ref, *line_refs = refs[: ROWS + 1]
    protos_ref, teach_ref, place_out_ref, valid_ref, base_ref, col_ref, pay_ref = refs[ROWS + 1 :]
    arrived = in_order(place_ref[2], line_refs, pay_ref, 0).astype(F32)
    tokens = teach_ref.shape[0]
    slots, width = arrived.shape
    real = arrived < jnp.inf
    pick = (iota((8, width), 1) == 0).astype(BF16)
    flags = dot_nt(pick, real.astype(F32).astype(BF16))
    held = dot_nn(
        flags.astype(BF16), (iota((slots, LANES), 0) // SLOTS == iota((slots, LANES), 1)).astype(BF16)
    )
    before = dot_nn(
        held.astype(BF16), (iota((LANES, slots), 0) < iota((LANES, slots), 1) // SLOTS).astype(BF16)
    )[:1]
    bases = dot_nn(
        held.astype(BF16), (iota((LANES, LANES), 0) < iota((LANES, LANES), 1)).astype(BF16)
    )
    base_ref[...] = (bases + 0.5).astype(jnp.int32)
    inner = (iota((1, slots), 1) % SLOTS).astype(F32)
    place = jnp.where(flags[:1] > 0.5, before + inner, -1.0)
    place_out_ref[...] = jnp.broadcast_to(place, place_out_ref.shape)
    total = jnp.max(place, axis=1, keepdims=True) + 1.0
    order = iota((8, LANES), 0) * LANES + iota((8, LANES), 1)
    valid_ref[...] = (order.astype(F32) < total).astype(F32)
    onehot = place_onehot(place, tokens)
    teach = dot_nn(onehot, jnp.where(real, arrived, 0.0).astype(BF16)).astype(BF16)
    teach_ref[...] = teach
    step = 2 * LANES
    alive = iota((tokens, step), 0).astype(F32) < total
    rows = []
    for start in range(0, protos_ref.shape[0], step):
        scores = dot_nt(teach, protos_ref[start : start + step, :]) * TEACHER_SCALE
        scores = jnp.where(alive, scores, FAR_BELOW)
        top = jnp.max(scores, axis=0, keepdims=True)
        lse = top + jnp.log(jnp.sum(jnp.exp(scores - top), axis=0, keepdims=True))
        rows += [lse[:, :LANES], lse[:, LANES:]]
    col_ref[...] = jnp.broadcast_to(jnp.concatenate(rows, axis=0)[None], col_ref.shape)


def wide(packed):
    return jnp.concatenate([packed[i : i + 1, :] for i in range(packed.shape[0])], axis=1)


def exps_below_top(left_ref, protos_ref, scale, shift, out_ref):
    step = 2 * LANES
    for start in range(0, protos_ref.shape[0], step):
        scores = dot_nt(left_ref[...], protos_ref[start : start + step, :]) * scale
        if shift is not None:
            scores = scores + shift[:, start : start + step]
        out_ref[:, start : start + step] = scores
    tops, totals = [], []
    starts = range(0, protos_ref.shape[0], LANES)
    for block, rows in blocks(left_ref.shape[0]):
        top = out_ref[rows, :LANES]
        for start in starts[1:]:
            top = jnp.maximum(top, out_ref[rows, start : start + LANES])
        top = jnp.broadcast_to(jnp.max(top, axis=1, keepdims=True), top.shape)
        sums = jnp.zeros_like(top)
        for start in starts:
            exps = jnp.exp(out_ref[rows, start : start + LANES] - top)
            out_ref[rows, start : start + LANES] = exps
            sums += exps
        tops.append(top)
        totals.append(sums)
    return turned(tops, True), turned(totals, False)


def second_kernel(teach_ref, protos_ref, col_ref, stud_row_ref, exp_ref, top_ref, row_ref, stud_out_ref):
    col_pot = -wide(lse_over_first(col_ref[...]))
    tops, totals = exps_below_top(teach_ref, protos_ref, TEACHER_SCALE, col_pot, exp_ref)
    top_ref[...] = tops
    lses = tops + jnp.log(jnp.where(totals > 0.0, totals, 1.0))
    row_ref[...] = jnp.broadcast_to(lses[None], row_ref.shape)
    stud_out_ref[...] = stud_row_ref[...]


def weighted_columns(exp_ref, weight):
    chunks = exp_ref.shape[1] // LANES
    sums = [jnp.zeros((8, LANES), F32) for _ in range(chunks)]
    weight = in_parts(weight)
    for block, rows in blocks(exp_ref.shape[0]):
        size = rows.stop - rows.start
        factor = column(weight, block, size)
        for chunk in range(chunks):
            part = exp_ref[rows, chunk * LANES : (chunk + 1) * LANES] * factor
            sums[chunk] += jnp.sum(part.reshape(size // 8, 8, LANES), axis=0)
    return jnp.concatenate([jnp.sum(part, axis=0, keepdims=True) for part in sums], axis=0)


def third_kernel(exp_ref, top_ref, valid_ref, row_ref, factor_ref, col_ref):
    row_pot = -lse_over_first(row_ref[...])
    factor = jnp.where(valid_ref[...] > 0.0, jnp.exp(top_ref[...] + row_pot), 0.0)
    factor_ref[...] = factor
    col_ref[...] = jnp.broadcast_to(weighted_columns(exp_ref, factor)[None], col_ref.shape)


def row_scale(valid_ref, sums):
    alive = valid_ref[...] > 0.0
    return jnp.where(alive, 1.0 / jnp.where(alive, sums, 1.0), 0.0)


def column_kernel(exp_ref, factor_ref, valid_ref, row_ref, col_ref):
    weight = row_scale(valid_ref, jnp.sum(row_ref[...], axis=0)) * factor_ref[...]
    col_ref[...] = jnp.broadcast_to(weighted_columns(exp_ref, weight)[None], col_ref.shape)


def weighted_rows(exp_ref, weight):
    sums = []
    for block, rows in blocks(exp_ref.shape[0]):
        part = jnp.zeros((rows.stop - rows.start, LANES), F32)
        for chunk in range(weight.shape[0]):
            values = exp_ref[rows, chunk * LANES : (chunk + 1) * LANES]
            part += values * weight[chunk : chunk + 1, :]
        sums.append(part)
    return turned(sums, False)


def row_kernel(first, exp_ref, factor_ref, col_ref, stud_row_ref, row_ref):
    weight = 1.0 / jnp.sum(col_ref[...], axis=0)
    sums = weighted_rows(exp_ref, weight) * factor_ref[...]
    free = 8 - USED
    both = jnp.concatenate([sums[:USED], stud_row_ref[first : first + free, :]], axis=0)
    row_ref[...] = jnp.broadcast_to(both[None], row_ref.shape)


def student_kernel(*refs):
    place_ref, *line_refs = refs[: ROWS + 1]
    slot_ref, protos_ref, stud_ref, row_ref, pay_ref, exp_ref = refs[ROWS + 1 :]
    arrived = in_order(place_ref[2], line_refs, pay_ref, SLOTS)
    onehot = place_onehot(slot_ref[:1, :], stud_ref.shape[0])
    stud_ref[...] = dot_nn(onehot, arrived).astype(BF16)
    tops, totals = exps_below_top(stud_ref, protos_ref, STUDENT_SCALE, None, exp_ref)
    row_ref[...] = tops + jnp.log(jnp.where(totals > 0.0, totals, 1.0))


def gradient_kernel(
    place_ref, base_ref, exp_ref, factor_ref, valid_ref, col_ref, early_ref, row_ref, stud_ref, protos_ref,
    tok_ref, near_ref, far_ref, grad_ref, part_ref, weight_ref, score_ref, scale_ref, lse_ref, total_ref,
):
    tokens, width = stud_ref.shape
    weights = 1.0 / jnp.sum(col_ref[...], axis=0)
    sums = jnp.sum(row_ref[...], axis=0)
    scale = row_scale(valid_ref, sums) * (factor_ref[...] * STUDENT_SCALE)
    early, late = lse_over_first(early_ref[...]), lse_over_first(row_ref[...])
    lses = jnp.concatenate([early[USED:], late[USED:], jnp.zeros((2, LANES), F32)], axis=0)
    lses = lses - math.log(STUDENT_SCALE)
    lses = jnp.where(valid_ref[...] > 0.0, lses, -FAR_BELOW)
    scale, lses = in_parts(scale), in_parts(lses)
    for block, rows in blocks(tokens):
        size = rows.stop - rows.start
        scale_ref[rows, :] = column(scale, block, size)
        lse_ref[rows, :] = column(lses, block, size)
    step = 2 * LANES
    group = place_ref[0]
    for owner in range(PROTO):
        weight_ref[owner, :, :] = weights[2 * owner : 2 * owner + 2, :]
    starts = []
    for away in range(PROTO):
        x = lax.rem(group // 2 + away, PROTO // 2)
        core = lax.rem(group + (1 if away < PROTO // 2 else 0), 2)
        starts.append(pl.multiple_of((2 * x + core) * step, step))

    def score(away):
        score_ref[away % 2] = dot_nt(stud_ref[...], protos_ref[pl.ds(starts[away], step), :])

    def product(away):
        out_ref = far_ref if away < PROTO // 2 else near_ref
        out_ref[away % (PROTO // 2), :, :] = dot_tn(part_ref[away % 2], stud_ref[...])

    score(0)
    for away in range(PROTO):
        if away + 1 < PROTO:
            score(away + 1)
        if away:
            product(away - 1)
        slot = away % 2
        weight = weight_ref[lax.div(starts[away], step)]
        for half in range(2):
            lanes = pl.ds(starts[away] + half * LANES, LANES)
            here = slice(half * LANES, (half + 1) * LANES)
            for _, rows in blocks(tokens):
                part = score_ref[slot, rows, here] * STUDENT_SCALE
                student = jnp.exp(part - lse_ref[rows, :])
                target = exp_ref[rows, lanes] * scale_ref[rows, :] * weight[half : half + 1, :]
                grads = (student - target).astype(BF16)
                part_ref[slot, rows, here] = grads
                grad_ref[rows, lanes] = grads
    product(PROTO - 1)
    total_ref[:tokens, :] = dot_nn(grad_ref[...], protos_ref[...])
    total_ref[tokens:, :] = jnp.zeros((SLOTS, width), F32)
    for device in range(tok_ref.shape[0]):
        base = base_ref[0, device]
        start = pl.multiple_of(base // 8 * 8, 8)
        rows = pltpu.roll(total_ref[pl.ds(start, SLOTS + 8), :], SLOTS + 8 - base % 8, 0)
        tok_ref[device, :, :] = rows[:SLOTS, :].astype(BF16)


def sum_kernel(parts_ref, out_ref):
    out_ref[...] = jnp.sum(parts_ref[...].astype(F32), axis=0)


def patch_kernel(place_ref, count_ref, mask_ref, near_ref, *refs):
    *far_refs, onehot_ref, proto_ref = refs
    patches = onehot_ref.shape[0]
    group, device = place_ref[0], place_ref[1]
    wanted = iota((patches, CAP), 1)
    block = wanted // SLOTS
    source = (group // 2 + block // 2) % (PROTO // 2) * 2 + (group + block) % 2
    rank = (wanted % SLOTS) * PROTO + row_offset(source, device)
    at = (iota((patches, CAP), 0) == rank).astype(F32)
    mask = jnp.broadcast_to(mask_ref[...].astype(F32), (8, patches))
    chosen = (dot_nn(mask, at, HIGH)[:1] + 0.5).astype(jnp.int32)
    chosen = jnp.where(rank[:1, :] < count_ref[0], chosen, -1)
    onehot_ref[...] = (iota((patches, CAP), 0) == chosen).astype(BF16)
    total = near_ref[0]
    for far_ref in far_refs:
        total = total + far_ref[...]
    proto_ref[...] = total


def spread_kernel(onehot_ref, *refs):
    *row_refs, out_ref = refs
    rest = jnp.concatenate([ref[i] for ref in row_refs for i in range(2)], axis=0)
    parts = []
    for _ in range(3):
        part = rest.astype(BF16)
        rest = rest - part.astype(F32)
        parts.append(part)
    onehot = onehot_ref[...]
    out_ref[...] = dot_nn(
        jnp.concatenate([onehot] * 3, axis=1), jnp.concatenate(parts, axis=0)
    )


def call(kernel, outs, inputs, scalars=0, scratch=(), cost=None):
    smem = [pl.BlockSpec(memory_space=pltpu.SMEM)] * scalars
    arrays = [pl.BlockSpec(memory_space=pltpu.VMEM)] * (len(inputs) - scalars)
    return pl.pallas_call(
        kernel,
        out_shape=[jax.ShapeDtypeStruct(shape, dtype) for shape, dtype in outs],
        in_specs=smem + arrays,
        out_specs=[pl.BlockSpec(memory_space=pltpu.VMEM)] * len(outs),
        scratch_shapes=list(scratch),
        compiler_params=pltpu.CompilerParams(vmem_limit_bytes=VMEM),
        cost_estimate=cost,
    )(*inputs)


def most_tokens(devices):
    slack = sum((PROTO - 1 - device % PROTO) for device in range(devices))
    return -(-((BAL * devices + slack) // PROTO) // 16) * 16


def exchange(parts, axis):
    return lax.all_to_all(parts, axis, 0, 0, tiled=True)


def on_device(devices, teacher_patches, student_patches, prototypes, mask_index, counts):
    patches, width = teacher_patches.shape
    share = prototypes.shape[0]
    protos_held = PROTO * share
    chunks = protos_held // LANES
    tokens = most_tokens(devices)
    line = devices // ROWS
    group = lax.axis_index("proto")
    y = lax.axis_index("y")
    device = y * line + lax.axis_index("z")
    place = jnp.stack([group, device, y]).astype(jnp.int32)

    half = PROTO // 2
    swap = [(p, p ^ 1) for p in range(PROTO)]
    routes = [[(p, (p + 2 * away) % PROTO) for p in range(PROTO)] for away in range(half)]
    (pay,) = pl.pallas_call(
        pick_kernel,
        out_shape=[
            jax.ShapeDtypeStruct((line, 2 * SLOTS, width), BF16),
        ],
        in_specs=[
            pl.BlockSpec(memory_space=pltpu.SMEM),
            pl.BlockSpec(memory_space=pltpu.VMEM),
            pl.BlockSpec(memory_space=pl.ANY),
            pl.BlockSpec(memory_space=pl.ANY),
        ],
        out_specs=[pl.BlockSpec(memory_space=pltpu.VMEM)],
        scratch_shapes=[pltpu.VMEM((2, patches, width), BF16), pltpu.SemaphoreType.DMA((2,))],
        compiler_params=pltpu.CompilerParams(vmem_limit_bytes=60 * 1024 * 1024),
    )(counts, mask_index, teacher_patches, student_patches)
    pay = exchange(pay, "z")
    lines = [pay]
    for away in range(1, ROWS):
        route = [(i, (i - away) % ROWS) for i in range(ROWS)]
        lines.append(lax.ppermute(pay, "y", route))
    pair = jnp.stack([prototypes, lax.ppermute(prototypes, "proto", swap)])
    pairs_held = [pair]
    for away in range(1, half):
        pairs_held.append(lax.ppermute(pair, "proto", routes[-away % half]))
    (protos,) = call(
        prototypes_kernel, [((protos_held, width), BF16)], (place, *pairs_held), scalars=1
    )
    packed = ((8, LANES), F32)
    col_out = ((PROTO, chunks, LANES), F32)
    row_out = ((devices, 8, LANES), F32)
    pay_scratch = pltpu.VMEM((devices, SLOTS, width), BF16)
    pairs = tokens * protos_held
    work = pl.CostEstimate(
        flops=2 * pairs * width, bytes_accessed=8 * pairs, transcendentals=pairs
    )
    teach, slots, valid, base, col = call(
        first_kernel,
        [
            ((tokens, width), BF16),
            ((8, devices * SLOTS), F32),
            packed,
            ((8, LANES), jnp.int32),
            col_out,
        ],
        (place, *lines, protos),
        scalars=1,
        scratch=(pay_scratch,),
        cost=work,
    )
    col = exchange(col, "proto")
    stud, stud_row = call(
        student_kernel,
        [((tokens, width), BF16), packed],
        (place, *lines, slots, protos),
        scalars=1,
        scratch=(pay_scratch, pltpu.VMEM((tokens, protos_held), F32)),
        cost=work,
    )
    exps, top, row, stud_row = call(
        second_kernel,
        [((tokens, protos_held), F32), packed, row_out, packed],
        (teach, protos, col, stud_row),
        cost=work,
    )
    row = exchange(row, TOK)
    factor, col = call(third_kernel, [packed, col_out], (exps, top, valid, row))
    col = exchange(col, "proto")
    (row,) = call(functools.partial(row_kernel, 0), [row_out], (exps, factor, col, stud_row))
    row = exchange(row, TOK)
    early = row
    (col,) = call(column_kernel, [col_out], (exps, factor, valid, row))
    col = exchange(col, "proto")
    (row,) = call(
        functools.partial(row_kernel, 8 - USED), [row_out], (exps, factor, col, stud_row)
    )
    row = exchange(row, TOK)
    grad_slots, near, far = call(
        gradient_kernel,
        [
            ((devices, SLOTS, width), BF16),
            ((half, share, width), F32),
            ((half, share, width), F32),
        ],
        (place, base, exps, factor, valid, col, early, row, stud, protos),
        scalars=2,
        scratch=(
            pltpu.VMEM((tokens, protos_held), BF16),
            pltpu.VMEM((2, tokens, 2 * LANES), BF16),
            pltpu.VMEM((PROTO, 2, LANES), F32),
            pltpu.VMEM((2, tokens, 2 * LANES), F32),
            pltpu.VMEM((tokens, LANES), F32),
            pltpu.VMEM((tokens, LANES), F32),
            pltpu.VMEM((tokens + SLOTS, width), F32),
        ),
        cost=work,
    )
    mine = near + lax.ppermute(far, "proto", swap)
    arrived = [lax.ppermute(mine[away], "proto", routes[away]) for away in range(1, half)]
    (rows,) = call(sum_kernel, [((SLOTS, width), F32)], (exchange(grad_slots, TOK),))
    rows = jnp.stack([rows, lax.ppermute(rows, "proto", swap)])
    all_rows = [rows]
    for away in range(1, half):
        all_rows.append(lax.ppermute(rows, "proto", routes[-away % half]))
    onehot, grad_prototypes = call(
        patch_kernel,
        [((patches, CAP), BF16), ((share, width), F32)],
        (place, counts, mask_index, mine, *arrived),
        scalars=2,
    )
    (grad_patches,) = call(spread_kernel, [((patches, width), F32)], (onehot, *all_rows))
    return (grad_patches, grad_prototypes)


def solution(mesh):
    devices, protos = mesh.devices.shape
    shape = (ROWS, devices // ROWS, protos)
    mesh = Mesh(mesh.devices.reshape(shape), (*TOK, "proto"))
    return jax.shard_map(
        functools.partial(on_device, devices),
        mesh=mesh,
        in_specs=(
            P(TOK, None),
            P(TOK, None),
            P(("proto", *TOK), None),
            P(TOK, None),
            P(TOK),
        ),
        out_specs=(P(TOK, None), P(("proto", *TOK), None)),
        check_vma=False,
    )
```

```python
import functools
import math

import jax
import jax.numpy as jnp
from jax import lax
from jax.experimental import pallas as pl
from jax.experimental.pallas import tpu as pltpu
from jax.sharding import Mesh, PartitionSpec as P

CAP = 256
BAL = 128
PROTO = 8
SLOTS = CAP // PROTO
ROWS = 4
TOK = ("y", "z")
USED = 5
LANES = 128
TEACHER_SCALE = 1.0 / 0.07
STUDENT_SCALE = 1.0 / 0.1
FAR_BELOW = -1e30
VMEM = 24 * 1024 * 1024
F32 = jnp.float32
BF16 = jnp.bfloat16
HIGH = lax.Precision.HIGHEST


def iota(shape, dim):
    return lax.broadcasted_iota(jnp.int32, shape, dim)


def dot_nt(a, b, precision=None):
    return lax.dot_general(
        a, b, (((1,), (1,)), ((), ())), precision=precision, preferred_element_type=F32
    )


def dot_tn(a, b, precision=None):
    return lax.dot_general(
        a, b, (((0,), (0,)), ((), ())), precision=precision, preferred_element_type=F32
    )


def dot_nn(a, b, precision=None):
    return jnp.dot(a, b, precision=precision, preferred_element_type=F32)


def blocks(tokens):
    return [(at // LANES, slice(at, min(at + LANES, tokens))) for at in range(0, tokens, LANES)]


def turned(parts, first_lane_only):
    count = len(parts)
    short = LANES - parts[-1].shape[0]
    if short:
        parts = parts + [jnp.zeros((short, LANES), F32)]
    at = jnp.ones((8, LANES), F32)
    if first_lane_only:
        at = (iota((8, LANES), 1) == 0).astype(F32)
    values = dot_nt(at, jnp.concatenate(parts, axis=0), HIGH)
    rows = [values[:1, block * LANES : (block + 1) * LANES] for block in range(count)]
    return jnp.concatenate(rows + [jnp.zeros((8 - count, LANES), F32)], axis=0)


def in_parts(packed):
    parts = []
    for _ in range(3):
        part = packed.astype(BF16).astype(F32)
        packed = packed - part
        parts.append(part)
    return jnp.concatenate(parts + [jnp.zeros((8, LANES), F32)], axis=0).astype(BF16)


def column(parts, block, size):
    at = (iota((32, LANES), 0) % 8 == block).astype(F32).astype(BF16)
    return dot_tn(parts, at)[:size]


def lse_over_first(values):
    top = jnp.max(values, axis=0)
    return top + jnp.log(jnp.sum(jnp.exp(values - top[None]), axis=0))


def row_offset(group, device):
    return lax.rem(group + device, PROTO)


def pick_kernel(
    count_ref, mask_ref, teacher_ref, student_ref, pay_ref, patch_ref, sem_ref,
):
    copies = [
        pltpu.make_async_copy(source, patch_ref.at[which], sem_ref.at[which])
        for which, source in enumerate((teacher_ref, student_ref))
    ]
    for copy in copies:
        copy.start()
    patches, width = teacher_ref.shape
    device = lax.axis_index("y") * pay_ref.shape[0] + lax.axis_index("z")
    offset = row_offset(lax.axis_index("proto"), device)
    at = (iota((SLOTS, patches), 1) == iota((SLOTS, patches), 0) * PROTO + offset).astype(BF16)
    mask = jnp.broadcast_to(mask_ref[...], (LANES, patches))
    high = dot_nt(at, (mask // 256).astype(F32).astype(BF16))
    low = dot_nt(at, (mask % 256).astype(F32).astype(BF16))
    chosen = (high * 256.0 + low + 0.5).astype(jnp.int32)
    lane = iota((SLOTS, LANES), 1)
    onehot = jnp.concatenate(
        [(lane + start == chosen).astype(F32).astype(BF16) for start in range(0, patches, LANES)],
        axis=1,
    )
    held = iota((SLOTS, width), 0) * PROTO + offset < count_ref[0]
    copies[0].wait()
    teach = jnp.where(held, dot_nn(onehot, patch_ref[0]), jnp.inf).astype(BF16)
    copies[1].wait()
    stud = dot_nn(onehot, patch_ref[1]).astype(BF16)
    both = jnp.concatenate([teach, stud], axis=0)
    pay_ref[...] = jnp.broadcast_to(both[None], pay_ref.shape)


def place_onehot(place, tokens):
    return (iota((tokens, place.shape[1]), 0).astype(F32) == place).astype(BF16)


def prototypes_kernel(place_ref, here_ref, next_ref, last_ref, own_ref, other_ref, protos_ref):
    share = own_ref.shape[0]
    group = place_ref[0]
    core = lax.rem(group, 2)
    step = 1 - 2 * core

    def put(values, away, other):
        x = lax.rem(group // 2 + away + PROTO // 2, PROTO // 2)
        start = pl.multiple_of((2 * x + lax.rem(core + other, 2)) * share, share)
        protos_ref[pl.ds(start, share), :] = values

    for other in range(2):
        put(here_ref[other], 0, other)
        put(next_ref[other], step, other)
        put(last_ref[other], -step, 1 - other)
    put(own_ref[...], 2, 0)
    put(other_ref[...], 2, 1)


def in_order(y, line_refs, pay_ref, first_slot):
    line = line_refs[0].shape[0]
    for away in range(ROWS):
        start = lax.rem(y + away, ROWS) * line
        pay_ref[pl.ds(start, line), :, :] = line_refs[away][:, first_slot : first_slot + SLOTS, :]
    devices, slots, width = pay_ref.shape
    return pay_ref[...].reshape(devices * slots, width)


def first_kernel(*refs):
    place_ref, *line_refs = refs[: ROWS + 1]
    protos_ref, teach_ref, place_out_ref, valid_ref, base_ref, col_ref, pay_ref = refs[ROWS + 1 :]
    arrived = in_order(place_ref[2], line_refs, pay_ref, 0).astype(F32)
    tokens = teach_ref.shape[0]
    slots, width = arrived.shape
    real = arrived < jnp.inf
    pick = (iota((8, width), 1) == 0).astype(BF16)
    flags = dot_nt(pick, real.astype(F32).astype(BF16))
    held = dot_nn(
        flags.astype(BF16), (iota((slots, LANES), 0) // SLOTS == iota((slots, LANES), 1)).astype(BF16)
    )
    before = dot_nn(
        held.astype(BF16), (iota((LANES, slots), 0) < iota((LANES, slots), 1) // SLOTS).astype(BF16)
    )[:1]
    bases = dot_nn(
        held.astype(BF16), (iota((LANES, LANES), 0) < iota((LANES, LANES), 1)).astype(BF16)
    )
    base_ref[...] = (bases + 0.5).astype(jnp.int32)
    inner = (iota((1, slots), 1) % SLOTS).astype(F32)
    place = jnp.where(flags[:1] > 0.5, before + inner, -1.0)
    place_out_ref[...] = jnp.broadcast_to(place, place_out_ref.shape)
    total = jnp.max(place, axis=1, keepdims=True) + 1.0
    order = iota((8, LANES), 0) * LANES + iota((8, LANES), 1)
    valid_ref[...] = (order.astype(F32) < total).astype(F32)
    onehot = place_onehot(place, tokens)
    teach = dot_nn(onehot, jnp.where(real, arrived, 0.0).astype(BF16)).astype(BF16)
    teach_ref[...] = teach
    step = 2 * LANES
    alive = iota((tokens, step), 0).astype(F32) < total
    rows = []
    for start in range(0, protos_ref.shape[0], step):
        scores = dot_nt(teach, protos_ref[start : start + step, :]) * TEACHER_SCALE
        scores = jnp.where(alive, scores, FAR_BELOW)
        top = jnp.max(scores, axis=0, keepdims=True)
        lse = top + jnp.log(jnp.sum(jnp.exp(scores - top), axis=0, keepdims=True))
        rows += [lse[:, :LANES], lse[:, LANES:]]
    col_ref[...] = jnp.broadcast_to(jnp.concatenate(rows, axis=0)[None], col_ref.shape)


def wide(packed):
    return jnp.concatenate([packed[i : i + 1, :] for i in range(packed.shape[0])], axis=1)


def exps_below_top(left_ref, protos_ref, scale, shift, out_ref):
    step = 2 * LANES
    for start in range(0, protos_ref.shape[0], step):
        scores = dot_nt(left_ref[...], protos_ref[start : start + step, :]) * scale
        if shift is not None:
            scores = scores + shift[:, start : start + step]
        out_ref[:, start : start + step] = scores
    tops, totals = [], []
    starts = range(0, protos_ref.shape[0], LANES)
    for block, rows in blocks(left_ref.shape[0]):
        top = out_ref[rows, :LANES]
        for start in starts[1:]:
            top = jnp.maximum(top, out_ref[rows, start : start + LANES])
        top = jnp.broadcast_to(jnp.max(top, axis=1, keepdims=True), top.shape)
        sums = jnp.zeros_like(top)
        for start in starts:
            exps = jnp.exp(out_ref[rows, start : start + LANES] - top)
            out_ref[rows, start : start + LANES] = exps
            sums += exps
        tops.append(top)
        totals.append(sums)
    return turned(tops, True), turned(totals, False)


def second_kernel(teach_ref, protos_ref, col_ref, stud_row_ref, exp_ref, top_ref, row_ref, stud_out_ref):
    col_pot = -wide(lse_over_first(col_ref[...]))
    tops, totals = exps_below_top(teach_ref, protos_ref, TEACHER_SCALE, col_pot, exp_ref)
    top_ref[...] = tops
    lses = tops + jnp.log(jnp.where(totals > 0.0, totals, 1.0))
    row_ref[...] = jnp.broadcast_to(lses[None], row_ref.shape)
    stud_out_ref[...] = stud_row_ref[...]


def weighted_columns(exp_ref, weight):
    chunks = exp_ref.shape[1] // LANES
    sums = [jnp.zeros((8, LANES), F32) for _ in range(chunks)]
    weight = in_parts(weight)
    for block, rows in blocks(exp_ref.shape[0]):
        size = rows.stop - rows.start
        factor = column(weight, block, size)
        for chunk in range(chunks):
            part = exp_ref[rows, chunk * LANES : (chunk + 1) * LANES] * factor
            sums[chunk] += jnp.sum(part.reshape(size // 8, 8, LANES), axis=0)
    return jnp.concatenate([jnp.sum(part, axis=0, keepdims=True) for part in sums], axis=0)


def third_kernel(exp_ref, top_ref, valid_ref, row_ref, factor_ref, col_ref):
    row_pot = -lse_over_first(row_ref[...])
    factor = jnp.where(valid_ref[...] > 0.0, jnp.exp(top_ref[...] + row_pot), 0.0)
    factor_ref[...] = factor
    col_ref[...] = jnp.broadcast_to(weighted_columns(exp_ref, factor)[None], col_ref.shape)


def row_scale(valid_ref, sums):
    alive = valid_ref[...] > 0.0
    return jnp.where(alive, 1.0 / jnp.where(alive, sums, 1.0), 0.0)


def column_kernel(exp_ref, factor_ref, valid_ref, row_ref, col_ref):
    weight = row_scale(valid_ref, jnp.sum(row_ref[...], axis=0)) * factor_ref[...]
    col_ref[...] = jnp.broadcast_to(weighted_columns(exp_ref, weight)[None], col_ref.shape)


def weighted_rows(exp_ref, weight):
    sums = []
    for block, rows in blocks(exp_ref.shape[0]):
        part = jnp.zeros((rows.stop - rows.start, LANES), F32)
        for chunk in range(weight.shape[0]):
            values = exp_ref[rows, chunk * LANES : (chunk + 1) * LANES]
            part += values * weight[chunk : chunk + 1, :]
        sums.append(part)
    return turned(sums, False)


def row_kernel(first, exp_ref, factor_ref, col_ref, stud_row_ref, row_ref):
    weight = 1.0 / jnp.sum(col_ref[...], axis=0)
    sums = weighted_rows(exp_ref, weight) * factor_ref[...]
    free = 8 - USED
    both = jnp.concatenate([sums[:USED], stud_row_ref[first : first + free, :]], axis=0)
    row_ref[...] = jnp.broadcast_to(both[None], row_ref.shape)


def student_kernel(*refs):
    place_ref, *line_refs = refs[: ROWS + 1]
    slot_ref, protos_ref, stud_ref, row_ref, pay_ref, exp_ref = refs[ROWS + 1 :]
    arrived = in_order(place_ref[2], line_refs, pay_ref, SLOTS)
    onehot = place_onehot(slot_ref[:1, :], stud_ref.shape[0])
    stud_ref[...] = dot_nn(onehot, arrived).astype(BF16)
    tops, totals = exps_below_top(stud_ref, protos_ref, STUDENT_SCALE, None, exp_ref)
    row_ref[...] = tops + jnp.log(jnp.where(totals > 0.0, totals, 1.0))


def gradient_kernel(
    base_ref, exp_ref, factor_ref, valid_ref, col_ref, early_ref, row_ref, stud_ref, protos_ref,
    tok_ref, grad_ref, score_ref, scale_ref, lse_ref, total_ref,
):
    tokens, width = stud_ref.shape
    weights = 1.0 / jnp.sum(col_ref[...], axis=0)
    sums = jnp.sum(row_ref[...], axis=0)
    scale = row_scale(valid_ref, sums) * (factor_ref[...] * STUDENT_SCALE)
    early, late = lse_over_first(early_ref[...]), lse_over_first(row_ref[...])
    lses = jnp.concatenate([early[USED:], late[USED:], jnp.zeros((2, LANES), F32)], axis=0)
    lses = lses - math.log(STUDENT_SCALE)
    lses = jnp.where(valid_ref[...] > 0.0, lses, -FAR_BELOW)
    scale, lses = in_parts(scale), in_parts(lses)
    for block, rows in blocks(tokens):
        size = rows.stop - rows.start
        scale_ref[rows, :] = column(scale, block, size)
        lse_ref[rows, :] = column(lses, block, size)
    step = 2 * LANES
    for chunk in range(protos_ref.shape[0] // step):
        slot = chunk % 2
        score_ref[slot] = dot_nt(stud_ref[...], protos_ref[chunk * step : (chunk + 1) * step, :])
        for half in range(2):
            index = 2 * chunk + half
            lanes = slice(index * LANES, (index + 1) * LANES)
            for _, rows in blocks(tokens):
                part = score_ref[slot, rows, half * LANES : (half + 1) * LANES] * STUDENT_SCALE
                student = jnp.exp(part - lse_ref[rows, :])
                target = exp_ref[rows, lanes] * scale_ref[rows, :] * weights[index : index + 1, :]
                grad_ref[rows, lanes] = (student - target).astype(BF16)
    total_ref[:tokens, :] = dot_nn(grad_ref[...], protos_ref[...])
    total_ref[tokens:, :] = jnp.zeros((SLOTS, width), F32)
    for device in range(tok_ref.shape[0]):
        base = base_ref[0, device]
        start = pl.multiple_of(base // 8 * 8, 8)
        rows = pltpu.roll(total_ref[pl.ds(start, SLOTS + 8), :], SLOTS + 8 - base % 8, 0)
        tok_ref[device, :, :] = rows[:SLOTS, :].astype(BF16)


def proto_kernel(place_ref, grad_ref, stud_ref, near_ref, far_ref):
    share = near_ref.shape[1]
    group = place_ref[0]
    for away in range(PROTO // 2):
        x = lax.rem(group // 2 + away, PROTO // 2)
        core = lax.rem(group, 2)
        start = pl.multiple_of((2 * x + 1 - core) * share, share)
        far_ref[away, :, :] = dot_tn(grad_ref[:, pl.ds(start, share)], stud_ref[...])
        start = pl.multiple_of((2 * x + core) * share, share)
        near_ref[away, :, :] = dot_tn(grad_ref[:, pl.ds(start, share)], stud_ref[...])


def sum_kernel(parts_ref, out_ref):
    out_ref[...] = jnp.sum(parts_ref[...].astype(F32), axis=0)


def patch_kernel(place_ref, count_ref, mask_ref, near_ref, *refs):
    *far_refs, onehot_ref, proto_ref = refs
    patches = onehot_ref.shape[0]
    group, device = place_ref[0], place_ref[1]
    wanted = iota((patches, CAP), 1)
    block = wanted // SLOTS
    source = (group // 2 + block // 2) % (PROTO // 2) * 2 + (group + block) % 2
    rank = (wanted % SLOTS) * PROTO + row_offset(source, device)
    at = (iota((patches, CAP), 0) == rank).astype(F32)
    mask = jnp.broadcast_to(mask_ref[...].astype(F32), (8, patches))
    chosen = (dot_nn(mask, at, HIGH)[:1] + 0.5).astype(jnp.int32)
    chosen = jnp.where(rank[:1, :] < count_ref[0], chosen, -1)
    onehot_ref[...] = (iota((patches, CAP), 0) == chosen).astype(BF16)
    total = near_ref[0]
    for far_ref in far_refs:
        total = total + far_ref[...]
    proto_ref[...] = total


def spread_kernel(onehot_ref, *refs):
    *row_refs, out_ref = refs
    rest = jnp.concatenate([ref[i] for ref in row_refs for i in range(2)], axis=0)
    total = None
    for _ in range(3):
        part = rest.astype(BF16)
        rest = rest - part.astype(F32)
        moved = dot_nn(onehot_ref[...], part)
        total = moved if total is None else total + moved
    out_ref[...] = total


def call(kernel, outs, inputs, scalars=0, scratch=(), cost=None):
    smem = [pl.BlockSpec(memory_space=pltpu.SMEM)] * scalars
    arrays = [pl.BlockSpec(memory_space=pltpu.VMEM)] * (len(inputs) - scalars)
    return pl.pallas_call(
        kernel,
        out_shape=[jax.ShapeDtypeStruct(shape, dtype) for shape, dtype in outs],
        in_specs=smem + arrays,
        out_specs=[pl.BlockSpec(memory_space=pltpu.VMEM)] * len(outs),
        scratch_shapes=list(scratch),
        compiler_params=pltpu.CompilerParams(vmem_limit_bytes=VMEM),
        cost_estimate=cost,
    )(*inputs)


def most_tokens(devices):
    slack = sum((PROTO - 1 - device % PROTO) for device in range(devices))
    return -(-((BAL * devices + slack) // PROTO) // 16) * 16


def exchange(parts, axis):
    return lax.all_to_all(parts, axis, 0, 0, tiled=True)


def on_device(devices, teacher_patches, student_patches, prototypes, mask_index, counts):
    patches, width = teacher_patches.shape
    share = prototypes.shape[0]
    protos_held = PROTO * share
    chunks = protos_held // LANES
    tokens = most_tokens(devices)
    line = devices // ROWS
    group = lax.axis_index("proto")
    y = lax.axis_index("y")
    device = y * line + lax.axis_index("z")
    place = jnp.stack([group, device, y]).astype(jnp.int32)

    half = PROTO // 2
    swap = [(p, p ^ 1) for p in range(PROTO)]
    routes = [[(p, (p + 2 * away) % PROTO) for p in range(PROTO)] for away in range(half)]
    (pay,) = pl.pallas_call(
        pick_kernel,
        out_shape=[
            jax.ShapeDtypeStruct((line, 2 * SLOTS, width), BF16),
        ],
        in_specs=[
            pl.BlockSpec(memory_space=pltpu.SMEM),
            pl.BlockSpec(memory_space=pltpu.VMEM),
            pl.BlockSpec(memory_space=pl.ANY),
            pl.BlockSpec(memory_space=pl.ANY),
        ],
        out_specs=[pl.BlockSpec(memory_space=pltpu.VMEM)],
        scratch_shapes=[pltpu.VMEM((2, patches, width), BF16), pltpu.SemaphoreType.DMA((2,))],
        compiler_params=pltpu.CompilerParams(vmem_limit_bytes=60 * 1024 * 1024),
    )(counts, mask_index, teacher_patches, student_patches)
    pay = exchange(pay, "z")
    lines = [pay]
    for away in range(1, ROWS):
        route = [(i, (i - away) % ROWS) for i in range(ROWS)]
        lines.append(lax.ppermute(pay, "y", route))
    pair = jnp.stack([prototypes, lax.ppermute(prototypes, "proto", swap)])
    apart = [(p, (p + (2 if p % 2 else -2)) % PROTO) for p in range(PROTO)]
    beside = lax.ppermute(pair, "proto", apart)
    opposite = lax.ppermute(prototypes, "proto", routes[2])
    (protos,) = call(
        prototypes_kernel,
        [((protos_held, width), BF16)],
        (
            place,
            pair,
            beside,
            lax.ppermute(beside, "proto", swap),
            opposite,
            lax.ppermute(opposite, "proto", swap),
        ),
        scalars=1,
    )

    packed = ((8, LANES), F32)
    col_out = ((PROTO, chunks, LANES), F32)
    row_out = ((devices, 8, LANES), F32)
    pay_scratch = pltpu.VMEM((devices, SLOTS, width), BF16)
    pairs = tokens * protos_held
    work = pl.CostEstimate(
        flops=2 * pairs * width, bytes_accessed=8 * pairs, transcendentals=pairs
    )
    teach, slots, valid, base, col = call(
        first_kernel,
        [
            ((tokens, width), BF16),
            ((8, devices * SLOTS), F32),
            packed,
            ((8, LANES), jnp.int32),
            col_out,
        ],
        (place, *lines, protos),
        scalars=1,
        scratch=(pay_scratch,),
        cost=work,
    )
    col = exchange(col, "proto")
    stud, stud_row = call(
        student_kernel,
        [((tokens, width), BF16), packed],
        (place, *lines, slots, protos),
        scalars=1,
        scratch=(pay_scratch, pltpu.VMEM((tokens, protos_held), F32)),
        cost=work,
    )
    exps, top, row, stud_row = call(
        second_kernel,
        [((tokens, protos_held), F32), packed, row_out, packed],
        (teach, protos, col, stud_row),
        cost=work,
    )
    row = exchange(row, TOK)
    factor, col = call(third_kernel, [packed, col_out], (exps, top, valid, row))
    col = exchange(col, "proto")
    (row,) = call(functools.partial(row_kernel, 0), [row_out], (exps, factor, col, stud_row))
    row = exchange(row, TOK)
    early = row
    (col,) = call(column_kernel, [col_out], (exps, factor, valid, row))
    col = exchange(col, "proto")
    (row,) = call(
        functools.partial(row_kernel, 8 - USED), [row_out], (exps, factor, col, stud_row)
    )
    row = exchange(row, TOK)
    grad_slots, grads = call(
        gradient_kernel,
        [((devices, SLOTS, width), BF16), ((tokens, protos_held), BF16)],
        (base, exps, factor, valid, col, early, row, stud, protos),
        scalars=1,
        scratch=(
            pltpu.VMEM((2, tokens, 2 * LANES), F32),
            pltpu.VMEM((tokens, LANES), F32),
            pltpu.VMEM((tokens, LANES), F32),
            pltpu.VMEM((tokens + SLOTS, width), F32),
        ),
        cost=work,
    )
    near, far = call(
        proto_kernel,
        [((half, share, width), F32), ((half, share, width), F32)],
        (place, grads, stud),
        scalars=1,
        cost=work,
    )
    mine = near + lax.ppermute(far, "proto", swap)
    arrived = [lax.ppermute(mine[away], "proto", routes[away]) for away in range(1, half)]
    (rows,) = call(sum_kernel, [((SLOTS, width), F32)], (exchange(grad_slots, TOK),))
    rows = jnp.stack([rows, lax.ppermute(rows, "proto", swap)])
    all_rows = [rows]
    for away in range(1, half):
        all_rows.append(lax.ppermute(rows, "proto", routes[-away % half]))
    onehot, grad_prototypes = call(
        patch_kernel,
        [((patches, CAP), BF16), ((share, width), F32)],
        (place, counts, mask_index, mine, *arrived),
        scalars=2,
    )
    (grad_patches,) = call(spread_kernel, [((patches, width), F32)], (onehot, *all_rows))
    return (grad_patches, grad_prototypes)


def solution(mesh):
    devices, protos = mesh.devices.shape
    shape = (ROWS, devices // ROWS, protos)
    mesh = Mesh(mesh.devices.reshape(shape), (*TOK, "proto"))
    return jax.shard_map(
        functools.partial(on_device, devices),
        mesh=mesh,
        in_specs=(
            P(TOK, None),
            P(TOK, None),
            P(("proto", *TOK), None),
            P(TOK, None),
            P(TOK),
        ),
        out_specs=(P(TOK, None), P(("proto", *TOK), None)),
        check_vma=False,
    )
```

```python
import functools
import math

import jax
import jax.numpy as jnp
from jax import lax
from jax.experimental import pallas as pl
from jax.experimental.pallas import tpu as pltpu
from jax.sharding import Mesh, PartitionSpec as P

CAP = 256
BAL = 128
PROTO = 8
SLOTS = CAP // PROTO
ROWS = 4
TOK = ("y", "z")
USED = 5
LANES = 128
TEACHER_SCALE = 1.0 / 0.07
STUDENT_SCALE = 1.0 / 0.1
FAR_BELOW = -1e30
VMEM = 24 * 1024 * 1024
F32 = jnp.float32
BF16 = jnp.bfloat16
HIGH = lax.Precision.HIGHEST


def iota(shape, dim):
    return lax.broadcasted_iota(jnp.int32, shape, dim)


def dot_nt(a, b, precision=None):
    return lax.dot_general(
        a, b, (((1,), (1,)), ((), ())), precision=precision, preferred_element_type=F32
    )


def dot_tn(a, b, precision=None):
    return lax.dot_general(
        a, b, (((0,), (0,)), ((), ())), precision=precision, preferred_element_type=F32
    )


def dot_nn(a, b, precision=None):
    return jnp.dot(a, b, precision=precision, preferred_element_type=F32)


def blocks(tokens):
    return [(at // LANES, slice(at, min(at + LANES, tokens))) for at in range(0, tokens, LANES)]


def turned(parts, first_lane_only):
    count = len(parts)
    short = LANES - parts[-1].shape[0]
    if short:
        parts = parts + [jnp.zeros((short, LANES), F32)]
    at = jnp.ones((8, LANES), F32)
    if first_lane_only:
        at = (iota((8, LANES), 1) == 0).astype(F32)
    values = dot_nt(at, jnp.concatenate(parts, axis=0), HIGH)
    rows = [values[:1, block * LANES : (block + 1) * LANES] for block in range(count)]
    return jnp.concatenate(rows + [jnp.zeros((8 - count, LANES), F32)], axis=0)


def in_parts(packed):
    parts = []
    for _ in range(3):
        part = packed.astype(BF16).astype(F32)
        packed = packed - part
        parts.append(part)
    return jnp.concatenate(parts + [jnp.zeros((8, LANES), F32)], axis=0).astype(BF16)


def column(parts, block, size):
    at = (iota((32, LANES), 0) % 8 == block).astype(F32).astype(BF16)
    return dot_tn(parts, at)[:size]


def lse_over_first(values):
    top = jnp.max(values, axis=0)
    return top + jnp.log(jnp.sum(jnp.exp(values - top[None]), axis=0))


def row_offset(group, device):
    return lax.rem(group + device, PROTO)


def pick_kernel(
    count_ref, mask_ref, teacher_ref, student_ref, pay_ref, patch_ref, sem_ref,
):
    copies = [
        pltpu.make_async_copy(source, patch_ref.at[which], sem_ref.at[which])
        for which, source in enumerate((teacher_ref, student_ref))
    ]
    for copy in copies:
        copy.start()
    patches, width = teacher_ref.shape
    device = lax.axis_index("y") * pay_ref.shape[0] + lax.axis_index("z")
    offset = row_offset(lax.axis_index("proto"), device)
    at = (iota((SLOTS, patches), 1) == iota((SLOTS, patches), 0) * PROTO + offset).astype(BF16)
    mask = jnp.broadcast_to(mask_ref[...], (LANES, patches))
    high = dot_nt(at, (mask // 256).astype(F32).astype(BF16))
    low = dot_nt(at, (mask % 256).astype(F32).astype(BF16))
    chosen = (high * 256.0 + low + 0.5).astype(jnp.int32)
    lane = iota((SLOTS, LANES), 1)
    onehot = jnp.concatenate(
        [(lane + start == chosen).astype(F32).astype(BF16) for start in range(0, patches, LANES)],
        axis=1,
    )
    held = iota((SLOTS, width), 0) * PROTO + offset < count_ref[0]
    copies[0].wait()
    teach = jnp.where(held, dot_nn(onehot, patch_ref[0]), jnp.inf).astype(BF16)
    copies[1].wait()
    stud = dot_nn(onehot, patch_ref[1]).astype(BF16)
    both = jnp.concatenate([teach, stud], axis=0)
    pay_ref[...] = jnp.broadcast_to(both[None], pay_ref.shape)


def place_onehot(place, tokens):
    return (iota((tokens, place.shape[1]), 0).astype(F32) == place).astype(BF16)


def prototypes_kernel(place_ref, *refs):
    *pair_refs, protos_ref = refs
    share = pair_refs[0].shape[1]
    group = place_ref[0]
    core = lax.rem(group, 2)
    for away, pair_ref in enumerate(pair_refs):
        x = lax.rem(group // 2 + away, PROTO // 2)
        for other in range(2):
            start = pl.multiple_of((2 * x + (core + other) % 2) * share, share)
            protos_ref[pl.ds(start, share), :] = pair_ref[other]


def in_order(y, line_refs, pay_ref, first_slot):
    line = line_refs[0].shape[0]
    for away in range(ROWS):
        start = lax.rem(y + away, ROWS) * line
        pay_ref[pl.ds(start, line), :, :] = line_refs[away][:, first_slot : first_slot + SLOTS, :]
    devices, slots, width = pay_ref.shape
    return pay_ref[...].reshape(devices * slots, width)


def first_kernel(*refs):
    place_ref, *line_refs = refs[: ROWS + 1]
    protos_ref, teach_ref, place_out_ref, valid_ref, base_ref, col_ref, pay_ref = refs[ROWS + 1 :]
    arrived = in_order(place_ref[2], line_refs, pay_ref, 0).astype(F32)
    tokens = teach_ref.shape[0]
    slots, width = arrived.shape
    real = arrived < jnp.inf
    pick = (iota((8, width), 1) == 0).astype(BF16)
    flags = dot_nt(pick, real.astype(F32).astype(BF16))
    held = dot_nn(
        flags.astype(BF16), (iota((slots, LANES), 0) // SLOTS == iota((slots, LANES), 1)).astype(BF16)
    )
    before = dot_nn(
        held.astype(BF16), (iota((LANES, slots), 0) < iota((LANES, slots), 1) // SLOTS).astype(BF16)
    )[:1]
    bases = dot_nn(
        held.astype(BF16), (iota((LANES, LANES), 0) < iota((LANES, LANES), 1)).astype(BF16)
    )
    base_ref[...] = (bases + 0.5).astype(jnp.int32)
    inner = (iota((1, slots), 1) % SLOTS).astype(F32)
    place = jnp.where(flags[:1] > 0.5, before + inner, -1.0)
    place_out_ref[...] = jnp.broadcast_to(place, place_out_ref.shape)
    total = jnp.max(place, axis=1, keepdims=True) + 1.0
    order = iota((8, LANES), 0) * LANES + iota((8, LANES), 1)
    valid_ref[...] = (order.astype(F32) < total).astype(F32)
    onehot = place_onehot(place, tokens)
    teach = dot_nn(onehot, jnp.where(real, arrived, 0.0).astype(BF16)).astype(BF16)
    teach_ref[...] = teach
    step = 2 * LANES
    alive = iota((tokens, step), 0).astype(F32) < total
    rows = []
    for start in range(0, protos_ref.shape[0], step):
        scores = dot_nt(teach, protos_ref[start : start + step, :]) * TEACHER_SCALE
        scores = jnp.where(alive, scores, FAR_BELOW)
        top = jnp.max(scores, axis=0, keepdims=True)
        lse = top + jnp.log(jnp.sum(jnp.exp(scores - top), axis=0, keepdims=True))
        rows += [lse[:, :LANES], lse[:, LANES:]]
    col_ref[...] = jnp.broadcast_to(jnp.concatenate(rows, axis=0)[None], col_ref.shape)


def wide(packed):
    return jnp.concatenate([packed[i : i + 1, :] for i in range(packed.shape[0])], axis=1)


def exps_below_top(left_ref, protos_ref, scale, shift, out_ref):
    step = 2 * LANES
    for start in range(0, protos_ref.shape[0], step):
        scores = dot_nt(left_ref[...], protos_ref[start : start + step, :]) * scale
        if shift is not None:
            scores = scores + shift[:, start : start + step]
        out_ref[:, start : start + step] = scores
    tops, totals = [], []
    starts = range(0, protos_ref.shape[0], LANES)
    for block, rows in blocks(left_ref.shape[0]):
        top = out_ref[rows, :LANES]
        for start in starts[1:]:
            top = jnp.maximum(top, out_ref[rows, start : start + LANES])
        top = jnp.broadcast_to(jnp.max(top, axis=1, keepdims=True), top.shape)
        sums = jnp.zeros_like(top)
        for start in starts:
            exps = jnp.exp(out_ref[rows, start : start + LANES] - top)
            out_ref[rows, start : start + LANES] = exps
            sums += exps
        tops.append(top)
        totals.append(sums)
    return turned(tops, True), turned(totals, False)


def second_kernel(teach_ref, protos_ref, col_ref, stud_row_ref, exp_ref, top_ref, row_ref, stud_out_ref):
    col_pot = -wide(lse_over_first(col_ref[...]))
    tops, totals = exps_below_top(teach_ref, protos_ref, TEACHER_SCALE, col_pot, exp_ref)
    top_ref[...] = tops
    lses = tops + jnp.log(jnp.where(totals > 0.0, totals, 1.0))
    row_ref[...] = jnp.broadcast_to(lses[None], row_ref.shape)
    stud_out_ref[...] = stud_row_ref[...]


def weighted_columns(exp_ref, weight):
    chunks = exp_ref.shape[1] // LANES
    sums = [jnp.zeros((8, LANES), F32) for _ in range(chunks)]
    weight = in_parts(weight)
    for block, rows in blocks(exp_ref.shape[0]):
        size = rows.stop - rows.start
        factor = column(weight, block, size)
        for chunk in range(chunks):
            part = exp_ref[rows, chunk * LANES : (chunk + 1) * LANES] * factor
            sums[chunk] += jnp.sum(part.reshape(size // 8, 8, LANES), axis=0)
    return jnp.concatenate([jnp.sum(part, axis=0, keepdims=True) for part in sums], axis=0)


def third_kernel(exp_ref, top_ref, valid_ref, row_ref, factor_ref, col_ref):
    row_pot = -lse_over_first(row_ref[...])
    factor = jnp.where(valid_ref[...] > 0.0, jnp.exp(top_ref[...] + row_pot), 0.0)
    factor_ref[...] = factor
    col_ref[...] = jnp.broadcast_to(weighted_columns(exp_ref, factor)[None], col_ref.shape)


def row_scale(valid_ref, sums):
    alive = valid_ref[...] > 0.0
    return jnp.where(alive, 1.0 / jnp.where(alive, sums, 1.0), 0.0)


def column_kernel(exp_ref, factor_ref, valid_ref, row_ref, col_ref):
    weight = row_scale(valid_ref, jnp.sum(row_ref[...], axis=0)) * factor_ref[...]
    col_ref[...] = jnp.broadcast_to(weighted_columns(exp_ref, weight)[None], col_ref.shape)


def weighted_rows(exp_ref, weight):
    sums = []
    for block, rows in blocks(exp_ref.shape[0]):
        part = jnp.zeros((rows.stop - rows.start, LANES), F32)
        for chunk in range(weight.shape[0]):
            values = exp_ref[rows, chunk * LANES : (chunk + 1) * LANES]
            part += values * weight[chunk : chunk + 1, :]
        sums.append(part)
    return turned(sums, False)


def row_kernel(first, exp_ref, factor_ref, col_ref, stud_row_ref, row_ref):
    weight = 1.0 / jnp.sum(col_ref[...], axis=0)
    sums = weighted_rows(exp_ref, weight) * factor_ref[...]
    free = 8 - USED
    both = jnp.concatenate([sums[:USED], stud_row_ref[first : first + free, :]], axis=0)
    row_ref[...] = jnp.broadcast_to(both[None], row_ref.shape)


def student_kernel(*refs):
    place_ref, *line_refs = refs[: ROWS + 1]
    slot_ref, protos_ref, stud_ref, row_ref, pay_ref, exp_ref = refs[ROWS + 1 :]
    arrived = in_order(place_ref[2], line_refs, pay_ref, SLOTS)
    onehot = place_onehot(slot_ref[:1, :], stud_ref.shape[0])
    stud_ref[...] = dot_nn(onehot, arrived).astype(BF16)
    tops, totals = exps_below_top(stud_ref, protos_ref, STUDENT_SCALE, None, exp_ref)
    row_ref[...] = tops + jnp.log(jnp.where(totals > 0.0, totals, 1.0))


def gradient_kernel(
    base_ref, exp_ref, factor_ref, valid_ref, col_ref, early_ref, row_ref, stud_ref, protos_ref,
    tok_ref, grad_ref, score_ref, scale_ref, lse_ref, total_ref,
):
    tokens, width = stud_ref.shape
    weights = 1.0 / jnp.sum(col_ref[...], axis=0)
    sums = jnp.sum(row_ref[...], axis=0)
    scale = row_scale(valid_ref, sums) * (factor_ref[...] * STUDENT_SCALE)
    early, late = lse_over_first(early_ref[...]), lse_over_first(row_ref[...])
    lses = jnp.concatenate([early[USED:], late[USED:], jnp.zeros((2, LANES), F32)], axis=0)
    lses = lses - math.log(STUDENT_SCALE)
    lses = jnp.where(valid_ref[...] > 0.0, lses, -FAR_BELOW)
    scale, lses = in_parts(scale), in_parts(lses)
    for block, rows in blocks(tokens):
        size = rows.stop - rows.start
        scale_ref[rows, :] = column(scale, block, size)
        lse_ref[rows, :] = column(lses, block, size)
    step = 2 * LANES
    for chunk in range(protos_ref.shape[0] // step):
        slot = chunk % 2
        score_ref[slot] = dot_nt(stud_ref[...], protos_ref[chunk * step : (chunk + 1) * step, :])
        for half in range(2):
            index = 2 * chunk + half
            lanes = slice(index * LANES, (index + 1) * LANES)
            for _, rows in blocks(tokens):
                part = score_ref[slot, rows, half * LANES : (half + 1) * LANES] * STUDENT_SCALE
                student = jnp.exp(part - lse_ref[rows, :])
                target = exp_ref[rows, lanes] * scale_ref[rows, :] * weights[index : index + 1, :]
                grad_ref[rows, lanes] = (student - target).astype(BF16)
    total_ref[:tokens, :] = dot_nn(grad_ref[...], protos_ref[...])
    total_ref[tokens:, :] = jnp.zeros((SLOTS, width), F32)
    for device in range(tok_ref.shape[0]):
        base = base_ref[0, device]
        start = pl.multiple_of(base // 8 * 8, 8)
        rows = pltpu.roll(total_ref[pl.ds(start, SLOTS + 8), :], SLOTS + 8 - base % 8, 0)
        tok_ref[device, :, :] = rows[:SLOTS, :].astype(BF16)


def proto_kernel(other, place_ref, grad_ref, stud_ref, out_ref):
    share = out_ref.shape[1]
    group = place_ref[0]
    for away in range(PROTO // 2):
        x = lax.rem(group // 2 + away, PROTO // 2)
        start = pl.multiple_of((2 * x + lax.rem(group + other, 2)) * share, share)
        out_ref[away, :, :] = dot_tn(grad_ref[:, pl.ds(start, share)], stud_ref[...])


def sum_kernel(parts_ref, out_ref):
    out_ref[...] = jnp.sum(parts_ref[...].astype(F32), axis=0)


def patch_kernel(place_ref, count_ref, mask_ref, near_ref, *refs):
    *far_refs, onehot_ref, proto_ref = refs
    patches = onehot_ref.shape[0]
    group, device = place_ref[0], place_ref[1]
    wanted = iota((patches, CAP), 1)
    block = wanted // SLOTS
    source = (group // 2 + block // 2) % (PROTO // 2) * 2 + (group + block) % 2
    rank = (wanted % SLOTS) * PROTO + row_offset(source, device)
    at = (iota((patches, CAP), 0) == rank).astype(F32)
    mask = jnp.broadcast_to(mask_ref[...].astype(F32), (8, patches))
    chosen = (dot_nn(mask, at, HIGH)[:1] + 0.5).astype(jnp.int32)
    chosen = jnp.where(rank[:1, :] < count_ref[0], chosen, -1)
    onehot_ref[...] = (iota((patches, CAP), 0) == chosen).astype(BF16)
    total = near_ref[0]
    for far_ref in far_refs:
        total = total + far_ref[...]
    proto_ref[...] = total


def spread_kernel(onehot_ref, *refs):
    *row_refs, out_ref = refs
    rest = jnp.concatenate([ref[i] for ref in row_refs for i in range(2)], axis=0)
    total = None
    for _ in range(3):
        part = rest.astype(BF16)
        rest = rest - part.astype(F32)
        moved = dot_nn(onehot_ref[...], part)
        total = moved if total is None else total + moved
    out_ref[...] = total


def call(kernel, outs, inputs, scalars=0, scratch=(), cost=None):
    smem = [pl.BlockSpec(memory_space=pltpu.SMEM)] * scalars
    arrays = [pl.BlockSpec(memory_space=pltpu.VMEM)] * (len(inputs) - scalars)
    return pl.pallas_call(
        kernel,
        out_shape=[jax.ShapeDtypeStruct(shape, dtype) for shape, dtype in outs],
        in_specs=smem + arrays,
        out_specs=[pl.BlockSpec(memory_space=pltpu.VMEM)] * len(outs),
        scratch_shapes=list(scratch),
        compiler_params=pltpu.CompilerParams(vmem_limit_bytes=VMEM),
        cost_estimate=cost,
    )(*inputs)


def most_tokens(devices):
    slack = sum((PROTO - 1 - device % PROTO) for device in range(devices))
    return -(-((BAL * devices + slack) // PROTO) // 16) * 16


def exchange(parts, axis):
    return lax.all_to_all(parts, axis, 0, 0, tiled=True)


def on_device(devices, teacher_patches, student_patches, prototypes, mask_index, counts):
    patches, width = teacher_patches.shape
    share = prototypes.shape[0]
    protos_held = PROTO * share
    chunks = protos_held // LANES
    tokens = most_tokens(devices)
    line = devices // ROWS
    group = lax.axis_index("proto")
    y = lax.axis_index("y")
    device = y * line + lax.axis_index("z")
    place = jnp.stack([group, device, y]).astype(jnp.int32)

    half = PROTO // 2
    swap = [(p, p ^ 1) for p in range(PROTO)]
    routes = [[(p, (p + 2 * away) % PROTO) for p in range(PROTO)] for away in range(half)]
    (pay,) = pl.pallas_call(
        pick_kernel,
        out_shape=[
            jax.ShapeDtypeStruct((line, 2 * SLOTS, width), BF16),
        ],
        in_specs=[
            pl.BlockSpec(memory_space=pltpu.SMEM),
            pl.BlockSpec(memory_space=pltpu.VMEM),
            pl.BlockSpec(memory_space=pl.ANY),
            pl.BlockSpec(memory_space=pl.ANY),
        ],
        out_specs=[pl.BlockSpec(memory_space=pltpu.VMEM)],
        scratch_shapes=[pltpu.VMEM((2, patches, width), BF16), pltpu.SemaphoreType.DMA((2,))],
        compiler_params=pltpu.CompilerParams(vmem_limit_bytes=60 * 1024 * 1024),
    )(counts, mask_index, teacher_patches, student_patches)
    pay = exchange(pay, "z")
    lines = [pay]
    for away in range(1, ROWS):
        route = [(i, (i - away) % ROWS) for i in range(ROWS)]
        lines.append(lax.ppermute(pay, "y", route))
    pair = jnp.stack([prototypes, lax.ppermute(prototypes, "proto", swap)])
    pairs_held = [pair]
    for away in range(1, half):
        pairs_held.append(lax.ppermute(pair, "proto", routes[-away % half]))
    (protos,) = call(
        prototypes_kernel, [((protos_held, width), BF16)], (place, *pairs_held), scalars=1
    )
    packed = ((8, LANES), F32)
    col_out = ((PROTO, chunks, LANES), F32)
    row_out = ((devices, 8, LANES), F32)
    pay_scratch = pltpu.VMEM((devices, SLOTS, width), BF16)
    pairs = tokens * protos_held
    work = pl.CostEstimate(
        flops=2 * pairs * width, bytes_accessed=8 * pairs, transcendentals=pairs
    )
    teach, slots, valid, base, col = call(
        first_kernel,
        [
            ((tokens, width), BF16),
            ((8, devices * SLOTS), F32),
            packed,
            ((8, LANES), jnp.int32),
            col_out,
        ],
        (place, *lines, protos),
        scalars=1,
        scratch=(pay_scratch,),
        cost=work,
    )
    col = exchange(col, "proto")
    stud, stud_row = call(
        student_kernel,
        [((tokens, width), BF16), packed],
        (place, *lines, slots, protos),
        scalars=1,
        scratch=(pay_scratch, pltpu.VMEM((tokens, protos_held), F32)),
        cost=work,
    )
    exps, top, row, stud_row = call(
        second_kernel,
        [((tokens, protos_held), F32), packed, row_out, packed],
        (teach, protos, col, stud_row),
        cost=work,
    )
    row = exchange(row, TOK)
    factor, col = call(third_kernel, [packed, col_out], (exps, top, valid, row))
    col = exchange(col, "proto")
    (row,) = call(functools.partial(row_kernel, 0), [row_out], (exps, factor, col, stud_row))
    row = exchange(row, TOK)
    early = row
    (col,) = call(column_kernel, [col_out], (exps, factor, valid, row))
    col = exchange(col, "proto")
    (row,) = call(
        functools.partial(row_kernel, 8 - USED), [row_out], (exps, factor, col, stud_row)
    )
    row = exchange(row, TOK)
    grad_slots, grads = call(
        gradient_kernel,
        [((devices, SLOTS, width), BF16), ((tokens, protos_held), BF16)],
        (base, exps, factor, valid, col, early, row, stud, protos),
        scalars=1,
        scratch=(
            pltpu.VMEM((2, tokens, 2 * LANES), F32),
            pltpu.VMEM((tokens, LANES), F32),
            pltpu.VMEM((tokens, LANES), F32),
            pltpu.VMEM((tokens + SLOTS, width), F32),
        ),
        cost=work,
    )
    far, near = [
        call(
            functools.partial(proto_kernel, other),
            [((half, share, width), F32)],
            (place, grads, stud),
            scalars=1,
            cost=work,
        )[0]
        for other in (1, 0)
    ]
    mine = near + lax.ppermute(far, "proto", swap)
    arrived = [lax.ppermute(mine[away], "proto", routes[away]) for away in range(1, half)]
    (rows,) = call(sum_kernel, [((SLOTS, width), F32)], (exchange(grad_slots, TOK),))
    rows = jnp.stack([rows, lax.ppermute(rows, "proto", swap)])
    all_rows = [rows]
    for away in range(1, half):
        all_rows.append(lax.ppermute(rows, "proto", routes[-away % half]))
    onehot, grad_prototypes = call(
        patch_kernel,
        [((patches, CAP), BF16), ((share, width), F32)],
        (place, counts, mask_index, mine, *arrived),
        scalars=2,
    )
    (grad_patches,) = call(spread_kernel, [((patches, width), F32)], (onehot, *all_rows))
    return (grad_patches, grad_prototypes)


def solution(mesh):
    devices, protos = mesh.devices.shape
    shape = (ROWS, devices // ROWS, protos)
    mesh = Mesh(mesh.devices.reshape(shape), (*TOK, "proto"))
    return jax.shard_map(
        functools.partial(on_device, devices),
        mesh=mesh,
        in_specs=(
            P(TOK, None),
            P(TOK, None),
            P(("proto", *TOK), None),
            P(TOK, None),
            P(TOK),
        ),
        out_specs=(P(TOK, None), P(("proto", *TOK), None)),
        check_vma=False,
    )
```
